32 devices in a mesh: groups: 2 (over x), zslab: 16 (over z, y, core).
Axes of the slice: x: 2, y: 2, z: 4, core: 2. Of those that a mesh axis runs over, the one named last changes fastest.
Arguments:
- feats: bfloat16 [64, 8, 64, 256], P(('groups', 'zslab')), parts along dimension 0, may hold values from -6 to 6
- voxmask: int32 [64, 512], P(('groups', 'zslab')), parts along dimension 0, may hold values 0 or 1
- links: int32 [64, 2], P(('groups', 'zslab')), parts along dimension 0, may hold values from -1 to 31, as said below
- weight: bfloat16 [27, 256, 256], replicated, may hold values from -0.078125 to 0.078125
- bias: float32 [256], replicated, may hold values from -3 to 3
- cotangent: bfloat16 [64, 8, 64, 256], P(('groups', 'zslab')), parts along dimension 0, may hold values from -6 to 6
Outputs:
- output: bfloat16 [64, 8, 64, 256], P(('groups', 'zslab')), parts along dimension 0
- grad_feats: bfloat16 [64, 8, 64, 256], P(('groups', 'zslab')), parts along dimension 0
- grad_weight: bfloat16 [54, 256, 256], P('groups'), parts along dimension 0
- grad_bias: float32 [512], P('groups'), parts along dimension 0
The draws below stay inside these ranges and needn't reach their ends.
There are 2 independent parts, one for each index of `groups`. The reference program is written for one: setup_inputs(seed, part) draws one part's arguments, and reference() takes and returns one part's arrays. A program takes and returns all parts, laid end to end along the dimension named above; an argument that names none is the same for every part. Nothing has to cross between parts.
Inputs may be any that keep to these rules, and one draw needn't show every extreme that they name: links[b, 0] == i >= 0 exactly when links[i, 1] == b; no brick is linked to itself; the bricks of one device (rows d * 2 to d * 2 + 1) have their upper links on pairwise different devices other than d, and their lower links too.
All inputs are finite; a program needn't handle non-finite values. No bound on the sum of `voxmask` on one device may be relied on, other than what follows from the above.
Results may differ from the reference program's by a relative error of at most 0.0055.
Values may be sent and summed in bfloat16 or wider, within the bound.
No kernel may reach another device: no remote copies, remote signals or barrier semaphores. Data moves between devices by JAX's collectives and lax.ppermute only.
A program may use at most 128 MiB of HBM per device.

```python
import jax
import jax.numpy as jnp
from jax import lax

C = 256
SLOTS = 2
BRICKS = 32
N_ZSLAB = 16


def draw_links(key, part):
    key = jax.random.fold_in(key, 11)
    lowers = jnp.full((BRICKS,), -1, jnp.int32)
    uppers = jnp.full((BRICKS,), -1, jnp.int32)
    devices = jnp.arange(N_ZSLAB, dtype=jnp.int32)
    order = jax.random.permutation(jax.random.fold_in(key, 500), N_ZSLAB).astype(jnp.int32)
    position = jnp.zeros((N_ZSLAB,), jnp.int32).at[order].set(devices)
    for layer in range(SLOTS):
        layer_key = jax.random.fold_in(key, layer)
        target = order[(position + layer + 1) % N_ZSLAB]
        broken = jax.random.randint(jax.random.fold_in(layer_key, 100), (N_ZSLAB,), 0, 4)
        source = devices * SLOTS + layer
        dest = target * SLOTS + (layer + 1) % SLOTS
        keep = broken != 0
        uppers = uppers.at[source].set(jnp.where(keep, dest, -1))
        lowers = lowers.at[dest].set(jnp.where(keep, source, -1))
    return jnp.stack([lowers, uppers], axis=1)


def touch_ends(drawn, key, low, top_value):
    spot = [jax.random.randint(jax.random.fold_in(key, axis), (), 0, length) for axis, length in enumerate(drawn.shape)]
    main_axis = drawn.shape.index(max(drawn.shape))
    next_to = spot[:main_axis] + [(spot[main_axis] + 1) % drawn.shape[main_axis]] + spot[main_axis + 1:]
    return drawn.at[tuple(spot)].set(low).at[tuple(next_to)].set(top_value)


def shard_levels(own_key, extent, cuts, low, top_value):
    level, own = 1.0, jax.random.fold_in(own_key, 6)
    for dim, blocks in cuts:
        steps = jnp.exp(jax.random.uniform(jax.random.fold_in(own, dim), (blocks,), jnp.float32, low / len(cuts), top_value / len(cuts)))
        level = level * jnp.repeat(steps, extent[dim] // blocks).reshape([-1 if axis == dim else 1 for axis in range(len(extent))])
    return level


def scatter_about(rng, dims, scale, bound, split=(), kind=jnp.bfloat16):
    gain = shard_levels(rng, dims, split, -0.22, 0.18) if split else 1.0
    entries = jax.random.normal(rng, dims, jnp.float32) * scale * gain
    return jnp.minimum(jnp.maximum(entries, -bound), bound).astype(kind)


def setup_inputs(seed: int = 0, part: int = 0) -> dict:
    splits = jax.random.split(jax.random.key(seed), 7)
    part_keys = jax.random.split(jax.random.fold_in(splits[6], part), 7)
    return {
        "feats": scatter_about(part_keys[0], (BRICKS, 8, 64, C), 1.0, 6.0, ((0, 16),)),
        "voxmask": touch_ends((jax.random.randint(part_keys[1], (BRICKS, 512), 0, 4) < 3).astype(jnp.int32), jax.random.fold_in(part_keys[1], 1), 0, 1),
        "links": draw_links(jax.random.fold_in(jax.random.fold_in(splits[6], part), 71), part),
        "weight": scatter_about(splits[3], (27, C, C), (27 * C) ** -0.5, 0.078125),
        "bias": scatter_about(splits[4], (C,), 0.5, 3.0, (), jnp.float32),
        "cotangent": scatter_about(part_keys[5], (BRICKS, 8, 64, C), 1.0, 6.0, ((0, 16),)),
    }


def extend_planes(planes, bottoms, tops, links):
    count = planes.shape[0]
    width = planes.shape[3]
    lower = links[:, 0]
    upper = links[:, 1]
    below = jnp.take(tops, jnp.maximum(lower, 0).astype(jnp.int32), axis=0)
    above = jnp.take(bottoms, jnp.maximum(upper, 0).astype(jnp.int32), axis=0)
    below = jnp.where((lower >= 0)[:, None, None], below, jnp.zeros_like(below))
    above = jnp.where((upper >= 0)[:, None, None], above, jnp.zeros_like(above))
    stacked = jnp.concatenate([below[:, None], planes, above[:, None]], axis=1)
    stacked = stacked.reshape(count, 10, 8, 8, width)
    return jnp.pad(stacked, ((0, 0), (0, 0), (1, 1), (1, 1), (0, 0)))


def forward_conv(extended, weight):
    count = extended.shape[0]
    width = extended.shape[4]
    total = jnp.zeros((count * 512, weight.shape[2]), jnp.float32)
    for depth in range(3):
        for row in range(3):
            for col in range(3):
                piece = extended[:, depth:depth + 8, row:row + 8, col:col + 8].reshape(count * 512, width)
                total = total + jnp.dot(piece, weight[9 * depth + 3 * row + col], preferred_element_type=jnp.float32)
    return total


def transpose_conv(grad_ext, weight):
    count = grad_ext.shape[0]
    width = grad_ext.shape[4]
    total = jnp.zeros((count * 512, weight.shape[1]), jnp.float32)
    for depth in range(3):
        for row in range(3):
            for col in range(3):
                piece = grad_ext[:, 2 - depth:10 - depth, 2 - row:10 - row, 2 - col:10 - col].reshape(count * 512, width)
                total = total + lax.dot_general(piece, weight[9 * depth + 3 * row + col], (((1,), (1,)), ((), ())), preferred_element_type=jnp.float32)
    return total


def weight_terms(extended, grad_rows):
    count = extended.shape[0]
    width = extended.shape[4]
    terms = []
    for depth in range(3):
        for row in range(3):
            for col in range(3):
                piece = extended[:, depth:depth + 8, row:row + 8, col:col + 8].reshape(count * 512, width)
                terms.append(lax.dot_general(piece, grad_rows, (((0,), (0,)), ((), ())), preferred_element_type=jnp.float32))
    return jnp.stack(terms, axis=0)


def reference(feats, voxmask, links, weight, bias, cotangent):
    count = feats.shape[0]
    width = feats.shape[3]
    keep = (voxmask == 1).reshape(count, 8, 64, 1)
    masked = jnp.where(keep, feats, jnp.zeros_like(feats))
    extended = extend_planes(masked, masked[:, 0], masked[:, 7], links)
    pre = forward_conv(extended, weight) + bias[None, :]
    keep_rows = keep.reshape(count * 512, 1)
    sigma = jax.nn.sigmoid(pre)
    output = jnp.where(keep_rows, pre * sigma, 0.0).astype(jnp.bfloat16)
    grad_pre = jnp.where(keep_rows, cotangent.reshape(count * 512, width).astype(jnp.float32) * sigma * (1.0 + pre * (1.0 - sigma)), 0.0).astype(jnp.bfloat16)
    grad_planes = grad_pre.reshape(count, 8, 64, width)
    grad_ext = extend_planes(grad_planes, grad_planes[:, 0], grad_planes[:, 7], links)
    grad_feats = jnp.where(keep_rows, transpose_conv(grad_ext, weight), 0.0).astype(jnp.bfloat16)
    grad_weight = weight_terms(extended, grad_pre).astype(jnp.bfloat16)
    grad_bias = jnp.sum(grad_pre.astype(jnp.float32), axis=0)
    return (output.reshape(count, 8, 64, width), grad_feats.reshape(count, 8, 64, width), grad_weight, grad_bias)
```

```python
import functools

import jax
import jax.numpy as jnp
from jax import lax
from jax.sharding import PartitionSpec as P


def extend_with(planes, below, above):
    count = planes.shape[0]
    width = planes.shape[3]
    stacked = jnp.concatenate([below[:, None], planes, above[:, None]], axis=1)
    stacked = stacked.reshape(count, 10, 8, 8, width)
    return jnp.pad(stacked, ((0, 0), (0, 0), (1, 1), (1, 1), (0, 0)))


def partners(size, bit):
    return [(i, i ^ bit) for i in range(size)]


def swap(x, size, bit):
    return lax.ppermute(x, "zslab", partners(size, bit))


def rotate(x, size, steps):
    return lax.ppermute(x, "zslab", [(i, (i + 4 * steps) % size) for i in range(size)])


def outer_gather(x, size):
    return [x] + [rotate(x, size, k) for k in range(1, size // 4)]


def gather_rims(rims, size):
    rows = jnp.concatenate([rims[None], swap(rims, size, 2)[None]], axis=0)
    return jnp.stack(outer_gather(rows, size), axis=0)


def rim_index(link, size, me):
    owner = jnp.maximum(link, 0) // 2
    steps = (me // 4 - owner // 4) % (size // 4)
    other = ((me // 2) ^ (owner // 2)) % 2
    return (steps * 2 + other) * 2 + link % 2, (link >= 0) & (owner % 2 == me % 2)


def pick_halos(rims, links, size):
    me = lax.axis_index("zslab")
    gathered = gather_rims(rims, size)
    count = gathered.shape[0] * gathered.shape[1] * gathered.shape[2]
    planes = gathered.reshape(count * 2, 64, gathered.shape[-1])

    def pick(wanted):
        flat = wanted.T.reshape(4)
        place, here = rim_index(flat, size, me)
        side = jnp.array([1, 1, 0, 0], jnp.int32)
        taken = jnp.take(planes, jnp.where(here, place * 2 + side, 0), axis=0)
        return jnp.where(here[:, None, None], taken, jnp.zeros_like(taken))

    mine = pick(links)
    theirs = pick(swap(links, size, 1))
    return mine + swap(theirs, size, 1)


def take_rows(x, place, rows):
    return lax.dynamic_slice_in_dim(x, place * rows, rows, axis=0)


def scatter_inner(x, size, bit):
    me = lax.axis_index("zslab")
    mine = (me // bit) % 2
    half = x.shape[0] // 2
    got = swap(take_rows(x, 1 - mine, half), size, bit)
    return (take_rows(x, mine, half).astype(jnp.float32) + got.astype(jnp.float32)).astype(jnp.bfloat16)


def scatter_outer(x, size):
    me = lax.axis_index("zslab")
    outer = size // 4
    place = me // 4
    rows = x.shape[0] // outer
    total = take_rows(x, place, rows).astype(jnp.float32)
    for k in range(1, outer):
        got = rotate(take_rows(x, (place + k) % outer, rows), size, k)
        total = total + got.astype(jnp.float32)
    return total.astype(jnp.bfloat16)


def gather_inner(x, size, bit):
    me = lax.axis_index("zslab")
    mine = (me // bit) % 2
    got = swap(x, size, bit)
    return jnp.where(mine == 0, jnp.concatenate([x, got]), jnp.concatenate([got, x]))


def gather_outer(x, size):
    me = lax.axis_index("zslab")
    outer = size // 4
    place = me // 4
    rows = x.shape[0]
    whole = jnp.zeros((outer * rows, x.shape[1]), x.dtype)
    for k, block in enumerate(outer_gather(x, size)):
        whole = lax.dynamic_update_slice_in_dim(whole, block, ((place - k) % outer) * rows, axis=0)
    return whole


def sum_terms(terms, size):
    part = scatter_inner(terms, size, 1)
    split = part.shape[0] * 16 // 27
    first, second = part[:split], part[split:]
    first = scatter_outer(scatter_inner(first, size, 2), size)
    second = scatter_inner(scatter_outer(second, size), size, 2)
    first = gather_inner(gather_outer(first, size), size, 2)
    second = gather_outer(gather_inner(second, size, 2), size)
    return gather_inner(jnp.concatenate([first, second]), size, 1)


def forward_conv(extended, weight):
    count = extended.shape[0]
    width = extended.shape[4]
    total = jnp.zeros((count * 512, weight.shape[2]), jnp.float32)
    for depth in range(3):
        for row in range(3):
            for col in range(3):
                piece = extended[:, depth : depth + 8, row : row + 8, col : col + 8].reshape(
                    count * 512, width
                )
                total = total + jnp.dot(
                    piece, weight[9 * depth + 3 * row + col], preferred_element_type=jnp.float32
                )
    return total


def transpose_conv(grad_ext, weight):
    count = grad_ext.shape[0]
    width = grad_ext.shape[4]
    total = jnp.zeros((count * 512, weight.shape[1]), jnp.float32)
    for depth in range(3):
        for row in range(3):
            for col in range(3):
                piece = grad_ext[
                    :, 2 - depth : 10 - depth, 2 - row : 10 - row, 2 - col : 10 - col
                ].reshape(count * 512, width)
                total = total + lax.dot_general(
                    piece,
                    weight[9 * depth + 3 * row + col],
                    (((1,), (1,)), ((), ())),
                    preferred_element_type=jnp.float32,
                )
    return total


def weight_terms(extended, grad_rows):
    count = extended.shape[0]
    width = extended.shape[4]
    terms = []
    for depth in range(3):
        for row in range(3):
            for col in range(3):
                piece = extended[:, depth : depth + 8, row : row + 8, col : col + 8].reshape(
                    count * 512, width
                )
                terms.append(
                    lax.dot_general(
                        piece,
                        grad_rows,
                        (((0,), (0,)), ((), ())),
                        preferred_element_type=jnp.float32,
                    )
                )
    return jnp.stack(terms, axis=0)


def per_device(size, feats, voxmask, links, weight, bias, cotangent):
    count = feats.shape[0]
    width = feats.shape[3]
    keep = (voxmask == 1).reshape(count, 8, 64, 1)
    masked = jnp.where(keep, feats, jnp.zeros_like(feats))
    rims = jnp.stack([masked[:, 0], masked[:, 7]], axis=1)
    halos = pick_halos(rims, links, size)
    extended = extend_with(masked, halos[:2], halos[2:])
    pre = forward_conv(extended, weight) + bias[None, :]
    keep_rows = keep.reshape(count * 512, 1)
    sigma = jax.nn.sigmoid(pre)
    output = jnp.where(keep_rows, pre * sigma, 0.0).astype(jnp.bfloat16)
    grad_pre = jnp.where(
        keep_rows,
        cotangent.reshape(count * 512, width).astype(jnp.float32)
        * sigma
        * (1.0 + pre * (1.0 - sigma)),
        0.0,
    ).astype(jnp.bfloat16)
    grad_planes = grad_pre.reshape(count, 8, 64, width)
    grad_edges = jnp.stack([grad_planes[:, 0], grad_planes[:, 7]], axis=1)
    grad_halos = pick_halos(grad_edges, links, size)
    grad_ext = extend_with(grad_planes, grad_halos[:2], grad_halos[2:])
    grad_feats = jnp.where(keep_rows, transpose_conv(grad_ext, weight), 0.0).astype(jnp.bfloat16)
    weight_local = weight_terms(extended, grad_pre)
    bias_local = jnp.sum(grad_pre.astype(jnp.float32), axis=0)
    bias_sum = lax.psum(bias_local, "zslab")
    terms = weight_local.reshape(-1, width).astype(jnp.bfloat16)
    grad_weight = sum_terms(terms, size).reshape(weight_local.shape)
    return (
        output.reshape(count, 8, 64, width),
        grad_feats.reshape(count, 8, 64, width),
        grad_weight,
        bias_sum,
    )


def solution(mesh):
    return jax.shard_map(
        functools.partial(per_device, mesh.shape["zslab"]),
        mesh=mesh,
        in_specs=(
            P(("groups", "zslab"), None, None, None),
            P(("groups", "zslab"), None),
            P(("groups", "zslab"), None),
            P(),
            P(),
            P(("groups", "zslab"), None, None, None),
        ),
        out_specs=(
            P(("groups", "zslab"), None, None, None),
            P(("groups", "zslab"), None, None, None),
            P("groups", None, None),
            P("groups"),
        ),
        check_vma=False,
    )
```

```python
import functools

import jax
import jax.numpy as jnp
from jax import lax
from jax.experimental import pallas as pl
from jax.experimental.pallas import tpu as pltpu
from jax.sharding import PartitionSpec as P

VMEM_LIMIT = 56 * 1024 * 1024
SIDES = (1, 1, 0, 0)


def params():
    return pltpu.CompilerParams(vmem_limit_bytes=VMEM_LIMIT)


def cost(flops, bytes_accessed):
    return pl.CostEstimate(flops=flops, bytes_accessed=bytes_accessed, transcendentals=0)


def swap(x, size, bit):
    return lax.ppermute(x, "zslab", [(i, i ^ bit) for i in range(size)])


def rotate(x, size, steps):
    return lax.ppermute(x, "zslab", [(i, (i + 4 * steps) % size) for i in range(size)])


def wanted(links):
    return links.T.reshape(4)


def route(links, size):
    me = lax.axis_index("zslab")
    side = jnp.array(SIDES, jnp.int32)
    places = []
    for steps in range(size // 4):
        want = wanted(links if steps == 0 else rotate(links, size, -steps))
        owner = jnp.maximum(want, 0) // 2
        group = ((owner % 2) ^ (me % 2)) * 2 + (((owner // 2) % 2) ^ ((me // 2) % 2))
        places.append((group * 2 + jnp.maximum(want, 0) % 2) * 2 + side)
    return places


def fetch_halos(rims, links, places, size):
    me = lax.axis_index("zslab")
    pair = jnp.concatenate([rims, swap(rims, size, 2)], axis=0)
    group = jnp.concatenate([pair, swap(pair, size, 1)], axis=0)
    planes = group.reshape(16, 64, rims.shape[-1])
    outer = size // 4
    want = wanted(links)
    step = (me // 4 - jnp.maximum(want, 0) // 8) % outer
    halos = jnp.zeros((4, 64, rims.shape[-1]), rims.dtype)
    for steps in range(outer):
        got = jnp.take(planes, places[steps], axis=0)
        if steps:
            got = rotate(got, size, steps)
        here = (step == steps) & (want >= 0)
        halos = jnp.where(here[:, None, None], got, halos)
    return halos


def take_rows(x, place, rows):
    return lax.dynamic_slice_in_dim(x, place * rows, rows, axis=0)


def scatter_inner(x, size):
    me = lax.axis_index("zslab")
    mine = (me // 2) % 2
    half = x.shape[0] // 2
    got = swap(take_rows(x, 1 - mine, half), size, 2)
    return (take_rows(x, mine, half).astype(jnp.float32) + got.astype(jnp.float32)).astype(jnp.bfloat16)


def scatter_outer(x, size):
    place = lax.axis_index("zslab") // 4
    outer = size // 4
    rows = x.shape[0] // outer
    total = take_rows(x, place, rows).astype(jnp.float32)
    for steps in range(1, outer):
        got = rotate(take_rows(x, (place + steps) % outer, rows), size, steps)
        total = total + got.astype(jnp.float32)
    return total.astype(jnp.bfloat16)


def gather_outer(x, size):
    place = lax.axis_index("zslab") // 4
    outer = size // 4
    rows = x.shape[0]
    whole = jnp.zeros((outer * rows, x.shape[1]), x.dtype)
    for steps in range(outer):
        block = x if steps == 0 else rotate(x, size, steps)
        whole = lax.dynamic_update_slice_in_dim(whole, block, ((place - steps) % outer) * rows, axis=0)
    return whole


def gather_inner(x, size):
    mine = (lax.axis_index("zslab") // 2) % 2
    got = swap(x, size, 2)
    return jnp.where(mine == 0, jnp.concatenate([x, got]), jnp.concatenate([got, x]))


def shifted(x, rows, cols):
    count = x.shape[0]
    index = lax.broadcasted_iota(jnp.int32, x.shape, 0)
    row = (index // 8) % 8 + rows
    col = index % 8 + cols
    move = 8 * rows + cols
    if move:
        x = pltpu.roll(x, (-move) % count, 0)
    inside = (row >= 0) & (row < 8) & (col >= 0) & (col < 8)
    return jnp.where(inside, x, 0.0)


def shifted_lanes(x, rows, cols):
    index = lax.broadcasted_iota(jnp.int32, x.shape, 1)
    row = (index // 8) % 8 + rows
    col = index % 8 + cols
    move = 8 * rows + cols
    if move:
        x = pltpu.roll(x, (-move) % x.shape[1], 1)
    inside = (row >= 0) & (row < 8) & (col >= 0) & (col < 8)
    return jnp.where(inside, x, 0.0)


def both(ref, z):
    return jnp.concatenate([ref[0, z], ref[1, z]], axis=0)


def wide(mask):
    return jnp.concatenate([mask, mask], axis=1) > 0


def activate(pre, cotangent, keep):
    sigma = 1.0 / (1.0 + jnp.exp(-pre))
    out = jnp.where(keep, pre * sigma, 0.0)
    grad = jnp.where(keep, cotangent * sigma * (1.0 + pre * (1.0 - sigma)), 0.0)
    return out, grad


def forward_kernel(feats, mask, weight, bias, cotangent, out, grad, edge, bias_sum, cols, pre):
    width = feats.shape[3]

    def fill(z, carry):
        keep = wide(mask[pl.ds(pl.multiple_of(z * 128, 128), 128), :])
        plane = jnp.where(keep, both(feats, z).astype(jnp.float32), 0.0)
        for p in range(3):
            for q in range(3):
                at = (3 * p + q) * width
                cols[pl.ds(pl.multiple_of(z * 128, 128), 128), at : at + width] = shifted(
                    plane, p - 1, q - 1
                ).astype(jnp.bfloat16)
        return carry

    lax.fori_loop(0, 8, fill, 0)
    taps = [weight[9 * a : 9 * a + 9].reshape(9 * width, width) for a in range(3)]
    pre[...] = jnp.dot(cols[...], taps[1], preferred_element_type=jnp.float32) + bias[...]
    pre[128:, :] += jnp.dot(cols[:896, :], taps[0], preferred_element_type=jnp.float32)
    pre[:896, :] += jnp.dot(cols[128:, :], taps[2], preferred_element_type=jnp.float32)
    edge[0] = pre[:128, :]
    edge[1] = pre[896:, :]
    bias_sum[...] = jnp.zeros_like(bias_sum)

    def finish(z, carry):
        rows = pl.ds(pl.multiple_of(z * 128, 128), 128)
        keep = wide(mask[rows, :])
        act, slope = activate(pre[rows, :], both(cotangent, z).astype(jnp.float32), keep)
        act = act.astype(jnp.bfloat16)
        slope = slope.astype(jnp.bfloat16)
        for b in range(2):
            out[b, z] = act[64 * b : 64 * b + 64]
            grad[b, z] = slope[64 * b : 64 * b + 64]
        bias_sum[...] += jnp.sum(slope.astype(jnp.float32), axis=0, keepdims=True)
        return carry

    lax.fori_loop(1, 7, finish, 0)


def forward_inside(feats, mask, weight, bias, cotangent):
    width = feats.shape[3]
    shape = jax.ShapeDtypeStruct(feats.shape, jnp.bfloat16)
    return pl.pallas_call(
        forward_kernel,
        out_shape=(
            shape,
            shape,
            jax.ShapeDtypeStruct((2, 128, width), jnp.float32),
            jax.ShapeDtypeStruct((1, width), jnp.float32),
        ),
        scratch_shapes=[
            pltpu.VMEM((1024, 9 * width), jnp.bfloat16),
            pltpu.VMEM((1024, width), jnp.float32),
        ],
        compiler_params=params(),
        cost_estimate=cost(2 * 1024 * 27 * width * width, 6 * 1024 * 1024),
        name="forward_inside",
    )(feats, mask, weight, bias, cotangent)


def edge_kernel(halos, mask, weight, edge, cotangent, inside, out_in, grad_in, out, grad, rims, bias_sum):
    width = halos.shape[3]
    side = pl.program_id(0)
    halo = jnp.concatenate([halos[0, 0], halos[0, 1]], axis=0).astype(jnp.float32)
    cols = jnp.concatenate(
        [shifted(halo, p - 1, q - 1).astype(jnp.bfloat16) for p in range(3) for q in range(3)], axis=1
    )
    taps = weight[...].reshape(9 * width, width)
    pre = edge[0] + jnp.dot(cols, taps, preferred_element_type=jnp.float32)
    act, slope = activate(pre, both(cotangent, 0).astype(jnp.float32), wide(mask[...]))
    act = act.astype(jnp.bfloat16)
    slope = slope.astype(jnp.bfloat16)
    for b in range(2):
        out[b, 0] = act[64 * b : 64 * b + 64]
        grad[b, 0] = slope[64 * b : 64 * b + 64]
        rims[b, 0] = slope[64 * b : 64 * b + 64]

    @pl.when(side == 0)
    def _():
        bias_sum[...] = inside[...]

    bias_sum[...] += jnp.sum(slope.astype(jnp.float32), axis=0, keepdims=True)


def forward_edges(halos, mask, weight, edge, cotangent, inside, out, grad):
    width = halos.shape[2]
    plane = pl.BlockSpec((2, 1, 64, width), lambda i: (0, 7 * i, 0, 0))
    once = pl.BlockSpec((1, width), lambda i: (0, 0))
    return pl.pallas_call(
        edge_kernel,
        grid=(2,),
        in_specs=[
            pl.BlockSpec((1, 2, 64, width), lambda i: (i, 0, 0, 0)),
            pl.BlockSpec((128, 128), lambda i: (7 * i, 0)),
            pl.BlockSpec((9, width, width), lambda i: (2 * i, 0, 0)),
            pl.BlockSpec((1, 128, width), lambda i: (i, 0, 0)),
            plane,
            once,
            pl.BlockSpec(memory_space=pl.ANY),
            pl.BlockSpec(memory_space=pl.ANY),
        ],
        out_specs=(
            plane,
            plane,
            pl.BlockSpec((2, 1, 64, width), lambda i: (0, i, 0, 0)),
            once,
        ),
        out_shape=(
            jax.ShapeDtypeStruct(out.shape, out.dtype),
            jax.ShapeDtypeStruct(grad.shape, grad.dtype),
            jax.ShapeDtypeStruct((2, 2, 64, width), jnp.bfloat16),
            jax.ShapeDtypeStruct((1, width), jnp.float32),
        ),
        input_output_aliases={6: 0, 7: 1},
        compiler_params=params(),
        cost_estimate=cost(2 * 256 * 9 * width * width, 3 * 1024 * 1024),
        name="forward_edges",
    )(halos.reshape(2, 2, 64, width), mask, weight, edge, cotangent, inside, out, grad)


def turned_kernel(mine, theirs, turned):
    half = mine.shape[3]

    def fill(z, carry):
        for who, ref in ((0, mine), (1, theirs)):
            plane = both(ref, z).astype(jnp.float32).T
            for p in range(3):
                for q in range(3):
                    at = (3 * p + q) * half
                    turned[at : at + half, pl.ds(pl.multiple_of(who * 1024 + z * 128, 128), 128)] = shifted_lanes(
                        plane, p - 1, q - 1
                    ).astype(jnp.bfloat16)
        return carry

    lax.fori_loop(0, 8, fill, 0)


def turn_features(mine, theirs):
    half = mine.shape[3]
    return pl.pallas_call(
        turned_kernel,
        out_shape=jax.ShapeDtypeStruct((9 * half, 2048), jnp.bfloat16),
        compiler_params=params(),
        cost_estimate=cost(0, 16 * 1024 * 1024),
        name="turn_features",
    )(mine, theirs)


def weight_kernel(turned, halos, their_halos, grad, their_grad, terms, rows, ends):
    half = halos.shape[2]

    def order(z, carry):
        for who, ref in ((0, grad), (1, their_grad)):
            rows[pl.ds(pl.multiple_of(who * 1024 + z * 128, 128), 128), :] = both(ref, z)
        return carry

    lax.fori_loop(0, 8, order, 0)
    for who, ref in ((0, halos), (1, their_halos)):
        for side in range(2):
            plane = jnp.concatenate([ref[2 * side], ref[2 * side + 1]], axis=0).astype(jnp.float32).T
            for p in range(3):
                for q in range(3):
                    at = (3 * p + q) * half
                    ends[side, at : at + half, who * 128 : who * 128 + 128] = shifted_lanes(
                        plane, p - 1, q - 1
                    ).astype(jnp.bfloat16)
    terms[1] = jnp.dot(turned[...], rows[...], preferred_element_type=jnp.float32).astype(jnp.bfloat16)
    for a, side in ((0, 0), (2, 1)):
        first = 0 if a == 0 else 128
        other = 128 - first
        total = jnp.dot(
            turned[:, first : first + 896], rows[other : other + 896, :], preferred_element_type=jnp.float32
        )
        total += jnp.dot(
            turned[:, 1024 + first : 1920 + first],
            rows[1024 + other : 1920 + other, :],
            preferred_element_type=jnp.float32,
        )
        rim = 0 if a == 0 else 896
        facing = jnp.concatenate([rows[rim : rim + 128, :], rows[1024 + rim : 1152 + rim, :]], axis=0)
        total += jnp.dot(ends[side], facing, preferred_element_type=jnp.float32)
        terms[a] = total.astype(jnp.bfloat16)


def weight_terms(turned, halos, their_halos, grad, their_grad):
    half = halos.shape[2]
    width = grad.shape[3]
    return pl.pallas_call(
        weight_kernel,
        out_shape=jax.ShapeDtypeStruct((3, 9 * half, width), jnp.bfloat16),
        scratch_shapes=[
            pltpu.VMEM((2048, width), jnp.bfloat16),
            pltpu.VMEM((2, 9 * half, 256), jnp.bfloat16),
        ],
        compiler_params=params(),
        cost_estimate=cost(2 * 2048 * 27 * half * width, 8 * 1024 * 1024),
        name="weight_terms",
    )(turned, halos, their_halos, grad, their_grad)


def backward_kernel(grad, halos, mask, weight, grad_feats, cols, total):
    width = grad.shape[3]

    def spread(plane, place):
        for p in range(3):
            for q in range(3):
                at = (3 * p + q) * width
                cols[pl.ds(pl.multiple_of(place, 128), 128), at : at + width] = shifted(
                    plane.astype(jnp.float32), 1 - p, 1 - q
                ).astype(jnp.bfloat16)

    def fill(z, carry):
        spread(both(grad, z), (z + 1) * 128)
        return carry

    spread(jnp.concatenate([halos[0], halos[1]], axis=0), 0)
    spread(jnp.concatenate([halos[2], halos[3]], axis=0), 1152)
    lax.fori_loop(0, 8, fill, 0)
    total[...] = jnp.zeros_like(total)

    def add(tap, carry):
        a, pq = tap // 9, tap % 9
        piece = cols[pl.ds(pl.multiple_of((2 - a) * 128, 128), 1024), pl.ds(pl.multiple_of(pq * width, 128), width)]
        total[...] += lax.dot_general(
            piece, weight[tap], (((1,), (1,)), ((), ())), preferred_element_type=jnp.float32
        )
        return carry

    lax.fori_loop(0, 27, add, 0)

    def finish(z, carry):
        rows = pl.ds(pl.multiple_of(z * 128, 128), 128)
        done = jnp.where(wide(mask[rows, :]), total[rows, :], 0.0).astype(jnp.bfloat16)
        for b in range(2):
            grad_feats[b, z] = done[64 * b : 64 * b + 64]
        return carry

    lax.fori_loop(0, 8, finish, 0)


def backward(grad, halos, mask, weight):
    width = grad.shape[3]
    return pl.pallas_call(
        backward_kernel,
        out_shape=jax.ShapeDtypeStruct(grad.shape, jnp.bfloat16),
        scratch_shapes=[
            pltpu.VMEM((1280, 9 * width), jnp.bfloat16),
            pltpu.VMEM((1024, width), jnp.float32),
        ],
        compiler_params=params(),
        cost_estimate=cost(2 * 1024 * 27 * width * width, 6 * 1024 * 1024),
        name="backward",
    )(grad, halos, mask, weight)


def per_device(size, feats, voxmask, links, weight, bias, cotangent):
    width = feats.shape[3]
    half = width // 2
    core = lax.axis_index("zslab") % 2
    keep = (voxmask == 1).reshape(2, 8, 64, 1)
    rims = jnp.stack([feats[:, 0], feats[:, 7]], axis=1)
    rims = jnp.where(jnp.stack([keep[:, 0], keep[:, 7]], axis=1), rims, jnp.zeros_like(rims))
    places = route(links, size)
    halos = fetch_halos(rims, links, places, size)

    mask = jnp.broadcast_to(keep.transpose(1, 0, 2, 3).astype(jnp.float32).reshape(1024, 1), (1024, 128))
    halves = jnp.where(keep, feats, jnp.zeros_like(feats)).reshape(2, 8, 64, 2, half)
    own = jnp.where(core == 0, halves[..., 0, :], halves[..., 1, :])
    give = jnp.where(core == 0, halves[..., 1, :], halves[..., 0, :])
    turned = turn_features(own, swap(give, size, 1))

    out, grad, edge, inside = forward_inside(feats, mask, weight, bias.reshape(1, width), cotangent)
    out, grad, grad_rims, bias_local = forward_edges(halos, mask, weight, edge, cotangent, inside, out, grad)
    grad_bias = jnp.sum(lax.all_gather(bias_local, "zslab", axis=0, tiled=True), axis=0)

    halves = halos.reshape(4, 64, 2, half)
    own_halos = jnp.where(core == 0, halves[..., 0, :], halves[..., 1, :])
    their_halos = swap(jnp.where(core == 0, halves[..., 1, :], halves[..., 0, :]), size, 1)
    terms = weight_terms(turned, own_halos, their_halos, grad, swap(grad, size, 1))

    grad_halos = fetch_halos(grad_rims, links, places, size)
    grad_feats = backward(grad, grad_halos, mask, weight)

    parts = []
    for a in range(3):
        part = scatter_outer(scatter_inner(terms[a], size), size)
        part = gather_inner(gather_outer(part, size), size)
        other = swap(part, size, 1)
        part = part.reshape(9, 1, half, width)
        other = other.reshape(9, 1, half, width)
        parts.append(
            jnp.where(
                core == 0, jnp.concatenate([part, other], axis=1), jnp.concatenate([other, part], axis=1)
            ).reshape(9, width, width)
        )
    grad_weight = jnp.concatenate(parts, axis=0)
    return out, grad_feats, grad_weight, grad_bias


def solution(mesh):
    return jax.shard_map(
        functools.partial(per_device, mesh.shape["zslab"]),
        mesh=mesh,
        in_specs=(
            P(("groups", "zslab"), None, None, None),
            P(("groups", "zslab"), None),
            P(("groups", "zslab"), None),
            P(),
            P(),
            P(("groups", "zslab"), None, None, None),
        ),
        out_specs=(
            P(("groups", "zslab"), None, None, None),
            P(("groups", "zslab"), None, None, None),
            P("groups", None, None),
            P("groups"),
        ),
        check_vma=False,
    )
```

```python
import functools

import jax
import jax.numpy as jnp
from jax import lax
from jax.experimental import pallas as pl
from jax.experimental.pallas import tpu as pltpu
from jax.sharding import PartitionSpec as P

VMEM_LIMIT = 56 * 1024 * 1024
SIDES = (1, 1, 0, 0)


def params():
    return pltpu.CompilerParams(vmem_limit_bytes=VMEM_LIMIT)


def cost(flops, bytes_accessed):
    return pl.CostEstimate(flops=flops, bytes_accessed=bytes_accessed, transcendentals=0)


def swap(x, size, bit):
    return lax.ppermute(x, "zslab", [(i, i ^ bit) for i in range(size)])


def rotate(x, size, steps):
    return lax.ppermute(x, "zslab", [(i, (i + 4 * steps) % size) for i in range(size)])


def wanted(links):
    return links.T.reshape(4)


def exact_terms(x):
    high = lax.reduce_precision(x, 8, 7)
    middle = lax.reduce_precision(x - high, 8, 7)
    low = x - high - middle
    return [term.astype(jnp.bfloat16) for term in (high, middle, low)]


def sum_terms(rows):
    return jnp.sum(rows.astype(jnp.float32), axis=tuple(range(rows.ndim - 1)))


def extra_rows(rows):
    rows = jnp.stack(rows)
    return jnp.concatenate([rows, jnp.zeros((16 - rows.shape[0], rows.shape[1]), rows.dtype)])


def gather_group(x, size, first):
    second = 3 - first
    pair = jnp.stack([x, swap(x, size, first)])
    other = swap(pair, size, second)
    if first == 1:
        return jnp.concatenate([pair, other])
    return jnp.stack([pair[0], other[0], pair[1], other[1]])


def group_links(codes, size):
    return codes[:, :4].astype(jnp.int32).reshape(16)


def pick_kernel(outer, where, links, planes, picks, table):
    for place in range(outer * 4):
        table[place] = 0
    for plane in range(16):
        dev, brick, side = plane // 4, plane // 2 % 2, plane % 2
        dest = links[dev * 4 + brick * 2 + side]

        @pl.when((dest >= 0) & ((dest // 2) % 4 == where[1]))
        def _():
            steps = lax.rem(dest // 8 - where[0] + outer, outer)
            slot = dest % 2 + (0 if side == 1 else 2)
            table[steps * 4 + slot] = plane

    def copy(place, carry):
        source = table[place]
        picks[place // 4, pl.ds(pl.multiple_of((place % 4) * 64, 64), 64), :] = planes[
            source // 4, pl.ds(pl.multiple_of((source % 4) * 64, 64), 64), :
        ]
        return carry

    lax.fori_loop(0, outer * 4, copy, 0)


def pick(links, planes, size):
    me = lax.axis_index("zslab")
    outer = size // 4
    where = jnp.stack([me // 4, me % 4]).astype(jnp.int32)
    smem = pl.BlockSpec(memory_space=pltpu.SMEM)
    return pl.pallas_call(
        functools.partial(pick_kernel, outer),
        in_specs=[smem, smem, pl.BlockSpec(memory_space=pltpu.VMEM)],
        out_shape=jax.ShapeDtypeStruct((outer, 256, planes.shape[2]), planes.dtype),
        scratch_shapes=[pltpu.SMEM((outer * 4,), jnp.int32)],
        compiler_params=params(),
        cost_estimate=cost(0, 2 * 1024 * 1024),
        name="pick_planes",
    )(where, links, planes)


def spread_picks(picks, links, size):
    me = lax.axis_index("zslab")
    outer = size // 4
    want = wanted(links)
    step = (me // 4 - jnp.maximum(want, 0) // 8) % outer
    halos = jnp.zeros((4, 64, picks[0].shape[1]), picks[0].dtype)
    extra = []
    for steps in range(outer):
        got = rotate(picks[steps], size, steps) if steps else picks[0]
        here = (step == steps) & (want >= 0)
        halos = jnp.where(here[:, None, None], got[:256].reshape(halos.shape), halos)
        extra.append(got[256:])
    return halos, extra


def take_rows(x, place, rows):
    return lax.dynamic_slice_in_dim(x, place * rows, rows, axis=0)


def bits(size):
    return [1 << k for k in range(1, size.bit_length() - 1)]


def halve(keep, got, size, bit):
    mine = (lax.axis_index("zslab") // bit) % 2
    half = keep.shape[0] // 2
    give = take_rows(keep, 1 - mine, half) + take_rows(got, 1 - mine, half).astype(jnp.float32)
    stay = take_rows(keep, mine, half) + take_rows(got, mine, half).astype(jnp.float32)
    return give.astype(jnp.bfloat16), stay


def sum_and_gather(give, stay, size):
    order = bits(size)
    got = swap(give, size, order[0])
    for bit in order[1:]:
        give, stay = halve(stay, got, size, bit)
        got = swap(give, size, bit)
    whole = (stay + got.astype(jnp.float32)).astype(jnp.bfloat16)
    for bit in reversed(order):
        mine = (lax.axis_index("zslab") // bit) % 2
        got = swap(whole, size, bit)
        whole = jnp.where(mine == 0, jnp.concatenate([whole, got]), jnp.concatenate([got, whole]))
    return whole


def shifted(x, rows, cols):
    count = x.shape[0]
    index = lax.broadcasted_iota(jnp.int32, x.shape, 0)
    row = (index // 8) % 8 + rows
    col = index % 8 + cols
    move = 8 * rows + cols
    if move:
        x = pltpu.roll(x, (-move) % count, 0)
    inside = (row >= 0) & (row < 8) & (col >= 0) & (col < 8)
    return jnp.where(inside, x, 0.0)


def shifted_lanes(x, rows, cols):
    index = lax.broadcasted_iota(jnp.int32, x.shape, 1)
    row = (index // 8) % 8 + rows
    col = index % 8 + cols
    move = 8 * rows + cols
    if move:
        x = pltpu.roll(x, (-move) % x.shape[1], 1)
    inside = (row >= 0) & (row < 8) & (col >= 0) & (col < 8)
    return jnp.where(inside, x, 0.0)


def both(ref, z):
    return jnp.concatenate([ref[0, z], ref[1, z]], axis=0)


def wide(mask):
    return jnp.concatenate([mask, mask], axis=1) > 0


def activate(pre, cotangent, keep):
    sigma = 1.0 / (1.0 + jnp.exp(-pre))
    out = jnp.where(keep, pre * sigma, 0.0)
    grad = jnp.where(keep, cotangent * sigma * (1.0 + pre * (1.0 - sigma)), 0.0)
    return out, grad


def forward_kernel(feats, mask, weight, bias, cotangent, out, grad, edge, bias_sum, cols, pre):
    width = feats.shape[3]

    def fill(z, carry):
        keep = wide(mask[pl.ds(pl.multiple_of(z * 128, 128), 128), :])
        plane = jnp.where(keep, both(feats, z).astype(jnp.float32), 0.0)
        for p in range(3):
            for q in range(3):
                at = (3 * p + q) * width
                cols[pl.ds(pl.multiple_of(z * 128, 128), 128), at : at + width] = shifted(
                    plane, p - 1, q - 1
                ).astype(jnp.bfloat16)
        return carry

    lax.fori_loop(0, 8, fill, 0)
    taps = [weight[9 * a : 9 * a + 9].reshape(9 * width, width) for a in range(3)]
    pre[...] = jnp.dot(cols[...], taps[1], preferred_element_type=jnp.float32) + bias[...]
    pre[128:, :] += jnp.dot(cols[:896, :], taps[0], preferred_element_type=jnp.float32)
    pre[:896, :] += jnp.dot(cols[128:, :], taps[2], preferred_element_type=jnp.float32)
    edge[0] = pre[:128, :]
    edge[1] = pre[896:, :]
    bias_sum[...] = jnp.zeros_like(bias_sum)

    def finish(z, carry):
        rows = pl.ds(pl.multiple_of(z * 128, 128), 128)
        keep = wide(mask[rows, :])
        act, slope = activate(pre[rows, :], both(cotangent, z).astype(jnp.float32), keep)
        act = act.astype(jnp.bfloat16)
        slope = slope.astype(jnp.bfloat16)
        for b in range(2):
            out[b, z] = act[64 * b : 64 * b + 64]
        grad[pl.ds(pl.multiple_of((z - 1) * 128, 128), 128), :] = slope
        bias_sum[...] += jnp.sum(slope.astype(jnp.float32), axis=0, keepdims=True)
        return carry

    lax.fori_loop(1, 7, finish, 0)


def forward_inside(feats, mask, weight, bias, cotangent):
    width = feats.shape[3]
    return pl.pallas_call(
        forward_kernel,
        out_shape=(
            jax.ShapeDtypeStruct(feats.shape, jnp.bfloat16),
            jax.ShapeDtypeStruct((768, width), jnp.bfloat16),
            jax.ShapeDtypeStruct((2, 128, width), jnp.float32),
            jax.ShapeDtypeStruct((1, width), jnp.float32),
        ),
        scratch_shapes=[
            pltpu.VMEM((1024, 9 * width), jnp.bfloat16),
            pltpu.VMEM((1024, width), jnp.float32),
        ],
        compiler_params=params(),
        cost_estimate=cost(2 * 1024 * 27 * width * width, 6 * 1024 * 1024),
        name="forward_inside",
    )(feats, mask, weight, bias, cotangent)


def edge_kernel(halos, mask, weight, edge, cotangent, inside, out_in, out, rims, bias_sum):
    width = halos.shape[2]
    side = pl.program_id(0)
    halo = halos[0].astype(jnp.float32)
    cols = jnp.concatenate(
        [shifted(halo, p - 1, q - 1).astype(jnp.bfloat16) for p in range(3) for q in range(3)], axis=1
    )
    taps = weight[...].reshape(9 * width, width)
    pre = edge[0] + jnp.dot(cols, taps, preferred_element_type=jnp.float32)
    act, slope = activate(pre, both(cotangent, 0).astype(jnp.float32), wide(mask[...]))
    act = act.astype(jnp.bfloat16)
    slope = slope.astype(jnp.bfloat16)
    for b in range(2):
        out[b, 0] = act[64 * b : 64 * b + 64]
        rims[b, 0] = slope[64 * b : 64 * b + 64]

    @pl.when(side == 0)
    def _():
        bias_sum[...] = inside[...]

    bias_sum[...] += jnp.sum(slope.astype(jnp.float32), axis=0, keepdims=True)


def forward_edges(halos, mask, weight, edge, cotangent, inside, out):
    width = halos.shape[2]
    plane = pl.BlockSpec((2, 1, 64, width), lambda i: (0, 7 * i, 0, 0))
    once = pl.BlockSpec((1, width), lambda i: (0, 0))
    return pl.pallas_call(
        edge_kernel,
        grid=(2,),
        in_specs=[
            pl.BlockSpec((1, 128, width), lambda i: (i, 0, 0)),
            pl.BlockSpec((128, 128), lambda i: (7 * i, 0)),
            pl.BlockSpec((9, width, width), lambda i: (2 * i, 0, 0)),
            pl.BlockSpec((1, 128, width), lambda i: (i, 0, 0)),
            plane,
            once,
            pl.BlockSpec(memory_space=pl.ANY),
        ],
        out_specs=(plane, pl.BlockSpec((2, 1, 64, width), lambda i: (0, i, 0, 0)), once),
        out_shape=(
            jax.ShapeDtypeStruct(out.shape, out.dtype),
            jax.ShapeDtypeStruct((2, 2, 64, width), jnp.bfloat16),
            jax.ShapeDtypeStruct((1, width), jnp.float32),
        ),
        input_output_aliases={6: 0},
        compiler_params=params(),
        cost_estimate=cost(2 * 256 * 9 * width * width, 3 * 1024 * 1024),
        name="forward_edges",
    )(halos.reshape(2, 128, width), mask, weight, edge, cotangent, inside, out)


def turned_kernel(ref, turned):
    half = ref.shape[3]

    def fill(z, carry):
        plane = both(ref, z).astype(jnp.float32).T
        for p in range(3):
            for q in range(3):
                at = (3 * p + q) * half
                turned[at : at + half, pl.ds(pl.multiple_of(z * 128, 128), 128)] = shifted_lanes(
                    plane, p - 1, q - 1
                ).astype(jnp.bfloat16)
        return carry

    lax.fori_loop(0, 8, fill, 0)


def turn_features(feats):
    half = feats.shape[3]
    return pl.pallas_call(
        turned_kernel,
        out_shape=jax.ShapeDtypeStruct((9 * half, 1024), jnp.bfloat16),
        compiler_params=params(),
        cost_estimate=cost(0, 6 * 1024 * 1024),
        name="turn_features",
    )(feats)


def inner_terms_kernel(mine, theirs, grad, their_grad, terms):
    for a in range(3):
        lanes = slice(128 * a, 128 * a + 768)
        terms[a] = jnp.dot(mine[:, lanes], grad[...], preferred_element_type=jnp.float32)
        terms[a] += jnp.dot(theirs[:, lanes], their_grad[...], preferred_element_type=jnp.float32)


def inner_terms(mine, theirs, grad, their_grad):
    rows, width = mine.shape[0], grad.shape[1]
    return pl.pallas_call(
        inner_terms_kernel,
        out_shape=jax.ShapeDtypeStruct((3, rows, width), jnp.float32),
        compiler_params=params(),
        cost_estimate=cost(2 * 1536 * 3 * rows * width, 8 * 1024 * 1024),
        name="inner_terms",
    )(mine, theirs, grad, their_grad)


def outer_terms_kernel(a, upper, mine_low, theirs_low, mine_high, theirs_high, rims, inner, give, stay, cols, total):
    half = cols.shape[0] // 9
    for place, ref in enumerate((mine_low, theirs_low, mine_high, theirs_high)):
        lanes = slice(128 * place, 128 * place + 128)
        if ref.shape[0] == 128:
            plane = ref[...].astype(jnp.float32).T
            for p in range(3):
                for q in range(3):
                    at = (3 * p + q) * half
                    cols[at : at + half, lanes] = shifted_lanes(plane, p - 1, q - 1).astype(jnp.bfloat16)
        else:
            cols[:, lanes] = ref[...]
    total[...] = inner[0] + jnp.dot(cols[...], rims[...], preferred_element_type=jnp.float32)
    rows = give.shape[0]
    mine = upper[0]
    give[...] = total[pl.ds(pl.multiple_of((1 - mine) * rows, 16), rows), :].astype(jnp.bfloat16)
    stay[...] = total[pl.ds(pl.multiple_of(mine * rows, 16), rows), :]


def outer_terms(a, mine, theirs, halos, their_halos, rims, inner, size):
    rows, width = inner.shape[1], inner.shape[2]
    half = rows // 9
    first = bits(size)[0]
    upper = ((lax.axis_index("zslab") // first) % 2).astype(jnp.int32).reshape(1)

    def lanes(place):
        return pl.BlockSpec((rows, 128), lambda i: (0, place))

    def halo(side):
        return pl.BlockSpec((128, half), lambda i: (side, 0))

    low = (halos, their_halos, halo(0)) if a == 0 else (mine, theirs, lanes(a - 1))
    high = (halos, their_halos, halo(1)) if a == 2 else (mine, theirs, lanes(6 + a))
    return pl.pallas_call(
        functools.partial(outer_terms_kernel, a),
        grid=(1,),
        in_specs=[
            pl.BlockSpec(memory_space=pltpu.SMEM),
            low[2],
            low[2],
            high[2],
            high[2],
            pl.BlockSpec((512, width), lambda i: (0, 0)),
            pl.BlockSpec((1, rows, width), lambda i: (a, 0, 0)),
        ],
        out_specs=(
            pl.BlockSpec((rows // 2, width), lambda i: (0, 0)),
            pl.BlockSpec((rows // 2, width), lambda i: (0, 0)),
        ),
        out_shape=(
            jax.ShapeDtypeStruct((rows // 2, width), jnp.bfloat16),
            jax.ShapeDtypeStruct((rows // 2, width), jnp.float32),
        ),
        scratch_shapes=[pltpu.VMEM((rows, 512), jnp.bfloat16), pltpu.VMEM((rows, width), jnp.float32)],
        compiler_params=params(),
        cost_estimate=cost(2 * 512 * rows * width, 4 * 1024 * 1024),
        name="outer_terms",
    )(upper, low[0], low[1], high[0], high[1], rims, inner)


def backward_kernel(first, last, grad, rims, halos, mask, weight, *rest):
    grad_feats, cols = rest[-2:]
    width = grad.shape[1]
    place = 0
    for plane in range(first - 1, last + 2):
        if plane < 0 or plane > 7:
            rows = halos[(0 if plane < 0 else 128) : (128 if plane < 0 else 256)]
        elif plane in (0, 7):
            side = plane // 7
            rows = jnp.concatenate([rims[0, side], rims[1, side]], axis=0)
        else:
            rows = grad[128 * (plane - 1) : 128 * plane]
        rows = rows.astype(jnp.float32)
        for p in range(3):
            for q in range(3):
                at = (3 * p + q) * width
                cols[place : place + 128, at : at + width] = shifted(rows, 1 - p, 1 - q).astype(jnp.bfloat16)
        place += 128
    count = 128 * (last - first + 1)
    total = jnp.zeros((count, width), jnp.float32)
    for a in range(3):
        for pq in range(9):
            piece = cols[(2 - a) * 128 : (2 - a) * 128 + count, pq * width : (pq + 1) * width]
            total += lax.dot_general(
                piece, weight[9 * a + pq], (((1,), (1,)), ((), ())), preferred_element_type=jnp.float32
            )
    for z in range(last - first + 1):
        rows = slice(128 * z, 128 * z + 128)
        done = jnp.where(wide(mask[rows, :]), total[rows, :], 0.0).astype(jnp.bfloat16)
        for b in range(2):
            grad_feats[b, z] = done[64 * b : 64 * b + 64]


def backward(first, last, grad, rims, halos, mask, weight, done):
    width = grad.shape[1]
    count = last - first + 1
    block = first // count

    def whole(x):
        return pl.BlockSpec(x.shape, lambda i: (0,) * x.ndim)

    given = [grad, rims, halos, mask, weight] + ([] if done is None else [done])
    return pl.pallas_call(
        functools.partial(backward_kernel, first, last),
        grid=(1,),
        in_specs=[
            whole(grad),
            whole(rims),
            whole(halos),
            pl.BlockSpec((128 * count, 128), lambda i: (block, 0)),
            whole(weight),
        ]
        + ([] if done is None else [pl.BlockSpec(memory_space=pl.ANY)]),
        out_specs=pl.BlockSpec((2, count, 64, width), lambda i: (0, block, 0, 0)),
        out_shape=jax.ShapeDtypeStruct((2, 8, 64, width), jnp.bfloat16),
        scratch_shapes=[pltpu.VMEM((128 * (count + 2), 9 * width), jnp.bfloat16)],
        input_output_aliases={} if done is None else {5: 0},
        compiler_params=params(),
        cost_estimate=cost(2 * 128 * count * 27 * width * width, 5 * 1024 * 1024),
        name="backward",
    )(*given)


def per_device(size, feats, voxmask, links, weight, bias, cotangent):
    width = feats.shape[3]
    half = width // 2
    core = lax.axis_index("zslab") % 2

    def halves(x):
        parts = x.reshape(x.shape[:-1] + (2, half))
        first, second = parts[..., 0, :], parts[..., 1, :]
        return jnp.where(core == 0, first, second), jnp.where(core == 0, second, first)

    keep = (voxmask == 1).reshape(2, 8, 64, 1)
    rims = jnp.stack([feats[:, 0], feats[:, 7]], axis=1)
    rims = jnp.where(jnp.stack([keep[:, 0], keep[:, 7]], axis=1), rims, jnp.zeros_like(rims))
    codes = jnp.pad(links.reshape(4).astype(jnp.bfloat16), (0, width - 4))
    parcel = jnp.concatenate([rims.reshape(256, width), extra_rows([codes])])
    group = gather_group(parcel, size, 2)
    near = group_links(group[:, 256], size)
    picks = pick(near, group, size)

    mask = jnp.broadcast_to(keep.transpose(1, 0, 2, 3).astype(jnp.float32).reshape(1024, 1), (1024, 128))
    own, give = halves(jnp.where(keep, feats, jnp.zeros_like(feats)))
    theirs = swap(give, size, 1)
    turned = turn_features(own)
    their_turned = turn_features(theirs)

    picks, feats, cotangent = lax.optimization_barrier((picks, feats, cotangent))
    halos, _ = spread_picks([picks[k] for k in range(size // 4)], links, size)

    out, grad, edge, inside = forward_inside(feats, mask, weight, bias.reshape(1, width), cotangent)
    their_grad = swap(grad, size, 1)
    inner = inner_terms(turned, their_turned, grad, their_grad)

    out, grad_rims, bias_local = forward_edges(halos, mask, weight, edge, cotangent, inside, out)
    own_halos, give = halves(halos.reshape(256, width))
    their_halos = swap(give, size, 1)

    parcel = jnp.concatenate([grad_rims.reshape(256, width), extra_rows(exact_terms(bias_local[0]))])
    group = gather_group(parcel, size, 1)
    bias_group = sum_terms(group[:, 256:])
    picks = pick(near, group, size)
    extra = extra_rows(exact_terms(bias_group))
    grad_halos, extra = spread_picks(
        [jnp.concatenate([picks[k], extra]) for k in range(size // 4)], links, size
    )
    grad_bias = sum_terms(jnp.stack(extra))

    sides = [group[who, :256].reshape(2, 2, 64, width)[:, side].reshape(128, width) for side in (0, 1) for who in (0, 1)]
    rims_rows = jnp.concatenate(sides)
    parts = []
    for a in range(3):
        give, stay = outer_terms(a, turned, their_turned, own_halos, their_halos, rims_rows, inner, size)
        part = sum_and_gather(give, stay, size)
        other = swap(part, size, 1)
        part = part.reshape(9, 1, half, width)
        other = other.reshape(9, 1, half, width)
        parts.append(
            jnp.where(
                core == 0, jnp.concatenate([part, other], axis=1), jnp.concatenate([other, part], axis=1)
            ).reshape(9, width, width)
        )
    grad_weight = jnp.concatenate(parts, axis=0)

    flat_halos = grad_halos.reshape(256, width)
    grad_feats = None
    for first, last in ((2, 3), (4, 5), (0, 1), (6, 7)):
        given = flat_halos if first in (0, 6) else halos.reshape(256, width)
        grad_feats = backward(first, last, grad, grad_rims, given, mask, weight, grad_feats)
    return out, grad_feats, grad_weight, grad_bias


def solution(mesh):
    return jax.shard_map(
        functools.partial(per_device, mesh.shape["zslab"]),
        mesh=mesh,
        in_specs=(
            P(("groups", "zslab"), None, None, None),
            P(("groups", "zslab"), None),
            P(("groups", "zslab"), None),
            P(),
            P(),
            P(("groups", "zslab"), None, None, None),
        ),
        out_specs=(
            P(("groups", "zslab"), None, None, None),
            P(("groups", "zslab"), None, None, None),
            P("groups", None, None),
            P("groups"),
        ),
        check_vma=False,
    )
```

```python
import functools

import jax
import jax.numpy as jnp
from jax import lax
from jax.experimental import pallas as pl
from jax.experimental.pallas import tpu as pltpu
from jax.sharding import PartitionSpec as P

VMEM_LIMIT = 40 * 1024 * 1024
EXTRA = 16


def params():
    return pltpu.CompilerParams(vmem_limit_bytes=VMEM_LIMIT)


def cost(flops, bytes_accessed):
    return pl.CostEstimate(flops=flops, bytes_accessed=bytes_accessed, transcendentals=0)


def near(x):
    return pltpu.with_memory_space_constraint(x, pltpu.VMEM)


SCALARS = pl.BlockSpec(memory_space=pltpu.SMEM)
WHOLE = pl.BlockSpec(memory_space=pltpu.VMEM)
FAR = pl.BlockSpec(memory_space=pl.ANY)


def swap(x, size, bit):
    return lax.ppermute(x, "zslab", [(i, i ^ bit) for i in range(size)])


def rotate(x, size, steps):
    return lax.ppermute(x, "zslab", [(i, (i + 4 * steps) % size) for i in range(size)])


def orders(size):
    bits = [1 << k for k in range(1, size.bit_length() - 1)]
    return bits, [bits[1], bits[0]] + bits[2:]


def swap_stage(x, size, stage):
    both = orders(size)
    return lax.ppermute(x, "zslab", [(i, i ^ both[i % 2][stage]) for i in range(size)])


def stage_half(size, stage, other=False):
    me = lax.axis_index("zslab")
    low, high = (order[stage] for order in orders(size))
    core = me % 2 == (1 if other else 0)
    return jnp.where(core, (me // low) % 2, (me // high) % 2)


def take_rows(x, place, rows):
    return lax.dynamic_slice_in_dim(x, place * rows, rows, axis=0)


def halve(stay, got, mine):
    half = stay.shape[0] // 2
    give = take_rows(stay, 1 - mine, half) + take_rows(got, 1 - mine, half).astype(jnp.float32)
    keep = take_rows(stay, mine, half) + take_rows(got, mine, half).astype(jnp.float32)
    return give.astype(jnp.bfloat16), keep


def join(part, got, mine):
    return jnp.where(mine == 0, jnp.concatenate([part, got]), jnp.concatenate([got, part]))


def mask_rows(voxmask, z):
    lanes = slice(64 * z, 64 * z + 64)
    line = jnp.concatenate([voxmask[0:1, lanes], voxmask[1:2, lanes]], axis=1)
    return jnp.broadcast_to((line == 1).astype(jnp.float32), (128, 128)).T


def wide(mask):
    return jnp.concatenate([mask, mask], axis=1) > 0


def both(ref, z):
    return jnp.concatenate([ref[0, z], ref[1, z]], axis=0)


def inside(shape, dim, rows, cols):
    index = lax.broadcasted_iota(jnp.int32, shape, dim)
    row = (index // 8) % 8 + rows
    col = index % 8 + cols
    return (row >= 0) & (row < 8) & (col >= 0) & (col < 8)


def windows(shape, dim):
    return [inside(shape, dim, p, q) for p in (-1, 0, 1) for q in (-1, 0, 1)]


def shifts(x, dim, valid, sign=1):
    count = x.shape[dim]
    moved = []
    for place in range(9):
        at = place if sign == 1 else 8 - place
        move = 8 * (at // 3 - 1) + at % 3 - 1
        turned = pltpu.roll(x, (-move) % count, dim) if move else x
        moved.append(jnp.where(valid[at], turned, 0.0).astype(jnp.bfloat16))
    return moved


def activate(pre, cotangent, keep):
    sigma = 1.0 / (1.0 + jnp.exp(-pre))
    out = jnp.where(keep, pre * sigma, 0.0)
    grad = jnp.where(keep, cotangent * sigma * (1.0 + pre * (1.0 - sigma)), 0.0)
    return out.astype(jnp.bfloat16), grad.astype(jnp.bfloat16)


def write_exact(rows, ref):
    high = rows.astype(jnp.bfloat16)
    left = rows - high.astype(jnp.float32)
    middle = left.astype(jnp.bfloat16)
    low = (left - middle.astype(jnp.float32)).astype(jnp.bfloat16)
    zeros = jnp.zeros((EXTRA - 3, rows.shape[1]), jnp.float32)
    terms = [term.astype(jnp.float32) for term in (high, middle, low)]
    ref[256:272, :] = jnp.concatenate(terms + [zeros], axis=0).astype(jnp.bfloat16)


def read_extra(ref):
    return jnp.sum(ref[256:272, :].astype(jnp.float32), axis=0, keepdims=True)


def rims_kernel(links, low, high, voxmask, parcel):
    width = low.shape[3]
    for side, ref in ((0, low), (1, high)):
        keep = wide(mask_rows(voxmask, 7 * side))
        plane = jnp.where(keep, both(ref, 0).astype(jnp.float32), 0.0)
        parcel[128 * side : 128 * side + 128, :] = plane.astype(jnp.bfloat16)
    lane = lax.broadcasted_iota(jnp.int32, (EXTRA, width), 1)
    codes = jnp.zeros((EXTRA, width), jnp.float32)
    for place in range(4):
        codes = jnp.where(lane == place, links[place // 2, place % 2].astype(jnp.float32), codes)
    parcel[256:272, :] = codes.astype(jnp.bfloat16)


def rims(links, feats, voxmask):
    width = feats.shape[3]

    def plane(z):
        return pl.BlockSpec((2, 1, 64, width), lambda i: (0, z, 0, 0))

    return pl.pallas_call(
        rims_kernel,
        grid=(1,),
        in_specs=[SCALARS, plane(0), plane(7), WHOLE],
        out_specs=WHOLE,
        out_shape=pltpu.VMEM((256 + EXTRA, width), jnp.bfloat16),
        compiler_params=params(),
        cost_estimate=cost(0, 512 * 1024),
        name="rims",
    )(links, feats, feats, voxmask)


def prepare_kernel(core, feats, voxmask, mask, give, turned):
    half = feats.shape[3] // 2
    valid = windows((half, 128), 1)
    for z in range(8):
        rows = slice(128 * z, 128 * z + 128)
        keep = mask_rows(voxmask, z)
        mask[rows, :] = keep
        plane = jnp.where(wide(keep), both(feats, z).astype(jnp.float32), 0.0)
        first = core[0] == 0
        own = jnp.where(first, plane[:, :half], plane[:, half:])
        give[rows, :] = jnp.where(first, plane[:, half:], plane[:, :half]).astype(jnp.bfloat16)
        for place, moved in enumerate(shifts(own.T, 1, valid)):
            turned[place * half : (place + 1) * half, rows] = moved


def prepare(core, feats, voxmask):
    half = feats.shape[3] // 2
    return pl.pallas_call(
        prepare_kernel,
        in_specs=[SCALARS, WHOLE, WHOLE],
        out_specs=(WHOLE, WHOLE, WHOLE),
        out_shape=(
            pltpu.VMEM((1024, 128), jnp.float32),
            pltpu.VMEM((1024, half), jnp.bfloat16),
            pltpu.VMEM((9 * half, 1024), jnp.bfloat16),
        ),
        compiler_params=params(),
        cost_estimate=cost(0, 8 * 1024 * 1024),
        name="prepare",
    )(core, near(feats), voxmask)


def turn_kernel(rows, turned):
    half = rows.shape[1]
    valid = windows((half, 128), 1)
    for z in range(8):
        span = slice(128 * z, 128 * z + 128)
        for place, moved in enumerate(shifts(rows[span, :].astype(jnp.float32).T, 1, valid)):
            turned[place * half : (place + 1) * half, span] = moved


def turn(rows):
    half = rows.shape[1]
    return pl.pallas_call(
        turn_kernel,
        in_specs=[WHOLE],
        out_specs=WHOLE,
        out_shape=pltpu.VMEM((9 * half, 1024), jnp.bfloat16),
        compiler_params=params(),
        cost_estimate=cost(0, 6 * 1024 * 1024),
        name="turn",
    )(near(rows))


def copy_picks(outer, table, parcels, picks):
    for steps in range(outer):
        for slot in range(4):
            plane = table[steps * 4 + slot]
            start = pl.ds(pl.multiple_of((plane % 4) * 64, 64), 64)
            for dev in range(4):

                @pl.when(plane // 4 == dev)
                def _():
                    picks[steps][64 * slot : 64 * slot + 64, :] = parcels[dev][start, :]


def route_kernel(outer, where, *refs):
    parcels, (table, *picks), (codes, links, done) = refs[:4], refs[4:-3], refs[-3:]
    for dev in range(4):
        row = parcels[dev][256:272, :128].astype(jnp.float32)
        codes[8 * dev : 8 * dev + 8, :] = row[:8, :].astype(jnp.int32)
    copy = pltpu.make_async_copy(codes, links, done)
    copy.start()
    copy.wait()
    for place in range(outer * 4):
        table[place] = 0
    for plane in range(16):
        dev, side, brick = plane // 4, plane // 2 % 2, plane % 2
        dest = links[dev * 8, brick * 2 + side]

        @pl.when((dest >= 0) & ((dest // 2) % 4 == where[1]))
        def _():
            steps = lax.rem(dest // 8 - where[0] + outer, outer)
            table[steps * 4 + dest % 2 + (0 if side == 1 else 2)] = plane

    copy_picks(outer, table, parcels, picks)


def route(where, parcels, outer):
    width = parcels[0].shape[1]
    results = pl.pallas_call(
        functools.partial(route_kernel, outer),
        in_specs=[SCALARS] + [WHOLE] * 4,
        out_specs=[SCALARS] + [WHOLE] * outer,
        out_shape=[jax.ShapeDtypeStruct((outer * 4,), jnp.int32)]
        + [pltpu.VMEM((256, width), jnp.bfloat16)] * outer,
        scratch_shapes=[
            pltpu.VMEM((32, 128), jnp.int32),
            pltpu.SMEM((32, 128), jnp.int32),
            pltpu.SemaphoreType.DMA(()),
        ],
        compiler_params=params(),
        cost_estimate=cost(0, 1024 * 1024),
        name="route",
    )(where, *[near(x) for x in parcels])
    return results[0], results[1:]


def repeat_kernel(outer, table, *refs):
    parcels, picks = refs[:4], refs[4:]
    copy_picks(outer, table, parcels, picks)
    total = sum(read_extra(ref) for ref in parcels)
    for ref in picks:
        write_exact(total, ref)


def repeat_route(table, parcels, outer):
    width = parcels[0].shape[1]
    return pl.pallas_call(
        functools.partial(repeat_kernel, outer),
        in_specs=[SCALARS] + [WHOLE] * 4,
        out_specs=[WHOLE] * outer,
        out_shape=[pltpu.VMEM((256 + EXTRA, width), jnp.bfloat16)] * outer,
        compiler_params=params(),
        cost_estimate=cost(0, 1024 * 1024),
        name="repeat_route",
    )(table, *[near(x) for x in parcels])


def chosen(step, slot, arrived):
    rows = slice(64 * slot, 64 * slot + 64)
    plane = jnp.zeros((64, arrived[0].shape[1]), jnp.float32)
    for steps, ref in enumerate(arrived):
        plane = jnp.where(step[slot] == steps, ref[rows, :].astype(jnp.float32), plane)
    return plane


def forward_kernel(feats, mask, weight, bias, cotangent, out, grad, edge, bias_sum, cols, pre):
    width = feats.shape[3]
    valid = windows((128, width), 0)
    for z in range(8):
        rows = slice(128 * z, 128 * z + 128)
        plane = jnp.where(wide(mask[rows, :]), both(feats, z).astype(jnp.float32), 0.0)
        for place, moved in enumerate(shifts(plane, 0, valid)):
            cols[rows, place * width : (place + 1) * width] = moved
    taps = [weight[9 * a : 9 * a + 9].reshape(9 * width, width) for a in range(3)]
    pre[...] = jnp.dot(cols[...], taps[1], preferred_element_type=jnp.float32) + bias[...]
    pre[128:, :] += jnp.dot(cols[:896, :], taps[0], preferred_element_type=jnp.float32)
    pre[:896, :] += jnp.dot(cols[128:, :], taps[2], preferred_element_type=jnp.float32)
    edge[0] = pre[:128, :]
    edge[1] = pre[896:, :]
    total = jnp.zeros((1, width), jnp.float32)
    for z in range(1, 7):
        rows = slice(128 * z, 128 * z + 128)
        act, slope = activate(pre[rows, :], both(cotangent, z).astype(jnp.float32), wide(mask[rows, :]))
        for b in range(2):
            out[b, z] = act[64 * b : 64 * b + 64]
        grad[128 * (z - 1) : 128 * z, :] = slope
        total += jnp.sum(slope.astype(jnp.float32), axis=0, keepdims=True)
    bias_sum[...] = total


def forward_inside(feats, mask, weight, bias, cotangent):
    width = feats.shape[3]
    return pl.pallas_call(
        forward_kernel,
        in_specs=[WHOLE] * 5,
        out_specs=(WHOLE,) * 4,
        out_shape=(
            pltpu.VMEM(feats.shape, jnp.bfloat16),
            pltpu.VMEM((768, width), jnp.bfloat16),
            pltpu.VMEM((2, 128, width), jnp.float32),
            pltpu.VMEM((1, width), jnp.float32),
        ),
        scratch_shapes=[
            pltpu.VMEM((1024, 9 * width), jnp.bfloat16),
            pltpu.VMEM((1024, width), jnp.float32),
        ],
        compiler_params=params(),
        cost_estimate=cost(2 * 1024 * 27 * width * width, 6 * 1024 * 1024),
        name="forward_inside",
    )(near(feats), near(mask), near(weight), bias, near(cotangent))


def inner_terms_kernel(mine, theirs, grad, their_grad, terms):
    rows = mine.shape[0]
    for a in range(3):
        lanes = slice(128 * a, 128 * a + 768)
        terms[a * rows : (a + 1) * rows, :] = jnp.dot(
            mine[:, lanes], grad[...], preferred_element_type=jnp.float32
        ) + jnp.dot(theirs[:, lanes], their_grad[...], preferred_element_type=jnp.float32)


def inner_terms(mine, theirs, grad, their_grad):
    rows, width = mine.shape[0], grad.shape[1]
    return pl.pallas_call(
        inner_terms_kernel,
        in_specs=[WHOLE] * 4,
        out_specs=WHOLE,
        out_shape=pltpu.VMEM((3 * rows, width), jnp.float32),
        compiler_params=params(),
        cost_estimate=cost(2 * 1536 * 3 * rows * width, 8 * 1024 * 1024),
        name="inner_terms",
    )(near(mine), near(theirs), near(grad), near(their_grad))


def edge_kernel(core, step, mask, weight, edge, cotangent, inner, out_in, *refs):
    arrived, (out, parcel, own, give) = refs[:-4], refs[-4:]
    width = edge.shape[2]
    half = width // 2
    valid = windows((128, width), 0)
    total = inner[...]
    for side in range(2):
        rows = slice(128 * side, 128 * side + 128)
        halo = jnp.concatenate([chosen(step, 2 * side + b, arrived) for b in range(2)], axis=0)
        first = core[0] == 0
        own[rows, :] = jnp.where(first, halo[:, :half], halo[:, half:]).astype(jnp.bfloat16)
        give[rows, :] = jnp.where(first, halo[:, half:], halo[:, :half]).astype(jnp.bfloat16)
        cols = jnp.concatenate(shifts(halo, 0, valid), axis=1)
        taps = weight[18 * side : 18 * side + 9].reshape(9 * width, width)
        pre = edge[side] + jnp.dot(cols, taps, preferred_element_type=jnp.float32)
        z = 7 * side
        keep = wide(mask[128 * z : 128 * z + 128, :])
        act, slope = activate(pre, both(cotangent, z).astype(jnp.float32), keep)
        for b in range(2):
            out[b, z] = act[64 * b : 64 * b + 64]
        parcel[rows, :] = slope
        total += jnp.sum(slope.astype(jnp.float32), axis=0, keepdims=True)
    write_exact(total, parcel)


def forward_edges(core, step, mask, weight, edge, cotangent, inner, out, arrived):
    width = edge.shape[2]
    return pl.pallas_call(
        edge_kernel,
        in_specs=[SCALARS, SCALARS] + [WHOLE] * (6 + len(arrived)),
        out_specs=(WHOLE,) * 4,
        out_shape=(
            pltpu.VMEM(out.shape, out.dtype),
            pltpu.VMEM((256 + EXTRA, width), jnp.bfloat16),
            pltpu.VMEM((256, width // 2), jnp.bfloat16),
            pltpu.VMEM((256, width // 2), jnp.bfloat16),
        ),
        input_output_aliases={7: 0},
        compiler_params=params(),
        cost_estimate=cost(2 * 256 * 9 * width * width, 3 * 1024 * 1024),
        name="forward_edges",
    )(
        core,
        step,
        near(mask),
        near(weight),
        near(edge),
        near(cotangent),
        near(inner),
        near(out),
        *[near(x) for x in arrived],
    )


def outer_terms_kernel(upper, mine, theirs, halos, their_halos, parcel, their_parcel, inner, give, stay, ends, cols, total):
    rows = mine.shape[0]
    half = rows // 9
    valid = windows((half, 128), 1)
    for who, ref in enumerate((halos, their_halos)):
        for side in range(2):
            plane = ref[128 * side : 128 * side + 128, :].astype(jnp.float32).T
            lanes = slice(256 * side + 128 * who, 256 * side + 128 * who + 128)
            for place, moved in enumerate(shifts(plane, 1, valid)):
                ends[place * half : (place + 1) * half, lanes] = moved
    facing = jnp.concatenate([parcel[:128], their_parcel[:128], parcel[128:256], their_parcel[128:256]], axis=0)
    for a in range(3):
        if a == 0:
            cols[:, :256] = ends[:, :256]
        else:
            cols[:, :128] = mine[:, 128 * (a - 1) : 128 * a]
            cols[:, 128:256] = theirs[:, 128 * (a - 1) : 128 * a]
        if a == 2:
            cols[:, 256:] = ends[:, 256:]
        else:
            cols[:, 256:384] = mine[:, 128 * (6 + a) : 128 * (7 + a)]
            cols[:, 384:] = theirs[:, 128 * (6 + a) : 128 * (7 + a)]
        span = slice(a * rows, (a + 1) * rows)
        total[span, :] = inner[span, :] + jnp.dot(cols[...], facing, preferred_element_type=jnp.float32)
    count = give.shape[0]
    give[...] = total[pl.ds(pl.multiple_of((1 - upper[0]) * count, 16), count), :].astype(jnp.bfloat16)
    stay[...] = total[pl.ds(pl.multiple_of(upper[0] * count, 16), count), :]


def outer_terms(upper, mine, theirs, halos, their_halos, parcel, their_parcel, inner):
    rows, width = inner.shape
    return pl.pallas_call(
        outer_terms_kernel,
        in_specs=[SCALARS] + [WHOLE] * 7,
        out_specs=(WHOLE, WHOLE),
        out_shape=(pltpu.VMEM((rows // 2, width), jnp.bfloat16), pltpu.VMEM((rows // 2, width), jnp.float32)),
        scratch_shapes=[
            pltpu.VMEM((rows // 3, 512), jnp.bfloat16),
            pltpu.VMEM((rows // 3, 512), jnp.bfloat16),
            pltpu.VMEM((rows, width), jnp.float32),
        ],
        compiler_params=params(),
        cost_estimate=cost(2 * 512 * rows * width, 8 * 1024 * 1024),
        name="outer_terms",
    )(upper, *[near(x) for x in (mine, theirs, halos, their_halos, parcel, their_parcel, inner)])


def backward_rows(planes, mask, weight, cols, place):
    width = weight.shape[1]
    valid = windows((128, width), 0)
    for index, plane in enumerate(planes):
        rows = slice(128 * (place + index), 128 * (place + index) + 128)
        for at, moved in enumerate(shifts(plane.astype(jnp.float32), 0, valid, -1)):
            cols[rows, at * width : (at + 1) * width] = moved
    count = 128 * (len(planes) - 2)
    total = jnp.zeros((count, width), jnp.float32)
    for a in range(3):
        for at in range(9):
            start = 128 * (place + 2 - a)
            total += lax.dot_general(
                cols[start : start + count, at * width : (at + 1) * width],
                weight[9 * a + at],
                (((1,), (1,)), ((), ())),
                preferred_element_type=jnp.float32,
            )
    return jnp.where(wide(mask), total, 0.0).astype(jnp.bfloat16)


def backward_inner_kernel(grad, parcel, mask, weight, grad_feats, cols):
    done = backward_rows(
        [grad[128 * (z - 1) : 128 * z, :] for z in range(1, 7)], mask[256:768, :], weight, cols, 0
    )
    for z in range(2, 6):
        for b in range(2):
            start = 128 * (z - 2) + 64 * b
            grad_feats[b, z] = done[start : start + 64]


def backward_inner(grad, parcel, mask, weight):
    width = grad.shape[1]
    return pl.pallas_call(
        backward_inner_kernel,
        in_specs=[WHOLE] * 4,
        out_specs=WHOLE,
        out_shape=pltpu.VMEM((2, 8, 64, width), jnp.bfloat16),
        scratch_shapes=[pltpu.VMEM((768, 9 * width), jnp.bfloat16)],
        compiler_params=params(),
        cost_estimate=cost(2 * 512 * 27 * width * width, 5 * 1024 * 1024),
        name="backward_inner",
    )(near(grad), near(parcel), near(mask), near(weight))


def backward_outer_kernel(step, grad, parcel, mask, weight, done, *refs):
    arrived, (grad_feats, bias_sum, cols) = refs[:-3], refs[-3:]
    for side in range(2):
        halo = jnp.concatenate([chosen(step, 2 * side + b, arrived) for b in range(2)], axis=0)
        rim = parcel[128 * side : 128 * side + 128, :]
        if side == 0:
            planes = [halo, rim, grad[:128, :], grad[128:256, :]]
        else:
            planes = [grad[512:640, :], grad[640:768, :], rim, halo]
        first = 6 * side
        rows = backward_rows(planes, mask[128 * first : 128 * first + 256, :], weight, cols, 4 * side)
        for z in range(2):
            for b in range(2):
                start = 128 * z + 64 * b
                grad_feats[b, first + z] = rows[start : start + 64]
    bias_sum[...] = sum(read_extra(ref) for ref in arrived)


def backward_outer(step, grad, parcel, mask, weight, done, arrived):
    width = grad.shape[1]
    return pl.pallas_call(
        backward_outer_kernel,
        in_specs=[SCALARS] + [WHOLE] * (5 + len(arrived)),
        out_specs=(WHOLE, WHOLE),
        out_shape=(pltpu.VMEM((2, 8, 64, width), jnp.bfloat16), pltpu.VMEM((1, width), jnp.float32)),
        scratch_shapes=[pltpu.VMEM((1024, 9 * width), jnp.bfloat16)],
        input_output_aliases={5: 0},
        compiler_params=params(),
        cost_estimate=cost(2 * 512 * 27 * width * width, 5 * 1024 * 1024),
        name="backward_outer",
    )(step, near(grad), near(parcel), near(mask), near(weight), near(done), *[near(x) for x in arrived])


def assemble_kernel(place, *refs):
    parts, out, done = refs[:4], refs[4], refs[5]
    half = out.shape[1] // 2
    taps = out.shape[0] // 2
    rest = parts[0].shape[0] - taps * half
    for index, ref in enumerate(parts):
        core, second = place[2 * index], place[2 * index + 1]
        for who in range(2):
            for upper in range(2):

                @pl.when((core == who) & (second == upper))
                def _():
                    full, cut = (taps + 1, 0) if upper else (0, taps * half)
                    body = rest if upper else 0
                    copies = [
                        pltpu.make_async_copy(
                            ref.at[pl.ds(body + half * tap, half)],
                            out.at[full + tap, pl.ds(half * who, half)],
                            done.at[index, tap],
                        )
                        for tap in range(taps)
                    ]
                    copies.append(
                        pltpu.make_async_copy(
                            ref.at[pl.ds(cut, rest)],
                            out.at[taps, pl.ds(half * who + rest * upper, rest)],
                            done.at[index, taps],
                        )
                    )
                    for copy in copies:
                        copy.start()

    for index, ref in enumerate(parts):
        for tap in range(taps):
            pltpu.make_async_copy(
                ref.at[pl.ds(half * tap, half)], out.at[tap, pl.ds(0, half)], done.at[index, tap]
            ).wait()
        pltpu.make_async_copy(ref.at[pl.ds(0, rest)], out.at[taps, pl.ds(0, rest)], done.at[index, taps]).wait()


def assemble(place, parts):
    rows, width = parts[0].shape
    taps = rows * 4 // width
    return pl.pallas_call(
        assemble_kernel,
        in_specs=[SCALARS] + [WHOLE] * 4,
        out_specs=FAR,
        out_shape=jax.ShapeDtypeStruct((taps, width, width), jnp.bfloat16),
        scratch_shapes=[pltpu.SemaphoreType.DMA((4, taps // 2 + 1))],
        compiler_params=params(),
        cost_estimate=cost(0, 8 * rows * width * 2),
        name="assemble",
    )(place, *[near(x) for x in parts])


def gather_group(parcel, size):
    inner = swap(parcel, size, 2)
    return [parcel, inner, swap(parcel, size, 1), swap(inner, size, 1)]


def per_device(size, feats, voxmask, links, weight, bias, cotangent):
    width = feats.shape[3]
    outer = size // 4
    me = lax.axis_index("zslab")
    core = (me % 2).astype(jnp.int32).reshape(1)
    where = jnp.stack([me // 4, me % 4]).astype(jnp.int32)
    want = links.T.reshape(4)
    step = jnp.where(want >= 0, (me // 4 - want // 8) % outer, -1)

    parcels = gather_group(rims(links, feats, voxmask), size)
    table, picks = route(where, parcels, outer)
    mask, give, turned = prepare(core, feats, voxmask)

    *picks, give, feats, cotangent = lax.optimization_barrier((*picks, give, feats, cotangent))
    arrived = [rotate(pick, size, steps) if steps else pick for steps, pick in enumerate(picks)]
    their_turned = turn(swap(give, size, 1))
    out, grad, edge, bias_local = forward_inside(feats, mask, weight, bias.reshape(1, width), cotangent)
    inner = inner_terms(turned, their_turned, grad, swap(grad, size, 1))

    *arrived, inner = lax.optimization_barrier((*arrived, inner))
    out, parcel, halos, give = forward_edges(core, step, mask, weight, edge, cotangent, bias_local, out, arrived)
    their_halos = swap(give, size, 1)
    parcels = gather_group(parcel, size)

    stages = len(orders(size)[0])
    halves = [stage_half(size, stage) for stage in range(stages)]
    give, stay = outer_terms(
        halves[0].astype(jnp.int32).reshape(1), turned, their_turned, halos, their_halos, parcel, parcels[2], inner
    )
    picks = repeat_route(table, parcels, outer)
    arrived = [rotate(pick, size, steps) if steps else pick for steps, pick in enumerate(picks)]
    got = swap_stage(give, size, 0)
    grad_feats = backward_inner(grad, parcel, mask, weight)
    stay, grad_feats = lax.optimization_barrier((stay, grad_feats))
    for stage in range(1, stages):
        give, stay = halve(stay, got, halves[stage])
        got = swap_stage(give, size, stage)
    part = (stay + got.astype(jnp.float32)).astype(jnp.bfloat16)
    for stage in reversed(range(1, stages)):
        part = join(part, swap_stage(part, size, stage), halves[stage])
    grad_feats, grad_bias = backward_outer(step, grad, parcel, mask, weight, grad_feats, arrived)
    last = swap_stage(part, size, 0)
    other = swap(part, size, 1)
    last, grad_feats, grad_bias = lax.optimization_barrier((last, grad_feats, grad_bias))
    other_last = swap(last, size, 1)
    theirs = stage_half(size, 0, other=True)
    place = jnp.stack([core[0], halves[0], core[0], 1 - halves[0], 1 - core[0], theirs, 1 - core[0], 1 - theirs])
    grad_weight = assemble(place.astype(jnp.int32), [part, last, other, other_last])
    return out, grad_feats, grad_weight, grad_bias.reshape(width)


def solution(mesh):
    return jax.shard_map(
        functools.partial(per_device, mesh.shape["zslab"]),
        mesh=mesh,
        in_specs=(
            P(("groups", "zslab"), None, None, None),
            P(("groups", "zslab"), None),
            P(("groups", "zslab"), None),
            P(),
            P(),
            P(("groups", "zslab"), None, None, None),
        ),
        out_specs=(
            P(("groups", "zslab"), None, None, None),
            P(("groups", "zslab"), None, None, None),
            P("groups", None, None),
            P("groups"),
        ),
        check_vma=False,
    )
```

```python
import functools

import jax
import jax.numpy as jnp
from jax import lax
from jax.experimental import pallas as pl
from jax.experimental.pallas import tpu as pltpu
from jax.sharding import PartitionSpec as P

VMEM_LIMIT = 16 * 1024 * 1024
EXTRA = 16


def params():
    return pltpu.CompilerParams(vmem_limit_bytes=VMEM_LIMIT)


def cost(flops, bytes_accessed):
    return pl.CostEstimate(flops=flops, bytes_accessed=bytes_accessed, transcendentals=0)


def near(x):
    return pltpu.with_memory_space_constraint(x, pltpu.VMEM)


def far(x):
    return pltpu.with_memory_space_constraint(x, pltpu.HBM)


SCALARS = pl.BlockSpec(memory_space=pltpu.SMEM)
WHOLE = pl.BlockSpec(memory_space=pltpu.VMEM)
FAR = pl.BlockSpec(memory_space=pl.ANY)


def swap(x, size, bit):
    return lax.ppermute(x, "zslab", [(i, i ^ bit) for i in range(size)])


def rotate(x, size, steps):
    return lax.ppermute(x, "zslab", [(i, (i + 4 * steps) % size) for i in range(size)])


def orders(size):
    bits = [1 << k for k in range(1, size.bit_length() - 1)]
    return bits, [bits[1], bits[0]] + bits[2:]


def swap_stage(x, size, stage):
    both = orders(size)
    return lax.ppermute(x, "zslab", [(i, i ^ both[i % 2][stage]) for i in range(size)])


def stage_half(size, stage, other=False):
    me = lax.axis_index("zslab")
    low, high = (order[stage] for order in orders(size))
    core = me % 2 == (1 if other else 0)
    return jnp.where(core, (me // low) % 2, (me // high) % 2)


def take_rows(x, place, rows):
    return lax.dynamic_slice_in_dim(x, place * rows, rows, axis=0)


def halve(stay, got, mine):
    half = stay.shape[0] // 2
    give = take_rows(stay, 1 - mine, half) + take_rows(got, 1 - mine, half).astype(jnp.float32)
    keep = take_rows(stay, mine, half) + take_rows(got, mine, half).astype(jnp.float32)
    return give.astype(jnp.bfloat16), keep


def join(part, got, mine):
    return jnp.where(mine == 0, jnp.concatenate([part, got]), jnp.concatenate([got, part]))


def mask_rows(voxmask, z):
    lanes = slice(64 * z, 64 * z + 64)
    line = jnp.concatenate([voxmask[0:1, lanes], voxmask[1:2, lanes]], axis=1)
    return jnp.broadcast_to((line == 1).astype(jnp.float32), (128, 128)).T


def wide(mask):
    return jnp.concatenate([mask, mask], axis=1) > 0


def both(ref, z):
    return jnp.concatenate([ref[0, z], ref[1, z]], axis=0)


def inside(shape, dim, rows, cols):
    index = lax.broadcasted_iota(jnp.int32, shape, dim)
    row = (index // 8) % 8 + rows
    col = index % 8 + cols
    return (row >= 0) & (row < 8) & (col >= 0) & (col < 8)


def windows(shape, dim):
    return [inside(shape, dim, p, q) for p in (-1, 0, 1) for q in (-1, 0, 1)]


def shifts(x, dim, valid, sign=1):
    count = x.shape[dim]
    moved = []
    for place in range(9):
        at = place if sign == 1 else 8 - place
        move = 8 * (at // 3 - 1) + at % 3 - 1
        turned = pltpu.roll(x, (-move) % count, dim) if move else x
        moved.append(jnp.where(valid[at], turned, 0.0).astype(jnp.bfloat16))
    return moved


def activate(pre, cotangent, keep):
    sigma = 1.0 / (1.0 + jnp.exp(-pre))
    out = jnp.where(keep, pre * sigma, 0.0)
    grad = jnp.where(keep, cotangent * sigma * (1.0 + pre * (1.0 - sigma)), 0.0)
    return out.astype(jnp.bfloat16), grad.astype(jnp.bfloat16)


def write_exact(rows, ref):
    high = rows.astype(jnp.bfloat16)
    left = rows - high.astype(jnp.float32)
    middle = left.astype(jnp.bfloat16)
    low = (left - middle.astype(jnp.float32)).astype(jnp.bfloat16)
    zeros = jnp.zeros((EXTRA - 3, rows.shape[1]), jnp.float32)
    terms = [term.astype(jnp.float32) for term in (high, middle, low)]
    ref[256:272, :] = jnp.concatenate(terms + [zeros], axis=0).astype(jnp.bfloat16)


def read_extra(ref):
    return jnp.sum(ref[256:272, :].astype(jnp.float32), axis=0, keepdims=True)


def rims_kernel(links, feats, voxmask, parcel, planes, masks, codes, done):
    width = feats.shape[3]
    copies = [
        pltpu.make_async_copy(feats.at[:, pl.ds(0, 1)], planes.at[0], done.at[0]),
        pltpu.make_async_copy(feats.at[:, pl.ds(7, 1)], planes.at[1], done.at[1]),
        pltpu.make_async_copy(voxmask, masks, done.at[2]),
        pltpu.make_async_copy(links, codes, done.at[3]),
    ]
    for copy in copies:
        copy.start()
    for copy in copies:
        copy.wait()
    for side in range(2):
        keep = wide(mask_rows(masks, 7 * side))
        plane = jnp.concatenate([planes[side, 0, 0], planes[side, 1, 0]], axis=0).astype(jnp.float32)
        parcel[128 * side : 128 * side + 128, :] = jnp.where(keep, plane, 0.0).astype(jnp.bfloat16)
    lane = lax.broadcasted_iota(jnp.int32, (EXTRA, width), 1)
    row = jnp.zeros((EXTRA, width), jnp.float32)
    for place in range(4):
        row = jnp.where(lane == place, codes[place // 2, place % 2].astype(jnp.float32), row)
    parcel[256:272, :] = row.astype(jnp.bfloat16)


def rims(links, feats, voxmask):
    width = feats.shape[3]
    return pl.pallas_call(
        rims_kernel,
        in_specs=[FAR] * 3,
        out_specs=WHOLE,
        out_shape=pltpu.VMEM((256 + EXTRA, width), jnp.bfloat16),
        scratch_shapes=[
            pltpu.VMEM((2, 2, 1, 64, width), jnp.bfloat16),
            pltpu.VMEM(voxmask.shape, jnp.int32),
            pltpu.SMEM(links.shape, jnp.int32),
            pltpu.SemaphoreType.DMA((4,)),
        ],
        compiler_params=params(),
        cost_estimate=cost(1024, 1024),
        name="rims",
    )(far(links), far(feats), far(voxmask))


def prepare_kernel(feats, voxmask, mask, rows, give, turned, planes, masks, done):
    half = feats.shape[3] // 2
    copies = [
        pltpu.make_async_copy(feats, planes, done.at[0]),
        pltpu.make_async_copy(voxmask, masks, done.at[1]),
    ]
    for copy in copies:
        copy.start()
    valid = windows((half, 128), 1)
    for copy in copies:
        copy.wait()
    first = lax.axis_index("zslab") % 2 == 0
    for z in range(8):
        span = slice(128 * z, 128 * z + 128)
        keep = mask_rows(masks, z)
        mask[span, :] = keep
        plane = jnp.where(wide(keep), both(planes, z).astype(jnp.float32), 0.0)
        rows[span, :] = plane.astype(jnp.bfloat16)
        own = jnp.where(first, plane[:, :half], plane[:, half:])
        give[span, :] = jnp.where(first, plane[:, half:], plane[:, :half]).astype(jnp.bfloat16)
        for place, moved in enumerate(shifts(own.T, 1, valid)):
            turned[place * half : (place + 1) * half, span] = moved


def prepare(feats, voxmask):
    width = feats.shape[3]
    half = width // 2
    return pl.pallas_call(
        prepare_kernel,
        in_specs=[FAR, FAR],
        out_specs=(WHOLE,) * 4,
        out_shape=(
            pltpu.VMEM((1024, 128), jnp.float32),
            pltpu.VMEM((1024, width), jnp.bfloat16),
            pltpu.VMEM((1024, half), jnp.bfloat16),
            pltpu.VMEM((9 * half, 1024), jnp.bfloat16),
        ),
        scratch_shapes=[
            pltpu.VMEM(feats.shape, jnp.bfloat16),
            pltpu.VMEM(voxmask.shape, jnp.int32),
            pltpu.SemaphoreType.DMA((2,)),
        ],
        compiler_params=params(),
        cost_estimate=cost(1024, 1024),
        name="prepare",
    )(far(feats), far(voxmask))


def turn_kernel(rows, turned):
    half = rows.shape[1]
    valid = windows((half, 128), 1)
    for z in range(8):
        span = slice(128 * z, 128 * z + 128)
        for place, moved in enumerate(shifts(rows[span, :].astype(jnp.float32).T, 1, valid)):
            turned[place * half : (place + 1) * half, span] = moved


def turn(rows):
    half = rows.shape[1]
    return pl.pallas_call(
        turn_kernel,
        in_specs=[WHOLE],
        out_specs=WHOLE,
        out_shape=pltpu.VMEM((9 * half, 1024), jnp.bfloat16),
        compiler_params=params(),
        cost_estimate=cost(1024, 1024),
        name="turn",
    )(near(rows))


def copy_picks(outer, table, parcels, picks):
    for steps in range(outer):
        for slot in range(4):
            plane = table[steps * 4 + slot]
            start = pl.ds(pl.multiple_of((plane % 4) * 64, 64), 64)
            for dev in range(4):

                @pl.when(plane // 4 == dev)
                def _():
                    picks[steps][64 * slot : 64 * slot + 64, :] = parcels[dev][start, :]


def route_kernel(outer, *refs):
    me = lax.axis_index("zslab")
    parcels, (table, *picks), (codes, links, done) = refs[:4], refs[4:-3], refs[-3:]
    for dev in range(4):
        row = parcels[dev][256:272, :128].astype(jnp.float32)
        codes[8 * dev : 8 * dev + 8, :] = row[:8, :].astype(jnp.int32)
    copy = pltpu.make_async_copy(codes, links, done)
    copy.start()
    copy.wait()
    for place in range(outer * 4):
        table[place] = 0
    for plane in range(16):
        dev, side, brick = plane // 4, plane // 2 % 2, plane % 2
        dest = links[dev * 8, brick * 2 + side]

        @pl.when((dest >= 0) & ((dest // 2) % 4 == me % 4))
        def _():
            steps = lax.rem(dest // 8 - me // 4 + outer, outer)
            table[steps * 4 + dest % 2 + (0 if side == 1 else 2)] = plane

    for brick in range(2):
        for side in range(2):
            dest = links[0, brick * 2 + side]
            steps = lax.rem(me // 4 - dest // 8 + outer, outer)
            table[outer * 4 + 2 * side + brick] = jnp.where(dest >= 0, steps, -1)

    copy_picks(outer, table, parcels, picks)


def route(parcels, outer):
    width = parcels[0].shape[1]
    results = pl.pallas_call(
        functools.partial(route_kernel, outer),
        in_specs=[WHOLE] * 4,
        out_specs=[SCALARS] + [WHOLE] * outer,
        out_shape=[jax.ShapeDtypeStruct((outer * 4 + 4,), jnp.int32)]
        + [pltpu.VMEM((256, width), jnp.bfloat16)] * outer,
        scratch_shapes=[
            pltpu.VMEM((32, 128), jnp.int32),
            pltpu.SMEM((32, 128), jnp.int32),
            pltpu.SemaphoreType.DMA(()),
        ],
        compiler_params=params(),
        cost_estimate=cost(1024, 1024),
        name="route",
    )(*[near(x) for x in parcels])
    return results[0], results[1:]


def repeat_kernel(outer, table, *refs):
    parcels, picks = refs[:4], refs[4:]
    copy_picks(outer, table, parcels, picks)
    total = sum(read_extra(ref) for ref in parcels)
    for ref in picks:
        write_exact(total, ref)


def repeat_route(table, parcels, outer):
    width = parcels[0].shape[1]
    return pl.pallas_call(
        functools.partial(repeat_kernel, outer),
        in_specs=[SCALARS] + [WHOLE] * 4,
        out_specs=[WHOLE] * outer,
        out_shape=[pltpu.VMEM((256 + EXTRA, width), jnp.bfloat16)] * outer,
        compiler_params=params(),
        cost_estimate=cost(1024, 1024),
        name="repeat_route",
    )(table, *[near(x) for x in parcels])


def chosen(table, slot, arrived):
    rows = slice(64 * slot, 64 * slot + 64)
    plane = jnp.zeros((64, arrived[0].shape[1]), jnp.float32)
    for steps, ref in enumerate(arrived):
        plane = jnp.where(table[4 * len(arrived) + slot] == steps, ref[rows, :].astype(jnp.float32), plane)
    return plane


def forward_kernel(rows, mask, weight, bias, cotangent, out, grad, edge, bias_sum, near_weight, ends, cols, pre, slopes, shift, done):
    width = rows.shape[1]
    copies = [pltpu.make_async_copy(bias, shift, done.at[4])]
    for a in (1, 0, 2):
        taps = pl.ds(9 * a, 9)
        copies.append(pltpu.make_async_copy(weight.at[taps], near_weight.at[taps], done.at[a]))
    copies.append(pltpu.make_async_copy(cotangent, slopes, done.at[3]))
    for copy in copies:
        copy.start()
    valid = windows((128, width), 0)
    for z in range(8):
        span = slice(128 * z, 128 * z + 128)
        for place, moved in enumerate(shifts(rows[span, :].astype(jnp.float32), 0, valid)):
            cols[span, place * width : (place + 1) * width] = moved

    def taps(a):
        return near_weight[9 * a : 9 * a + 9].reshape(9 * width, width)

    copies[0].wait()
    copies[1].wait()
    pre[...] = jnp.dot(cols[...], taps(1), preferred_element_type=jnp.float32) + shift[...]
    copies[2].wait()
    pre[128:, :] += jnp.dot(cols[:896, :], taps(0), preferred_element_type=jnp.float32)
    copies[3].wait()
    pre[:896, :] += jnp.dot(cols[128:, :], taps(2), preferred_element_type=jnp.float32)
    copies[4].wait()
    for side in range(2):
        edge[side] = pre[896 * side : 896 * side + 128, :]
        ends[side] = both(slopes, 7 * side)
    total = jnp.zeros((1, width), jnp.float32)
    for z in range(1, 7):
        span = slice(128 * z, 128 * z + 128)
        act, slope = activate(pre[span, :], both(slopes, z).astype(jnp.float32), wide(mask[span, :]))
        for b in range(2):
            out[b, z] = act[64 * b : 64 * b + 64]
        grad[128 * (z - 1) : 128 * z, :] = slope
        total += jnp.sum(slope.astype(jnp.float32), axis=0, keepdims=True)
    bias_sum[...] = total


def forward_inside(rows, mask, weight, bias, cotangent):
    width = rows.shape[1]
    return pl.pallas_call(
        forward_kernel,
        in_specs=[WHOLE, WHOLE, FAR, FAR, FAR],
        out_specs=(WHOLE,) * 6,
        out_shape=(
            jax.ShapeDtypeStruct(cotangent.shape, jnp.bfloat16),
            pltpu.VMEM((768, width), jnp.bfloat16),
            pltpu.VMEM((2, 128, width), jnp.float32),
            pltpu.VMEM((1, width), jnp.float32),
            pltpu.VMEM(weight.shape, jnp.bfloat16),
            pltpu.VMEM((2, 128, width), jnp.bfloat16),
        ),
        scratch_shapes=[
            pltpu.VMEM((1024, 9 * width), jnp.bfloat16),
            pltpu.VMEM((1024, width), jnp.float32),
            pltpu.VMEM(cotangent.shape, jnp.bfloat16),
            pltpu.VMEM((1, width), jnp.float32),
            pltpu.SemaphoreType.DMA((5,)),
        ],
        compiler_params=params(),
        cost_estimate=cost(1024, 1024),
        name="forward_inside",
    )(near(rows), near(mask), far(weight), far(bias), far(cotangent))


def inner_terms_kernel(mine, theirs, grad, their_grad, terms):
    rows = mine.shape[0]
    for a in range(3):
        lanes = slice(128 * a, 128 * a + 768)
        terms[a * rows : (a + 1) * rows, :] = jnp.dot(
            mine[:, lanes], grad[...], preferred_element_type=jnp.float32
        ) + jnp.dot(theirs[:, lanes], their_grad[...], preferred_element_type=jnp.float32)


def inner_terms(mine, theirs, grad, their_grad):
    rows, width = mine.shape[0], grad.shape[1]
    return pl.pallas_call(
        inner_terms_kernel,
        in_specs=[WHOLE] * 4,
        out_specs=WHOLE,
        out_shape=pltpu.VMEM((3 * rows, width), jnp.float32),
        compiler_params=params(),
        cost_estimate=cost(1024, 1024),
        name="inner_terms",
    )(near(mine), near(theirs), near(grad), near(their_grad))


def edge_kernel(table, mask, weight, edge, ends, inner, out_in, *refs):
    arrived, (out, parcel, own, give, planes, done) = refs[:-6], refs[-6:]
    width = edge.shape[2]
    half = width // 2
    valid = windows((128, width), 0)
    total = inner[...]
    for side in range(2):
        rows = slice(128 * side, 128 * side + 128)
        halo = jnp.concatenate([chosen(table, 2 * side + b, arrived) for b in range(2)], axis=0)
        first = lax.axis_index("zslab") % 2 == 0
        own[rows, :] = jnp.where(first, halo[:, :half], halo[:, half:]).astype(jnp.bfloat16)
        give[rows, :] = jnp.where(first, halo[:, half:], halo[:, :half]).astype(jnp.bfloat16)
        cols = jnp.concatenate(shifts(halo, 0, valid), axis=1)
        taps = weight[18 * side : 18 * side + 9].reshape(9 * width, width)
        pre = edge[side] + jnp.dot(cols, taps, preferred_element_type=jnp.float32)
        z = 7 * side
        keep = wide(mask[128 * z : 128 * z + 128, :])
        act, slope = activate(pre, ends[side].astype(jnp.float32), keep)
        for b in range(2):
            planes[side, b, 0] = act[64 * b : 64 * b + 64]
        pltpu.make_async_copy(planes.at[side], out.at[:, pl.ds(z, 1)], done.at[side]).start()
        parcel[rows, :] = slope
        total += jnp.sum(slope.astype(jnp.float32), axis=0, keepdims=True)
    write_exact(total, parcel)
    for side in range(2):
        pltpu.make_async_copy(planes.at[side], out.at[:, pl.ds(7 * side, 1)], done.at[side]).wait()


def forward_edges(table, mask, weight, edge, ends, inner, out, arrived):
    width = edge.shape[2]
    return pl.pallas_call(
        edge_kernel,
        in_specs=[SCALARS] + [WHOLE] * 5 + [FAR] + [WHOLE] * len(arrived),
        out_specs=(FAR, WHOLE, WHOLE, WHOLE),
        out_shape=(
            jax.ShapeDtypeStruct(out.shape, out.dtype),
            pltpu.VMEM((256 + EXTRA, width), jnp.bfloat16),
            pltpu.VMEM((256, width // 2), jnp.bfloat16),
            pltpu.VMEM((256, width // 2), jnp.bfloat16),
        ),
        scratch_shapes=[pltpu.VMEM((2, 2, 1, 64, width), jnp.bfloat16), pltpu.SemaphoreType.DMA((2,))],
        input_output_aliases={6: 0},
        compiler_params=params(),
        cost_estimate=cost(1024, 1024),
        name="forward_edges",
    )(
        table,
        near(mask),
        near(weight),
        near(edge),
        near(ends),
        near(inner),
        out,
        *[near(x) for x in arrived],
    )


def outer_terms_kernel(taps, size, mine, theirs, halos, their_halos, parcel, their_parcel, inner, give, stay, cols, total):
    half = mine.shape[0] // 9
    piece = half // 2
    valid = windows((half, 128), 1)
    facing = jnp.concatenate([parcel[:128], their_parcel[:128], parcel[128:256], their_parcel[128:256]], axis=0)
    for a in range(3):
        first, last = max(taps[0], 9 * a), min(taps[1], 9 * a + 9)
        if first >= last:
            continue
        low, high = (first - 9 * a) * half, (last - 9 * a) * half
        for place, (ref, ends) in enumerate(((mine, halos), (theirs, their_halos), (mine, halos), (theirs, their_halos))):
            side = place // 2
            plane = a - 1 + 7 * side
            lanes = slice(128 * place, 128 * place + 128)
            if 0 <= plane < 8:
                cols[low:high, lanes] = ref[low:high, 128 * plane : 128 * plane + 128]
            else:
                moved = shifts(ends[128 * side : 128 * side + 128, :].astype(jnp.float32).T, 1, valid)
                for at in range(first - 9 * a, last - 9 * a):
                    cols[at * half : (at + 1) * half, lanes] = moved[at]
        start = (first - taps[0]) * half
        total[start : start + high - low, :] = inner[first * half : last * half, :] + jnp.dot(
            cols[low:high, :], facing, preferred_element_type=jnp.float32
        )
    upper = stage_half(size, 0)
    for tap in range(taps[1] - taps[0]):
        rows = slice(piece * tap, piece * tap + piece)
        other = pl.ds(pl.multiple_of(half * tap + (1 - upper) * piece, 16), piece)
        own = pl.ds(pl.multiple_of(half * tap + upper * piece, 16), piece)
        give[rows, :] = total[other, :].astype(jnp.bfloat16)
        stay[rows, :] = total[own, :]


def outer_terms(taps, size, mine, theirs, halos, their_halos, parcel, their_parcel, inner):
    width = inner.shape[1]
    half = mine.shape[0] // 9
    count = taps[1] - taps[0]
    rows = count * half // 2
    return pl.pallas_call(
        functools.partial(outer_terms_kernel, taps, size),
        in_specs=[WHOLE] * 7,
        out_specs=(WHOLE, WHOLE),
        out_shape=(pltpu.VMEM((rows, width), jnp.bfloat16), pltpu.VMEM((rows, width), jnp.float32)),
        scratch_shapes=[
            pltpu.VMEM((9 * half, 512), jnp.bfloat16),
            pltpu.VMEM((count * half, width), jnp.float32),
        ],
        compiler_params=params(),
        cost_estimate=cost(1024, 1024),
        name="outer_terms",
    )(*[near(x) for x in (mine, theirs, halos, their_halos, parcel, their_parcel, inner)])


def backward_rows(planes, mask, weight, cols, place):
    width = weight.shape[1]
    valid = windows((128, width), 0)
    for index, plane in enumerate(planes):
        rows = slice(128 * (place + index), 128 * (place + index) + 128)
        for at, moved in enumerate(shifts(plane.astype(jnp.float32), 0, valid, -1)):
            cols[rows, at * width : (at + 1) * width] = moved
    count = 128 * (len(planes) - 2)
    total = jnp.zeros((count, width), jnp.float32)
    for a in range(3):
        for at in range(9):
            start = 128 * (place + 2 - a)
            total += lax.dot_general(
                cols[start : start + count, at * width : (at + 1) * width],
                weight[9 * a + at],
                (((1,), (1,)), ((), ())),
                preferred_element_type=jnp.float32,
            )
    return jnp.where(wide(mask), total, 0.0).astype(jnp.bfloat16)


def backward_inner_kernel(grad, mask, weight, grad_feats, cols):
    planes = [grad[128 * (z - 1) : 128 * z, :] for z in range(1, 7)]
    done = backward_rows(planes, mask[256:768, :], weight, cols, 0)
    for z in range(2, 6):
        for b in range(2):
            start = 128 * (z - 2) + 64 * b
            grad_feats[b, z] = done[start : start + 64]


def backward_inner(grad, mask, weight):
    width = grad.shape[1]
    return pl.pallas_call(
        backward_inner_kernel,
        in_specs=[WHOLE] * 3,
        out_specs=WHOLE,
        out_shape=jax.ShapeDtypeStruct((2, 8, 64, width), jnp.bfloat16),
        scratch_shapes=[pltpu.VMEM((768, 9 * width), jnp.bfloat16)],
        compiler_params=params(),
        cost_estimate=cost(1024, 1024),
        name="backward_inner",
    )(near(grad), near(mask), near(weight))


def backward_outer_kernel(table, grad, parcel, mask, weight, done, *refs):
    arrived, (grad_feats, bias_sum, cols, planes, sent) = refs[:-5], refs[-5:]
    for side in range(2):
        halo = jnp.concatenate([chosen(table, 2 * side + b, arrived) for b in range(2)], axis=0)
        rim = parcel[128 * side : 128 * side + 128, :]
        if side == 0:
            around = [halo, rim, grad[:128, :], grad[128:256, :]]
        else:
            around = [grad[512:640, :], grad[640:768, :], rim, halo]
        first = 6 * side
        rows = backward_rows(around, mask[128 * first : 128 * first + 256, :], weight, cols, 4 * side)
        for z in range(2):
            for b in range(2):
                start = 128 * z + 64 * b
                planes[side, b, z] = rows[start : start + 64]
        pltpu.make_async_copy(planes.at[side], grad_feats.at[:, pl.ds(first, 2)], sent.at[side]).start()
    bias_sum[...] = sum(read_extra(ref) for ref in arrived)
    for side in range(2):
        pltpu.make_async_copy(planes.at[side], grad_feats.at[:, pl.ds(6 * side, 2)], sent.at[side]).wait()


def backward_outer(table, grad, parcel, mask, weight, done, arrived):
    width = grad.shape[1]
    return pl.pallas_call(
        backward_outer_kernel,
        in_specs=[SCALARS] + [WHOLE] * 4 + [FAR] + [WHOLE] * len(arrived),
        out_specs=(FAR, WHOLE),
        out_shape=(jax.ShapeDtypeStruct(done.shape, done.dtype), jax.ShapeDtypeStruct((1, width), jnp.float32)),
        scratch_shapes=[
            pltpu.VMEM((1024, 9 * width), jnp.bfloat16),
            pltpu.VMEM((2, 2, 2, 64, width), jnp.bfloat16),
            pltpu.SemaphoreType.DMA((2,)),
        ],
        input_output_aliases={5: 0},
        compiler_params=params(),
        cost_estimate=cost(1024, 1024),
        name="backward_outer",
    )(table, near(grad), near(parcel), near(mask), near(weight), done, *[near(x) for x in arrived])


def assemble_kernel(first, size, *refs):
    parts, (out, done) = refs[:4], refs[-2:]
    count = parts[0].shape[0]
    core = lax.axis_index("zslab") % 2
    mine, theirs = stage_half(size, 0), stage_half(size, 0, other=True)
    places = (2 * core + mine, 2 * core + 1 - mine, 2 - 2 * core + theirs, 3 - 2 * core - theirs)
    copies = [
        pltpu.make_async_copy(ref, out.at[pl.ds(first, count), place], done.at[index])
        for index, (ref, place) in enumerate(zip(parts, places))
    ]
    for copy in copies:
        copy.start()
    for copy in copies:
        copy.wait()


def assemble(first, size, parts, shape, done):
    given = [] if done is None else [done]
    return pl.pallas_call(
        functools.partial(assemble_kernel, first, size),
        in_specs=[WHOLE] * 4 + [FAR] * len(given),
        out_specs=FAR,
        out_shape=jax.ShapeDtypeStruct(shape, jnp.bfloat16),
        scratch_shapes=[pltpu.SemaphoreType.DMA((4,))],
        input_output_aliases={4: 0} if given else {},
        compiler_params=params(),
        cost_estimate=cost(1024, 1024),
        name="assemble",
    )(*[near(x) for x in parts], *given)


def gather_group(parcel, size):
    inner = swap(parcel, size, 2)
    return [parcel, inner, swap(parcel, size, 1), swap(inner, size, 1)]


def per_device(size, feats, voxmask, links, weight, bias, cotangent):
    width = feats.shape[3]
    outer = size // 4

    parcels = gather_group(rims(links, feats, voxmask), size)
    mask, rows, give, turned = prepare(feats, voxmask)
    rows, parcels[1] = lax.optimization_barrier((rows, parcels[1]))
    out, grad, edge, bias_local, weight, ends = forward_inside(rows, mask, weight, bias.reshape(1, width), cotangent)
    *parcels, grad = lax.optimization_barrier((*parcels, grad))
    table, picks = route(parcels, outer)

    *picks, give = lax.optimization_barrier((*picks, give))
    arrived = [rotate(pick, size, steps) if steps else pick for steps, pick in enumerate(picks)]
    their_turned = turn(swap(give, size, 1))
    inner = inner_terms(turned, their_turned, grad, swap(grad, size, 1))

    *arrived, inner = lax.optimization_barrier((*arrived, inner))
    out, parcel, halos, give = forward_edges(table, mask, weight, edge, ends, bias_local, out, arrived)
    their_halos = swap(give, size, 1)
    parcels = gather_group(parcel, size)

    stages = len(orders(size)[0])
    halves = [stage_half(size, stage) for stage in range(stages)]
    count = weight.shape[0]
    cuts = [(0, count // 2), (count // 2, count)]
    sums = []
    for taps in cuts:
        give, stay = outer_terms(taps, size, turned, their_turned, halos, their_halos, parcel, parcels[2], inner)
        sums.append((stay, swap_stage(give, size, 0)))

    grad_feats = backward_inner(grad, mask, weight)
    picks = repeat_route(table, parcels, outer)
    (stay, got), other = sums
    stay, grad_feats, *picks = lax.optimization_barrier((stay, grad_feats, *picks))
    sums = [(stay, got), other]
    arrived = [rotate(pick, size, steps) if steps else pick for steps, pick in enumerate(picks)]
    for stage in range(1, stages):
        for index, (stay, got) in enumerate(sums):
            give, stay = halve(stay, got, halves[stage])
            sums[index] = (stay, swap_stage(give, size, stage))
    parts = [(stay + got.astype(jnp.float32)).astype(jnp.bfloat16) for stay, got in sums]
    parts[0], *arrived = lax.optimization_barrier((parts[0], *arrived))
    for stage in reversed(range(1, stages)):
        parts = [join(part, swap_stage(part, size, stage), halves[stage]) for part in parts]
    grad_feats, grad_bias = backward_outer(table, grad, parcel, mask, weight, grad_feats, arrived)

    grad_weight = None
    for taps, part in zip(cuts, parts):
        last = swap_stage(part, size, 0)
        other = swap(part, size, 1)
        if grad_weight is None:
            last, grad_feats, grad_bias = lax.optimization_barrier((last, grad_feats, grad_bias))
        pieces = [x.reshape(taps[1] - taps[0], width // 4, width) for x in (part, last, other, swap(last, size, 1))]
        grad_weight = assemble(taps[0], size, pieces, (count, 4, width // 4, width), grad_weight)
    return out, grad_feats, grad_weight.reshape(count, width, width), grad_bias.reshape(width)


def solution(mesh):
    return jax.shard_map(
        functools.partial(per_device, mesh.shape["zslab"]),
        mesh=mesh,
        in_specs=(
            P(("groups", "zslab"), None, None, None),
            P(("groups", "zslab"), None),
            P(("groups", "zslab"), None),
            P(),
            P(),
            P(("groups", "zslab"), None, None, None),
        ),
        out_specs=(
            P(("groups", "zslab"), None, None, None),
            P(("groups", "zslab"), None, None, None),
            P("groups", None, None),
            P("groups"),
        ),
        check_vma=False,
    )
```

```python
import functools

import jax
import jax.numpy as jnp
from jax import lax
from jax.experimental import pallas as pl
from jax.experimental.pallas import tpu as pltpu
from jax.sharding import PartitionSpec as P

VMEM_LIMIT = 11 * 1024 * 1024
EXTRA = 16


def params():
    return pltpu.CompilerParams(vmem_limit_bytes=VMEM_LIMIT)


def cost(flops, bytes_accessed):
    return pl.CostEstimate(flops=flops, bytes_accessed=bytes_accessed, transcendentals=0)


def near(x):
    return pltpu.with_memory_space_constraint(x, pltpu.VMEM)


def far(x):
    return pltpu.with_memory_space_constraint(x, pltpu.HBM)


SCALARS = pl.BlockSpec(memory_space=pltpu.SMEM)
WHOLE = pl.BlockSpec(memory_space=pltpu.VMEM)
FAR = pl.BlockSpec(memory_space=pl.ANY)


def swap(x, size, bit):
    return lax.ppermute(x, "zslab", [(i, i ^ bit) for i in range(size)])


def rotate(x, size, steps):
    return lax.ppermute(x, "zslab", [(i, (i + 4 * steps) % size) for i in range(size)])


def orders(size):
    bits = [1 << k for k in range(1, size.bit_length() - 1)]
    return bits, [bits[1], bits[0]] + bits[2:]


def swap_stage(x, size, stage):
    both = orders(size)
    return lax.ppermute(x, "zslab", [(i, i ^ both[i % 2][stage]) for i in range(size)])


def stage_half(size, stage, other=False):
    me = lax.axis_index("zslab")
    low, high = (order[stage] for order in orders(size))
    core = me % 2 == (1 if other else 0)
    return jnp.where(core, (me // low) % 2, (me // high) % 2)


def take_rows(x, place, rows):
    return lax.dynamic_slice_in_dim(x, place * rows, rows, axis=0)


def halve(stay, got, mine):
    half = stay.shape[0] // 2
    give = take_rows(stay, 1 - mine, half) + take_rows(got, 1 - mine, half).astype(jnp.float32)
    keep = take_rows(stay, mine, half) + take_rows(got, mine, half).astype(jnp.float32)
    return give.astype(jnp.bfloat16), keep


def join(part, got, mine):
    return jnp.where(mine == 0, jnp.concatenate([part, got]), jnp.concatenate([got, part]))


def mask_rows(voxmask, z):
    lanes = slice(64 * z, 64 * z + 64)
    line = jnp.concatenate([voxmask[0:1, lanes], voxmask[1:2, lanes]], axis=1)
    return jnp.broadcast_to((line == 1).astype(jnp.float32), (128, 128)).T


def wide(mask):
    return jnp.concatenate([mask, mask], axis=1) > 0


def both(ref, z):
    return jnp.concatenate([ref[0, z], ref[1, z]], axis=0)


def inside(shape, dim, rows, cols):
    index = lax.broadcasted_iota(jnp.int32, shape, dim)
    row = (index // 8) % 8 + rows
    col = index % 8 + cols
    return (row >= 0) & (row < 8) & (col >= 0) & (col < 8)


def windows(shape, dim):
    return [inside(shape, dim, p, q) for p in (-1, 0, 1) for q in (-1, 0, 1)]


def shifts(x, dim, valid, sign=1):
    count = x.shape[dim]
    moved = []
    for place in range(9):
        at = place if sign == 1 else 8 - place
        move = 8 * (at // 3 - 1) + at % 3 - 1
        turned = pltpu.roll(x, (-move) % count, dim) if move else x
        moved.append(jnp.where(valid[at], turned, 0.0).astype(jnp.bfloat16))
    return moved


def activate(pre, cotangent, keep):
    sigma = 1.0 / (1.0 + jnp.exp(-pre))
    out = jnp.where(keep, pre * sigma, 0.0)
    grad = jnp.where(keep, cotangent * sigma * (1.0 + pre * (1.0 - sigma)), 0.0)
    return out.astype(jnp.bfloat16), grad.astype(jnp.bfloat16)


def write_exact(rows, ref):
    high = rows.astype(jnp.bfloat16)
    left = rows - high.astype(jnp.float32)
    middle = left.astype(jnp.bfloat16)
    low = (left - middle.astype(jnp.float32)).astype(jnp.bfloat16)
    zeros = jnp.zeros((EXTRA - 3, rows.shape[1]), jnp.float32)
    terms = [term.astype(jnp.float32) for term in (high, middle, low)]
    ref[256:272, :] = jnp.concatenate(terms + [zeros], axis=0).astype(jnp.bfloat16)


def read_extra(ref):
    return jnp.sum(ref[256:272, :].astype(jnp.float32), axis=0, keepdims=True)


def rims_kernel(links, feats, voxmask, parcel, planes, masks, codes, done):
    width = feats.shape[3]
    copies = [
        pltpu.make_async_copy(feats.at[:, pl.ds(0, 1)], planes.at[0], done.at[0]),
        pltpu.make_async_copy(feats.at[:, pl.ds(7, 1)], planes.at[1], done.at[1]),
        pltpu.make_async_copy(voxmask, masks, done.at[2]),
        pltpu.make_async_copy(links, codes, done.at[3]),
    ]
    for copy in copies:
        copy.start()
    for copy in copies:
        copy.wait()
    for side in range(2):
        keep = wide(mask_rows(masks, 7 * side))
        plane = jnp.concatenate([planes[side, 0, 0], planes[side, 1, 0]], axis=0).astype(jnp.float32)
        parcel[128 * side : 128 * side + 128, :] = jnp.where(keep, plane, 0.0).astype(jnp.bfloat16)
    lane = lax.broadcasted_iota(jnp.int32, (EXTRA, width), 1)
    row = jnp.zeros((EXTRA, width), jnp.float32)
    for place in range(4):
        row = jnp.where(lane == place, codes[place // 2, place % 2].astype(jnp.float32), row)
    parcel[256:272, :] = row.astype(jnp.bfloat16)


def rims(links, feats, voxmask):
    width = feats.shape[3]
    return pl.pallas_call(
        rims_kernel,
        in_specs=[FAR] * 3,
        out_specs=WHOLE,
        out_shape=pltpu.VMEM((256 + EXTRA, width), jnp.bfloat16),
        scratch_shapes=[
            pltpu.VMEM((2, 2, 1, 64, width), jnp.bfloat16),
            pltpu.VMEM(voxmask.shape, jnp.int32),
            pltpu.SMEM(links.shape, jnp.int32),
            pltpu.SemaphoreType.DMA((4,)),
        ],
        compiler_params=params(),
        cost_estimate=cost(1024, 1024),
        name="rims",
    )(far(links), far(feats), far(voxmask))


def prepare_kernel(feats, voxmask, mask, rows, give, turned, planes, masks, done):
    half = feats.shape[3] // 2
    pltpu.make_async_copy(voxmask, masks, done.at[8]).start()
    for z in range(8):
        pltpu.make_async_copy(feats.at[:, pl.ds(z, 1)], planes.at[:, pl.ds(z, 1)], done.at[z]).start()
    valid = windows((half, 128), 1)
    first = lax.axis_index("zslab") % 2 == 0
    pltpu.make_async_copy(voxmask, masks, done.at[8]).wait()
    for z in range(8):
        pltpu.make_async_copy(feats.at[:, pl.ds(z, 1)], planes.at[:, pl.ds(z, 1)], done.at[z]).wait()
        span = slice(128 * z, 128 * z + 128)
        keep = mask_rows(masks, z)
        mask[span, :] = keep
        plane = jnp.where(wide(keep), both(planes, z).astype(jnp.float32), 0.0)
        rows[span, :] = plane.astype(jnp.bfloat16)
        own = jnp.where(first, plane[:, :half], plane[:, half:])
        give[span, :] = jnp.where(first, plane[:, half:], plane[:, :half]).astype(jnp.bfloat16)
        for place, moved in enumerate(shifts(own.T, 1, valid)):
            turned[place * half : (place + 1) * half, span] = moved


def prepare(feats, voxmask):
    width = feats.shape[3]
    half = width // 2
    return pl.pallas_call(
        prepare_kernel,
        in_specs=[FAR, FAR],
        out_specs=(WHOLE,) * 4,
        out_shape=(
            pltpu.VMEM((1024, 128), jnp.float32),
            pltpu.VMEM((1024, width), jnp.bfloat16),
            pltpu.VMEM((1024, half), jnp.bfloat16),
            pltpu.VMEM((9 * half, 1024), jnp.bfloat16),
        ),
        scratch_shapes=[
            pltpu.VMEM(feats.shape, jnp.bfloat16),
            pltpu.VMEM(voxmask.shape, jnp.int32),
            pltpu.SemaphoreType.DMA((9,)),
        ],
        compiler_params=params(),
        cost_estimate=cost(1024, 1024),
        name="prepare",
    )(far(feats), far(voxmask))


def turn_kernel(rows, turned):
    half = rows.shape[1]
    valid = windows((half, 128), 1)
    for z in range(8):
        span = slice(128 * z, 128 * z + 128)
        for place, moved in enumerate(shifts(rows[span, :].astype(jnp.float32).T, 1, valid)):
            turned[place * half : (place + 1) * half, span] = moved


def turn(rows):
    half = rows.shape[1]
    return pl.pallas_call(
        turn_kernel,
        in_specs=[WHOLE],
        out_specs=WHOLE,
        out_shape=pltpu.VMEM((9 * half, 1024), jnp.bfloat16),
        compiler_params=params(),
        cost_estimate=cost(1024, 1024),
        name="turn",
    )(near(rows))


def copy_picks(outer, table, parcels, picks, planes):
    for dev in range(4):
        planes[256 * dev : 256 * dev + 256, :] = parcels[dev][:256, :]
    for steps in range(outer):
        for slot in range(4):
            start = pl.multiple_of(table[steps * 4 + slot] * 64, 64)
            picks[steps][64 * slot : 64 * slot + 64, :] = planes[pl.ds(start, 64), :]


def route_kernel(outer, *refs):
    me = lax.axis_index("zslab")
    parcels, (table, *picks), (codes, links, planes, done) = refs[:4], refs[4:-4], refs[-4:]
    for dev in range(4):
        row = parcels[dev][256:272, :128].astype(jnp.float32)
        codes[8 * dev : 8 * dev + 8, :] = row[:8, :].astype(jnp.int32)
    copy = pltpu.make_async_copy(codes, links, done)
    copy.start()
    copy.wait()
    for place in range(outer * 4):
        table[place] = 0
    for plane in range(16):
        dev, side, brick = plane // 4, plane // 2 % 2, plane % 2
        dest = links[dev * 8, brick * 2 + side]

        @pl.when((dest >= 0) & ((dest // 2) % 4 == me % 4))
        def _():
            steps = lax.rem(dest // 8 - me // 4 + outer, outer)
            table[steps * 4 + dest % 2 + (0 if side == 1 else 2)] = plane

    for brick in range(2):
        for side in range(2):
            dest = links[0, brick * 2 + side]
            steps = lax.rem(me // 4 - dest // 8 + outer, outer)
            table[outer * 4 + 2 * side + brick] = jnp.where(dest >= 0, steps, -1)

    copy_picks(outer, table, parcels, picks, planes)


def route(parcels, outer):
    width = parcels[0].shape[1]
    results = pl.pallas_call(
        functools.partial(route_kernel, outer),
        in_specs=[WHOLE] * 4,
        out_specs=[SCALARS] + [WHOLE] * outer,
        out_shape=[jax.ShapeDtypeStruct((outer * 4 + 4,), jnp.int32)]
        + [pltpu.VMEM((256, width), jnp.bfloat16)] * outer,
        scratch_shapes=[
            pltpu.VMEM((32, 128), jnp.int32),
            pltpu.SMEM((32, 128), jnp.int32),
            pltpu.VMEM((1024, width), jnp.bfloat16),
            pltpu.SemaphoreType.DMA(()),
        ],
        compiler_params=params(),
        cost_estimate=cost(1024, 1024),
        name="route",
    )(*[near(x) for x in parcels])
    return results[0], results[1:]


def repeat_kernel(outer, table, *refs):
    parcels, picks, planes = refs[:4], refs[4:-1], refs[-1]
    copy_picks(outer, table, parcels, picks, planes)
    total = sum(read_extra(ref) for ref in parcels)
    for ref in picks:
        write_exact(total, ref)


def repeat_route(table, parcels, outer):
    width = parcels[0].shape[1]
    return pl.pallas_call(
        functools.partial(repeat_kernel, outer),
        in_specs=[SCALARS] + [WHOLE] * 4,
        out_specs=[WHOLE] * outer,
        out_shape=[pltpu.VMEM((256 + EXTRA, width), jnp.bfloat16)] * outer,
        scratch_shapes=[pltpu.VMEM((1024, width), jnp.bfloat16)],
        compiler_params=params(),
        cost_estimate=cost(1024, 1024),
        name="repeat_route",
    )(table, *[near(x) for x in parcels])


def chosen(table, slot, arrived):
    rows = slice(64 * slot, 64 * slot + 64)
    plane = jnp.zeros((64, arrived[0].shape[1]), jnp.float32)
    for steps, ref in enumerate(arrived):
        plane = jnp.where(table[4 * len(arrived) + slot] == steps, ref[rows, :].astype(jnp.float32), plane)
    return plane


def fetch_taps(weight, near_weight, done):
    for tap in range(weight.shape[0]):
        pltpu.make_async_copy(weight.at[tap], near_weight.at[tap], done.at[tap]).start()


def await_taps(first, last, weight, near_weight, done):
    for tap in range(first, last):
        pltpu.make_async_copy(weight.at[tap], near_weight.at[tap], done.at[tap]).wait()


def forward_kernel(rows, mask, weight, bias, cotangent, out, grad, edge, bias_sum, near_weight, ends, cols, pre, slopes, shift, done):
    width = rows.shape[1]
    count = weight.shape[0]
    copies = [pltpu.make_async_copy(bias, shift, done.at[count])]
    for z in range(8):
        part = pl.ds(z, 1)
        copies.append(pltpu.make_async_copy(cotangent.at[:, part], slopes.at[:, part], done.at[count + 1 + z]))
    fetch_taps(weight, near_weight, done)
    for copy in copies:
        copy.start()
    valid = windows((128, width), 0)
    for z in range(8):
        span = slice(128 * z, 128 * z + 128)
        for place, moved in enumerate(shifts(rows[span, :].astype(jnp.float32), 0, valid)):
            cols[span, place * width : (place + 1) * width] = moved

    def taps(a):
        return near_weight[9 * a : 9 * a + 9].reshape(9 * width, width)

    copies[0].wait()
    await_taps(9, 18, weight, near_weight, done)
    pre[...] = jnp.dot(cols[...], taps(1), preferred_element_type=jnp.float32) + shift[...]
    await_taps(0, 9, weight, near_weight, done)
    pre[128:, :] += jnp.dot(cols[:896, :], taps(0), preferred_element_type=jnp.float32)
    await_taps(18, 27, weight, near_weight, done)
    pre[:896, :] += jnp.dot(cols[128:, :], taps(2), preferred_element_type=jnp.float32)
    for copy in copies[1:]:
        copy.wait()
    for side in range(2):
        edge[side] = pre[896 * side : 896 * side + 128, :]
        ends[side] = both(slopes, 7 * side)
    total = jnp.zeros((1, width), jnp.float32)
    for z in range(1, 7):
        span = slice(128 * z, 128 * z + 128)
        act, slope = activate(pre[span, :], both(slopes, z).astype(jnp.float32), wide(mask[span, :]))
        for b in range(2):
            out[b, z] = act[64 * b : 64 * b + 64]
        grad[128 * (z - 1) : 128 * z, :] = slope
        total += jnp.sum(slope.astype(jnp.float32), axis=0, keepdims=True)
    bias_sum[...] = total


def forward_inside(rows, mask, weight, bias, cotangent):
    width = rows.shape[1]
    return pl.pallas_call(
        forward_kernel,
        in_specs=[WHOLE, WHOLE, FAR, FAR, FAR],
        out_specs=(WHOLE,) * 6,
        out_shape=(
            jax.ShapeDtypeStruct(cotangent.shape, jnp.bfloat16),
            pltpu.VMEM((768, width), jnp.bfloat16),
            pltpu.VMEM((2, 128, width), jnp.float32),
            pltpu.VMEM((1, width), jnp.float32),
            pltpu.VMEM(weight.shape, jnp.bfloat16),
            pltpu.VMEM((2, 128, width), jnp.bfloat16),
        ),
        scratch_shapes=[
            pltpu.VMEM((1024, 9 * width), jnp.bfloat16),
            pltpu.VMEM((1024, width), jnp.float32),
            pltpu.VMEM(cotangent.shape, jnp.bfloat16),
            pltpu.VMEM((1, width), jnp.float32),
            pltpu.SemaphoreType.DMA((weight.shape[0] + 9,)),
        ],
        compiler_params=params(),
        cost_estimate=cost(1024, 1024),
        name="forward_inside",
    )(near(rows), near(mask), far(weight), far(bias), far(cotangent))


def inner_terms_kernel(mine, theirs, grad, their_grad, terms):
    rows = mine.shape[0]
    for a in range(3):
        lanes = slice(128 * a, 128 * a + 768)
        terms[a * rows : (a + 1) * rows, :] = jnp.dot(
            mine[:, lanes], grad[...], preferred_element_type=jnp.float32
        ) + jnp.dot(theirs[:, lanes], their_grad[...], preferred_element_type=jnp.float32)


def inner_terms(mine, theirs, grad, their_grad):
    rows, width = mine.shape[0], grad.shape[1]
    return pl.pallas_call(
        inner_terms_kernel,
        in_specs=[WHOLE] * 4,
        out_specs=WHOLE,
        out_shape=pltpu.VMEM((3 * rows, width), jnp.float32),
        compiler_params=params(),
        cost_estimate=cost(1024, 1024),
        name="inner_terms",
    )(near(mine), near(theirs), near(grad), near(their_grad))


def edge_kernel(table, mask, weight, edge, ends, inner, out_in, *refs):
    arrived, (out, parcel, own, give, planes, done) = refs[:-6], refs[-6:]
    width = edge.shape[2]
    half = width // 2
    valid = windows((128, width), 0)
    total = inner[...]
    for side in range(2):
        rows = slice(128 * side, 128 * side + 128)
        halo = jnp.concatenate([chosen(table, 2 * side + b, arrived) for b in range(2)], axis=0)
        first = lax.axis_index("zslab") % 2 == 0
        own[rows, :] = jnp.where(first, halo[:, :half], halo[:, half:]).astype(jnp.bfloat16)
        give[rows, :] = jnp.where(first, halo[:, half:], halo[:, :half]).astype(jnp.bfloat16)
        cols = jnp.concatenate(shifts(halo, 0, valid), axis=1)
        taps = weight[18 * side : 18 * side + 9].reshape(9 * width, width)
        pre = edge[side] + jnp.dot(cols, taps, preferred_element_type=jnp.float32)
        z = 7 * side
        keep = wide(mask[128 * z : 128 * z + 128, :])
        act, slope = activate(pre, ends[side].astype(jnp.float32), keep)
        for b in range(2):
            planes[side, b, 0] = act[64 * b : 64 * b + 64]
        pltpu.make_async_copy(planes.at[side], out.at[:, pl.ds(z, 1)], done.at[side]).start()
        parcel[rows, :] = slope
        total += jnp.sum(slope.astype(jnp.float32), axis=0, keepdims=True)
    write_exact(total, parcel)
    for side in range(2):
        pltpu.make_async_copy(planes.at[side], out.at[:, pl.ds(7 * side, 1)], done.at[side]).wait()


def forward_edges(table, mask, weight, edge, ends, inner, out, arrived):
    width = edge.shape[2]
    return pl.pallas_call(
        edge_kernel,
        in_specs=[SCALARS] + [WHOLE] * 5 + [FAR] + [WHOLE] * len(arrived),
        out_specs=(FAR, WHOLE, WHOLE, WHOLE),
        out_shape=(
            jax.ShapeDtypeStruct(out.shape, out.dtype),
            pltpu.VMEM((256 + EXTRA, width), jnp.bfloat16),
            pltpu.VMEM((256, width // 2), jnp.bfloat16),
            pltpu.VMEM((256, width // 2), jnp.bfloat16),
        ),
        scratch_shapes=[pltpu.VMEM((2, 2, 1, 64, width), jnp.bfloat16), pltpu.SemaphoreType.DMA((2,))],
        input_output_aliases={6: 0},
        compiler_params=params(),
        cost_estimate=cost(1024, 1024),
        name="forward_edges",
    )(
        table,
        near(mask),
        near(weight),
        near(edge),
        near(ends),
        near(inner),
        out,
        *[near(x) for x in arrived],
    )


def outer_terms_kernel(taps, size, mine, theirs, halos, their_halos, parcel, their_parcel, inner, give, stay, cols, total):
    half = mine.shape[0] // 9
    piece = half // 2
    valid = windows((half, 128), 1)
    facing = jnp.concatenate([parcel[:128], their_parcel[:128], parcel[128:256], their_parcel[128:256]], axis=0)
    for a in range(3):
        first, last = max(taps[0], 9 * a), min(taps[1], 9 * a + 9)
        if first >= last:
            continue
        low, high = (first - 9 * a) * half, (last - 9 * a) * half
        for place, (ref, ends) in enumerate(((mine, halos), (theirs, their_halos), (mine, halos), (theirs, their_halos))):
            side = place // 2
            plane = a - 1 + 7 * side
            lanes = slice(128 * place, 128 * place + 128)
            if 0 <= plane < 8:
                cols[low:high, lanes] = ref[low:high, 128 * plane : 128 * plane + 128]
            else:
                moved = shifts(ends[128 * side : 128 * side + 128, :].astype(jnp.float32).T, 1, valid)
                for at in range(first - 9 * a, last - 9 * a):
                    cols[at * half : (at + 1) * half, lanes] = moved[at]
        start = (first - taps[0]) * half
        total[start : start + high - low, :] = inner[first * half : last * half, :] + jnp.dot(
            cols[low:high, :], facing, preferred_element_type=jnp.float32
        )
    upper = stage_half(size, 0)
    for tap in range(taps[1] - taps[0]):
        rows = slice(piece * tap, piece * tap + piece)
        other = pl.ds(pl.multiple_of(half * tap + (1 - upper) * piece, 16), piece)
        own = pl.ds(pl.multiple_of(half * tap + upper * piece, 16), piece)
        give[rows, :] = total[other, :].astype(jnp.bfloat16)
        stay[rows, :] = total[own, :]


def outer_terms(taps, size, mine, theirs, halos, their_halos, parcel, their_parcel, inner):
    width = inner.shape[1]
    half = mine.shape[0] // 9
    count = taps[1] - taps[0]
    rows = count * half // 2
    return pl.pallas_call(
        functools.partial(outer_terms_kernel, taps, size),
        in_specs=[WHOLE] * 7,
        out_specs=(WHOLE, WHOLE),
        out_shape=(pltpu.VMEM((rows, width), jnp.bfloat16), pltpu.VMEM((rows, width), jnp.float32)),
        scratch_shapes=[
            pltpu.VMEM((9 * half, 512), jnp.bfloat16),
            pltpu.VMEM((count * half, width), jnp.float32),
        ],
        compiler_params=params(),
        cost_estimate=cost(1024, 1024),
        name="outer_terms",
    )(*[near(x) for x in (mine, theirs, halos, their_halos, parcel, their_parcel, inner)])


def backward_rows(planes, mask, weight, cols, place, await_weight=None):
    width = weight.shape[1]
    valid = windows((128, width), 0)
    for index, plane in enumerate(planes):
        rows = slice(128 * (place + index), 128 * (place + index) + 128)
        for at, moved in enumerate(shifts(plane.astype(jnp.float32), 0, valid, -1)):
            cols[rows, at * width : (at + 1) * width] = moved
    if await_weight:
        await_weight()
    count = 128 * (len(planes) - 2)
    total = jnp.zeros((count, width), jnp.float32)
    for a in range(3):
        for at in range(9):
            start = 128 * (place + 2 - a)
            total += lax.dot_general(
                cols[start : start + count, at * width : (at + 1) * width],
                weight[9 * a + at],
                (((1,), (1,)), ((), ())),
                preferred_element_type=jnp.float32,
            )
    return jnp.where(wide(mask), total, 0.0).astype(jnp.bfloat16)


def backward_inner_kernel(grad, mask, weight, grad_feats, cols):
    planes = [grad[128 * (z - 1) : 128 * z, :] for z in range(1, 7)]
    done = backward_rows(planes, mask[256:768, :], weight, cols, 0)
    for z in range(2, 6):
        for b in range(2):
            start = 128 * (z - 2) + 64 * b
            grad_feats[b, z] = done[start : start + 64]


def backward_inner(grad, mask, weight):
    width = grad.shape[1]
    return pl.pallas_call(
        backward_inner_kernel,
        in_specs=[WHOLE] * 3,
        out_specs=WHOLE,
        out_shape=jax.ShapeDtypeStruct((2, 8, 64, width), jnp.bfloat16),
        scratch_shapes=[pltpu.VMEM((768, 9 * width), jnp.bfloat16)],
        compiler_params=params(),
        cost_estimate=cost(1024, 1024),
        name="backward_inner",
    )(near(grad), near(mask), near(weight))


def backward_outer_kernel(table, grad, parcel, mask, weight, done, *refs):
    arrived, (grad_feats, bias_sum, cols, planes, near_weight, fetched, sent) = refs[:-7], refs[-7:]
    fetch_taps(weight, near_weight, fetched)
    for side in range(2):
        halo = jnp.concatenate([chosen(table, 2 * side + b, arrived) for b in range(2)], axis=0)
        rim = parcel[128 * side : 128 * side + 128, :]
        if side == 0:
            around = [halo, rim, grad[:128, :], grad[128:256, :]]
        else:
            around = [grad[512:640, :], grad[640:768, :], rim, halo]
        first = 6 * side
        await_now = (lambda: await_taps(0, weight.shape[0], weight, near_weight, fetched)) if side == 0 else None
        keep = mask[128 * first : 128 * first + 256, :]
        rows = backward_rows(around, keep, near_weight, cols, 4 * side, await_now)
        for z in range(2):
            for b in range(2):
                start = 128 * z + 64 * b
                planes[side, b, z] = rows[start : start + 64]
        pltpu.make_async_copy(planes.at[side], grad_feats.at[:, pl.ds(first, 2)], sent.at[side]).start()
    bias_sum[...] = sum(read_extra(ref) for ref in arrived)
    for side in range(2):
        pltpu.make_async_copy(planes.at[side], grad_feats.at[:, pl.ds(6 * side, 2)], sent.at[side]).wait()


def backward_outer(table, grad, parcel, mask, weight, done, arrived):
    width = grad.shape[1]
    return pl.pallas_call(
        backward_outer_kernel,
        in_specs=[SCALARS] + [WHOLE] * 3 + [FAR, FAR] + [WHOLE] * len(arrived),
        out_specs=(FAR, WHOLE),
        out_shape=(jax.ShapeDtypeStruct(done.shape, done.dtype), jax.ShapeDtypeStruct((1, width), jnp.float32)),
        scratch_shapes=[
            pltpu.VMEM((1024, 9 * width), jnp.bfloat16),
            pltpu.VMEM((2, 2, 2, 64, width), jnp.bfloat16),
            pltpu.VMEM(weight.shape, jnp.bfloat16),
            pltpu.SemaphoreType.DMA((weight.shape[0],)),
            pltpu.SemaphoreType.DMA((2,)),
        ],
        input_output_aliases={5: 0},
        compiler_params=params(),
        cost_estimate=cost(1024, 1024),
        name="backward_outer",
    )(table, near(grad), near(parcel), near(mask), far(weight), done, *[near(x) for x in arrived])


def assemble_kernel(first, size, *refs):
    parts, (out, done) = refs[:4], refs[-2:]
    count = parts[0].shape[0]
    core = lax.axis_index("zslab") % 2
    mine, theirs = stage_half(size, 0), stage_half(size, 0, other=True)
    places = (2 * core + mine, 2 * core + 1 - mine, 2 - 2 * core + theirs, 3 - 2 * core - theirs)
    copies = [
        pltpu.make_async_copy(ref, out.at[pl.ds(first, count), place], done.at[index])
        for index, (ref, place) in enumerate(zip(parts, places))
    ]
    for copy in copies:
        copy.start()
    for copy in copies:
        copy.wait()


def assemble(first, size, parts, shape, done):
    given = [] if done is None else [done]
    return pl.pallas_call(
        functools.partial(assemble_kernel, first, size),
        in_specs=[WHOLE] * 4 + [FAR] * len(given),
        out_specs=FAR,
        out_shape=jax.ShapeDtypeStruct(shape, jnp.bfloat16),
        scratch_shapes=[pltpu.SemaphoreType.DMA((4,))],
        input_output_aliases={4: 0} if given else {},
        compiler_params=params(),
        cost_estimate=cost(1024, 1024),
        name="assemble",
    )(*[near(x) for x in parts], *given)


def gather_group(parcel, size, before=()):
    inner, *before = lax.optimization_barrier((swap(parcel, size, 2), *before))
    return [parcel, inner, swap(parcel, size, 1), swap(inner, size, 1)], *before


def per_device(size, feats, voxmask, links, weight, bias, cotangent):
    width = feats.shape[3]
    outer = size // 4

    mask, rows, give, turned = prepare(feats, voxmask)
    parcels, rows = gather_group(rims(links, feats, voxmask), size, (rows,))
    out, grad, edge, bias_local, taps, ends = forward_inside(rows, mask, weight, bias.reshape(1, width), cotangent)
    *parcels, grad = lax.optimization_barrier((*parcels, grad))
    table, picks = route(parcels, outer)

    *picks, give = lax.optimization_barrier((*picks, give))
    arrived = [rotate(pick, size, steps) if steps else pick for steps, pick in enumerate(picks)]
    their_turned = turn(swap(give, size, 1))
    inner = inner_terms(turned, their_turned, grad, swap(grad, size, 1))

    grad_feats = backward_inner(grad, mask, taps)
    *arrived, inner, grad_feats = lax.optimization_barrier((*arrived, inner, grad_feats))
    out, parcel, halos, give = forward_edges(table, mask, taps, edge, ends, bias_local, out, arrived)
    their_halos = swap(give, size, 1)
    parcels, halos = gather_group(parcel, size, (halos,))

    stages = len(orders(size)[0])
    halves = [stage_half(size, stage) for stage in range(stages)]
    count = weight.shape[0]
    cuts = [(0, count // 2), (count // 2, count)]
    sums = []
    for cut in cuts:
        give, stay = outer_terms(cut, size, turned, their_turned, halos, their_halos, parcel, parcels[2], inner)
        sums.append((stay, swap_stage(give, size, 0)))

    picks = repeat_route(table, parcels, outer)
    (stay, got), other = sums
    stay, *picks = lax.optimization_barrier((stay, *picks))
    sums = [(stay, got), other]
    arrived = [rotate(pick, size, steps) if steps else pick for steps, pick in enumerate(picks)]
    for stage in range(1, stages):
        for index, (stay, got) in enumerate(sums):
            give, stay = halve(stay, got, halves[stage])
            sums[index] = (stay, swap_stage(give, size, stage))
    parts = [(stay + got.astype(jnp.float32)).astype(jnp.bfloat16) for stay, got in sums]
    parts[0], *arrived = lax.optimization_barrier((parts[0], *arrived))
    for stage in reversed(range(1, stages)):
        parts = [join(part, swap_stage(part, size, stage), halves[stage]) for part in parts]
    grad_feats, grad_bias = backward_outer(table, grad, parcel, mask, weight, grad_feats, arrived)

    grad_weight = None
    for cut, part in zip(cuts, parts):
        last = swap_stage(part, size, 0)
        other = swap(part, size, 1)
        if grad_weight is None:
            last, grad_feats, grad_bias = lax.optimization_barrier((last, grad_feats, grad_bias))
        pieces = [x.reshape(cut[1] - cut[0], width // 4, width) for x in (part, last, other, swap(last, size, 1))]
        grad_weight = assemble(cut[0], size, pieces, (count, 4, width // 4, width), grad_weight)
    return out, grad_feats, grad_weight.reshape(count, width, width), grad_bias.reshape(width)


def solution(mesh):
    return jax.shard_map(
        functools.partial(per_device, mesh.shape["zslab"]),
        mesh=mesh,
        in_specs=(
            P(("groups", "zslab"), None, None, None),
            P(("groups", "zslab"), None),
            P(("groups", "zslab"), None),
            P(),
            P(),
            P(("groups", "zslab"), None, None, None),
        ),
        out_specs=(
            P(("groups", "zslab"), None, None, None),
            P(("groups", "zslab"), None, None, None),
            P("groups", None, None),
            P("groups"),
        ),
        check_vma=False,
    )
```

```python
import functools

import jax
import jax.numpy as jnp
from jax import lax
from jax.experimental import pallas as pl
from jax.experimental.pallas import tpu as pltpu
from jax.sharding import PartitionSpec as P

EXTRA = 16


def params(mebibytes=6):
    return pltpu.CompilerParams(vmem_limit_bytes=mebibytes * 1024 * 1024)


def cost(flops, bytes_accessed):
    return pl.CostEstimate(flops=flops, bytes_accessed=bytes_accessed, transcendentals=0)


def near(x):
    return pltpu.with_memory_space_constraint(x, pltpu.VMEM)


def far(x):
    return pltpu.with_memory_space_constraint(x, pltpu.HBM)


SCALARS = pl.BlockSpec(memory_space=pltpu.SMEM)
WHOLE = pl.BlockSpec(memory_space=pltpu.VMEM)
FAR = pl.BlockSpec(memory_space=pl.ANY)


def swap(x, size, bit):
    return lax.ppermute(x, "zslab", [(i, i ^ bit) for i in range(size)])


def rotate(x, size, steps):
    return lax.ppermute(x, "zslab", [(i, (i + 4 * steps) % size) for i in range(size)])


def stage_count(size):
    return size.bit_length() - 2


def swap_stage(x, size, stage):
    return swap(x, size, 2 << stage)


def stage_half(size, stage):
    return (lax.axis_index("zslab") // (2 << stage)) % 2


def take_rows(x, place, rows):
    return lax.dynamic_slice_in_dim(x, place * rows, rows, axis=0)


def halve(stay, got, mine):
    half = stay.shape[0] // 2
    give = take_rows(stay, 1 - mine, half) + take_rows(got, 1 - mine, half).astype(jnp.float32)
    keep = take_rows(stay, mine, half) + take_rows(got, mine, half).astype(jnp.float32)
    return give.astype(jnp.bfloat16), keep


def join(part, got, mine):
    return jnp.where(mine == 0, jnp.concatenate([part, got]), jnp.concatenate([got, part]))


def mask_rows(voxmask, z):
    lanes = slice(64 * z, 64 * z + 64)
    line = jnp.concatenate([voxmask[0:1, lanes], voxmask[1:2, lanes]], axis=1)
    return jnp.broadcast_to((line == 1).astype(jnp.float32), (128, 128)).T


def wide(mask):
    return jnp.concatenate([mask, mask], axis=1) > 0


def both(ref, z):
    return jnp.concatenate([ref[0, z], ref[1, z]], axis=0)


def inside(shape, dim, rows, cols):
    index = lax.broadcasted_iota(jnp.int32, shape, dim)
    row = (index // 8) % 8 + rows
    col = index % 8 + cols
    return (row >= 0) & (row < 8) & (col >= 0) & (col < 8)


def windows(shape, dim):
    return [inside(shape, dim, p, q) for p in (-1, 0, 1) for q in (-1, 0, 1)]


def shifts(x, dim, valid, sign=1):
    count = x.shape[dim]
    moved = []
    for place in range(9):
        at = place if sign == 1 else 8 - place
        move = 8 * (at // 3 - 1) + at % 3 - 1
        turned = pltpu.roll(x, (-move) % count, dim) if move else x
        moved.append(jnp.where(valid[at], turned, 0.0).astype(jnp.bfloat16))
    return moved


def activate(pre, cotangent, keep):
    sigma = 1.0 / (1.0 + jnp.exp(-pre))
    out = jnp.where(keep, pre * sigma, 0.0)
    grad = jnp.where(keep, cotangent * sigma * (1.0 + pre * (1.0 - sigma)), 0.0)
    return out.astype(jnp.bfloat16), grad.astype(jnp.bfloat16)


def write_exact(rows, ref):
    high = rows.astype(jnp.bfloat16)
    left = rows - high.astype(jnp.float32)
    middle = left.astype(jnp.bfloat16)
    low = (left - middle.astype(jnp.float32)).astype(jnp.bfloat16)
    zeros = jnp.zeros((EXTRA - 3, rows.shape[1]), jnp.float32)
    terms = [term.astype(jnp.float32) for term in (high, middle, low)]
    ref[256:272, :] = jnp.concatenate(terms + [zeros], axis=0).astype(jnp.bfloat16)


def read_extra(ref):
    return jnp.sum(ref[256:272, :].astype(jnp.float32), axis=0, keepdims=True)


def rims_kernel(links, feats, voxmask, parcel, planes, masks, codes, done):
    width = feats.shape[3]
    copies = [
        pltpu.make_async_copy(feats.at[:, pl.ds(0, 1)], planes.at[0], done.at[0]),
        pltpu.make_async_copy(feats.at[:, pl.ds(7, 1)], planes.at[1], done.at[1]),
        pltpu.make_async_copy(voxmask, masks, done.at[2]),
        pltpu.make_async_copy(links, codes, done.at[3]),
    ]
    for copy in copies:
        copy.start()
    for copy in copies:
        copy.wait()
    for side in range(2):
        keep = wide(mask_rows(masks, 7 * side))
        plane = jnp.concatenate([planes[side, 0, 0], planes[side, 1, 0]], axis=0).astype(jnp.float32)
        parcel[128 * side : 128 * side + 128, :] = jnp.where(keep, plane, 0.0).astype(jnp.bfloat16)
    lane = lax.broadcasted_iota(jnp.int32, (EXTRA, width), 1)
    row = jnp.zeros((EXTRA, width), jnp.float32)
    for place in range(4):
        row = jnp.where(lane == place, codes[place // 2, place % 2].astype(jnp.float32), row)
    parcel[256:272, :] = row.astype(jnp.bfloat16)


def rims(links, feats, voxmask):
    width = feats.shape[3]
    return pl.pallas_call(
        rims_kernel,
        in_specs=[FAR] * 3,
        out_specs=WHOLE,
        out_shape=pltpu.VMEM((256 + EXTRA, width), jnp.bfloat16),
        scratch_shapes=[
            pltpu.VMEM((2, 2, 1, 64, width), jnp.bfloat16),
            pltpu.VMEM(voxmask.shape, jnp.int32),
            pltpu.SMEM(links.shape, jnp.int32),
            pltpu.SemaphoreType.DMA((4,)),
        ],
        compiler_params=params(),
        cost_estimate=cost(1024, 1024),
        name="rims",
    )(far(links), far(feats), far(voxmask))


def fetch_taps(weight, near_weight, done):
    for tap in range(weight.shape[0]):
        pltpu.make_async_copy(weight.at[tap], near_weight.at[tap], done.at[tap]).start()


def await_taps(first, last, weight, near_weight, done):
    for tap in range(first, last):
        pltpu.make_async_copy(weight.at[tap], near_weight.at[tap], done.at[tap]).wait()


def prepare_kernel(feats, voxmask, weight, cotangent, mask, rows, give, turned, taps, slopes, planes, masks, done, fetched):
    half = feats.shape[3] // 2
    count = weight.shape[0]
    pltpu.make_async_copy(voxmask, masks, done.at[8]).start()
    for z in range(8):
        pltpu.make_async_copy(feats.at[:, pl.ds(z, 1)], planes.at[:, pl.ds(z, 1)], done.at[z]).start()
    fetch_taps(weight, taps, fetched)
    for z in range(8):
        pltpu.make_async_copy(cotangent.at[:, pl.ds(z, 1)], slopes.at[:, pl.ds(z, 1)], fetched.at[count + z]).start()
    valid = windows((half, 128), 1)
    first = lax.axis_index("zslab") % 2 == 0
    pltpu.make_async_copy(voxmask, masks, done.at[8]).wait()
    for z in range(8):
        pltpu.make_async_copy(feats.at[:, pl.ds(z, 1)], planes.at[:, pl.ds(z, 1)], done.at[z]).wait()
        span = slice(128 * z, 128 * z + 128)
        keep = mask_rows(masks, z)
        mask[span, :] = keep
        plane = jnp.where(wide(keep), both(planes, z).astype(jnp.float32), 0.0)
        rows[span, :] = plane.astype(jnp.bfloat16)
        own = jnp.where(first, plane[:, :half], plane[:, half:])
        give[span, :] = jnp.where(first, plane[:, half:], plane[:, :half]).astype(jnp.bfloat16)
        for place, moved in enumerate(shifts(own.T, 1, valid)):
            turned[place * half : (place + 1) * half, span] = moved
    await_taps(0, count, weight, taps, fetched)
    for z in range(8):
        pltpu.make_async_copy(cotangent.at[:, pl.ds(z, 1)], slopes.at[:, pl.ds(z, 1)], fetched.at[count + z]).wait()


def prepare(feats, voxmask, weight, cotangent):
    width = feats.shape[3]
    half = width // 2
    return pl.pallas_call(
        prepare_kernel,
        in_specs=[FAR] * 4,
        out_specs=(WHOLE,) * 6,
        out_shape=(
            pltpu.VMEM((1024, 128), jnp.float32),
            pltpu.VMEM((1024, width), jnp.bfloat16),
            pltpu.VMEM((1024, half), jnp.bfloat16),
            pltpu.VMEM((9 * half, 1024), jnp.bfloat16),
            pltpu.VMEM(weight.shape, jnp.bfloat16),
            pltpu.VMEM(cotangent.shape, jnp.bfloat16),
        ),
        scratch_shapes=[
            pltpu.VMEM(feats.shape, jnp.bfloat16),
            pltpu.VMEM(voxmask.shape, jnp.int32),
            pltpu.SemaphoreType.DMA((9,)),
            pltpu.SemaphoreType.DMA((weight.shape[0] + 8,)),
        ],
        compiler_params=params(10),
        cost_estimate=cost(1024, 1024),
        name="prepare",
    )(far(feats), far(voxmask), far(weight), far(cotangent))


def turn_kernel(rows, turned):
    half = rows.shape[1]
    valid = windows((half, 128), 1)
    for z in range(8):
        span = slice(128 * z, 128 * z + 128)
        for place, moved in enumerate(shifts(rows[span, :].astype(jnp.float32).T, 1, valid)):
            turned[place * half : (place + 1) * half, span] = moved


def turn(rows):
    half = rows.shape[1]
    return pl.pallas_call(
        turn_kernel,
        in_specs=[WHOLE],
        out_specs=WHOLE,
        out_shape=pltpu.VMEM((9 * half, 1024), jnp.bfloat16),
        compiler_params=params(),
        cost_estimate=cost(1024, 1024),
        name="turn",
    )(near(rows))


def copy_picks(outer, table, parcels, picks, planes):
    for dev in range(4):
        planes[256 * dev : 256 * dev + 256, :] = parcels[dev][:256, :]
    for steps in range(outer):
        for slot in range(4):
            start = pl.multiple_of(table[steps * 4 + slot] * 64, 64)
            picks[steps][64 * slot : 64 * slot + 64, :] = planes[pl.ds(start, 64), :]


def route_kernel(outer, *refs):
    me = lax.axis_index("zslab")
    parcels, (table, *picks), (codes, links, planes, done) = refs[:4], refs[4:-4], refs[-4:]
    for dev in range(4):
        row = parcels[dev][256:272, :128].astype(jnp.float32)
        codes[8 * dev : 8 * dev + 8, :] = row[:8, :].astype(jnp.int32)
    copy = pltpu.make_async_copy(codes, links, done)
    copy.start()
    copy.wait()
    for place in range(outer * 4):
        table[place] = 0
    for plane in range(16):
        dev, side, brick = plane // 4, plane // 2 % 2, plane % 2
        dest = links[dev * 8, brick * 2 + side]

        @pl.when((dest >= 0) & ((dest // 2) % 4 == me % 4))
        def _():
            steps = lax.rem(dest // 8 - me // 4 + outer, outer)
            table[steps * 4 + dest % 2 + (0 if side == 1 else 2)] = plane

    for brick in range(2):
        for side in range(2):
            dest = links[0, brick * 2 + side]
            steps = lax.rem(me // 4 - dest // 8 + outer, outer)
            table[outer * 4 + 2 * side + brick] = jnp.where(dest >= 0, steps, -1)

    copy_picks(outer, table, parcels, picks, planes)


def route(parcels, outer):
    width = parcels[0].shape[1]
    results = pl.pallas_call(
        functools.partial(route_kernel, outer),
        in_specs=[WHOLE] * 4,
        out_specs=[SCALARS] + [WHOLE] * outer,
        out_shape=[jax.ShapeDtypeStruct((outer * 4 + 4,), jnp.int32)]
        + [pltpu.VMEM((256, width), jnp.bfloat16)] * outer,
        scratch_shapes=[
            pltpu.VMEM((32, 128), jnp.int32),
            pltpu.SMEM((32, 128), jnp.int32),
            pltpu.VMEM((1024, width), jnp.bfloat16),
            pltpu.SemaphoreType.DMA(()),
        ],
        compiler_params=params(),
        cost_estimate=cost(1024, 1024),
        name="route",
    )(*[near(x) for x in parcels])
    return results[0], results[1:]


def repeat_kernel(outer, table, *refs):
    parcels, picks, planes = refs[:4], refs[4:-1], refs[-1]
    copy_picks(outer, table, parcels, picks, planes)
    total = sum(read_extra(ref) for ref in parcels)
    for ref in picks:
        write_exact(total, ref)


def repeat_route(table, parcels, outer):
    width = parcels[0].shape[1]
    return pl.pallas_call(
        functools.partial(repeat_kernel, outer),
        in_specs=[SCALARS] + [WHOLE] * 4,
        out_specs=[WHOLE] * outer,
        out_shape=[pltpu.VMEM((256 + EXTRA, width), jnp.bfloat16)] * outer,
        scratch_shapes=[pltpu.VMEM((1024, width), jnp.bfloat16)],
        compiler_params=params(),
        cost_estimate=cost(1024, 1024),
        name="repeat_route",
    )(table, *[near(x) for x in parcels])


def chosen(table, slot, arrived):
    rows = slice(64 * slot, 64 * slot + 64)
    plane = jnp.zeros((64, arrived[0].shape[1]), jnp.float32)
    for steps, ref in enumerate(arrived):
        plane = jnp.where(table[4 * len(arrived) + slot] == steps, ref[rows, :].astype(jnp.float32), plane)
    return plane


def forward_kernel(rows, mask, weight, bias, slopes, out, grad, edge, bias_sum, cols, pre):
    width = rows.shape[1]
    valid = windows((128, width), 0)
    for z in range(8):
        span = slice(128 * z, 128 * z + 128)
        for place, moved in enumerate(shifts(rows[span, :].astype(jnp.float32), 0, valid)):
            cols[span, place * width : (place + 1) * width] = moved

    def taps(a):
        return weight[9 * a : 9 * a + 9].reshape(9 * width, width)

    pre[...] = jnp.dot(cols[...], taps(1), preferred_element_type=jnp.float32) + bias[...]
    pre[128:, :] += jnp.dot(cols[:896, :], taps(0), preferred_element_type=jnp.float32)
    pre[:896, :] += jnp.dot(cols[128:, :], taps(2), preferred_element_type=jnp.float32)
    for side in range(2):
        edge[side] = pre[896 * side : 896 * side + 128, :]
    total = jnp.zeros((1, width), jnp.float32)
    for z in range(1, 7):
        span = slice(128 * z, 128 * z + 128)
        act, slope = activate(pre[span, :], both(slopes, z).astype(jnp.float32), wide(mask[span, :]))
        for b in range(2):
            out[b, z] = act[64 * b : 64 * b + 64]
        grad[128 * (z - 1) : 128 * z, :] = slope
        total += jnp.sum(slope.astype(jnp.float32), axis=0, keepdims=True)
    bias_sum[...] = total


def forward_inside(rows, mask, weight, bias, cotangent):
    width = rows.shape[1]
    return pl.pallas_call(
        forward_kernel,
        in_specs=[WHOLE] * 5,
        out_specs=(WHOLE,) * 4,
        out_shape=(
            jax.ShapeDtypeStruct(cotangent.shape, jnp.bfloat16),
            pltpu.VMEM((768, width), jnp.bfloat16),
            pltpu.VMEM((2, 128, width), jnp.float32),
            pltpu.VMEM((1, width), jnp.float32),
        ),
        scratch_shapes=[
            pltpu.VMEM((1024, 9 * width), jnp.bfloat16),
            pltpu.VMEM((1024, width), jnp.float32),
        ],
        compiler_params=params(12),
        cost_estimate=cost(1024, 1024),
        name="forward_inside",
    )(near(rows), near(mask), near(weight), bias, near(cotangent))


def inner_terms_kernel(mine, theirs, grad, their_grad, terms):
    rows = mine.shape[0]
    for a in range(3):
        lanes = slice(128 * a, 128 * a + 768)
        terms[a * rows : (a + 1) * rows, :] = jnp.dot(
            mine[:, lanes], grad[...], preferred_element_type=jnp.float32
        ) + jnp.dot(theirs[:, lanes], their_grad[...], preferred_element_type=jnp.float32)


def inner_terms(mine, theirs, grad, their_grad):
    rows, width = mine.shape[0], grad.shape[1]
    return pl.pallas_call(
        inner_terms_kernel,
        in_specs=[WHOLE] * 4,
        out_specs=WHOLE,
        out_shape=pltpu.VMEM((3 * rows, width), jnp.float32),
        compiler_params=params(10),
        cost_estimate=cost(1024, 1024),
        name="inner_terms",
    )(near(mine), near(theirs), near(grad), near(their_grad))


def edge_kernel(table, mask, weight, edge, ends, inner, out_in, *refs):
    arrived, (out, parcel, own, give, planes, done) = refs[:-6], refs[-6:]
    width = edge.shape[2]
    half = width // 2
    valid = windows((128, width), 0)
    total = inner[...]
    for side in range(2):
        rows = slice(128 * side, 128 * side + 128)
        halo = jnp.concatenate([chosen(table, 2 * side + b, arrived) for b in range(2)], axis=0)
        first = lax.axis_index("zslab") % 2 == 0
        own[rows, :] = jnp.where(first, halo[:, :half], halo[:, half:]).astype(jnp.bfloat16)
        give[rows, :] = jnp.where(first, halo[:, half:], halo[:, :half]).astype(jnp.bfloat16)
        cols = jnp.concatenate(shifts(halo, 0, valid), axis=1)
        taps = weight[18 * side : 18 * side + 9].reshape(9 * width, width)
        pre = edge[side] + jnp.dot(cols, taps, preferred_element_type=jnp.float32)
        z = 7 * side
        keep = wide(mask[128 * z : 128 * z + 128, :])
        act, slope = activate(pre, both(ends, z).astype(jnp.float32), keep)
        for b in range(2):
            planes[side, b, 0] = act[64 * b : 64 * b + 64]
        pltpu.make_async_copy(planes.at[side], out.at[:, pl.ds(z, 1)], done.at[side]).start()
        parcel[rows, :] = slope
        total += jnp.sum(slope.astype(jnp.float32), axis=0, keepdims=True)
    write_exact(total, parcel)
    for side in range(2):
        pltpu.make_async_copy(planes.at[side], out.at[:, pl.ds(7 * side, 1)], done.at[side]).wait()


def forward_edges(table, mask, weight, edge, ends, inner, out, arrived):
    width = edge.shape[2]
    return pl.pallas_call(
        edge_kernel,
        in_specs=[SCALARS] + [WHOLE] * 5 + [FAR] + [WHOLE] * len(arrived),
        out_specs=(FAR, WHOLE, WHOLE, WHOLE),
        out_shape=(
            jax.ShapeDtypeStruct(out.shape, out.dtype),
            pltpu.VMEM((256 + EXTRA, width), jnp.bfloat16),
            pltpu.VMEM((256, width // 2), jnp.bfloat16),
            pltpu.VMEM((256, width // 2), jnp.bfloat16),
        ),
        scratch_shapes=[pltpu.VMEM((2, 2, 1, 64, width), jnp.bfloat16), pltpu.SemaphoreType.DMA((2,))],
        input_output_aliases={6: 0},
        compiler_params=params(),
        cost_estimate=cost(1024, 1024),
        name="forward_edges",
    )(
        table,
        near(mask),
        near(weight),
        near(edge),
        near(ends),
        near(inner),
        out,
        *[near(x) for x in arrived],
    )


def outer_terms_kernel(taps, size, mine, theirs, halos, their_halos, parcel, their_parcel, inner, give, stay, cols, total):
    half = mine.shape[0] // 9
    piece = half // 2
    valid = windows((half, 128), 1)
    facing = jnp.concatenate([parcel[:128], their_parcel[:128], parcel[128:256], their_parcel[128:256]], axis=0)
    for a in range(3):
        first, last = max(taps[0], 9 * a), min(taps[1], 9 * a + 9)
        if first >= last:
            continue
        low, high = (first - 9 * a) * half, (last - 9 * a) * half
        for place, (ref, ends) in enumerate(((mine, halos), (theirs, their_halos), (mine, halos), (theirs, their_halos))):
            side = place // 2
            plane = a - 1 + 7 * side
            lanes = slice(128 * place, 128 * place + 128)
            if 0 <= plane < 8:
                cols[low:high, lanes] = ref[low:high, 128 * plane : 128 * plane + 128]
            else:
                moved = shifts(ends[128 * side : 128 * side + 128, :].astype(jnp.float32).T, 1, valid)
                for at in range(first - 9 * a, last - 9 * a):
                    cols[at * half : (at + 1) * half, lanes] = moved[at]
        start = (first - taps[0]) * half
        total[start : start + high - low, :] = inner[first * half : last * half, :] + jnp.dot(
            cols[low:high, :], facing, preferred_element_type=jnp.float32
        )
    upper = stage_half(size, 0)
    for tap in range(taps[1] - taps[0]):
        rows = slice(piece * tap, piece * tap + piece)
        other = pl.ds(pl.multiple_of(half * tap + (1 - upper) * piece, 16), piece)
        own = pl.ds(pl.multiple_of(half * tap + upper * piece, 16), piece)
        give[rows, :] = total[other, :].astype(jnp.bfloat16)
        stay[rows, :] = total[own, :]


def outer_terms(taps, size, mine, theirs, halos, their_halos, parcel, their_parcel, inner):
    width = inner.shape[1]
    half = mine.shape[0] // 9
    count = taps[1] - taps[0]
    rows = count * half // 2
    return pl.pallas_call(
        functools.partial(outer_terms_kernel, taps, size),
        in_specs=[WHOLE] * 7,
        out_specs=(WHOLE, WHOLE),
        out_shape=(pltpu.VMEM((rows, width), jnp.bfloat16), pltpu.VMEM((rows, width), jnp.float32)),
        scratch_shapes=[
            pltpu.VMEM((9 * half, 512), jnp.bfloat16),
            pltpu.VMEM((count * half, width), jnp.float32),
        ],
        compiler_params=params(8),
        cost_estimate=cost(1024, 1024),
        name="outer_terms",
    )(*[near(x) for x in (mine, theirs, halos, their_halos, parcel, their_parcel, inner)])


def backward_rows(planes, mask, weight, cols, place, await_weight=None):
    width = weight.shape[1]
    valid = windows((128, width), 0)
    for index, plane in enumerate(planes):
        rows = slice(128 * (place + index), 128 * (place + index) + 128)
        for at, moved in enumerate(shifts(plane.astype(jnp.float32), 0, valid, -1)):
            cols[rows, at * width : (at + 1) * width] = moved
    if await_weight:
        await_weight()
    count = 128 * (len(planes) - 2)
    total = jnp.zeros((count, width), jnp.float32)
    for a in range(3):
        for at in range(9):
            start = 128 * (place + 2 - a)
            total += lax.dot_general(
                cols[start : start + count, at * width : (at + 1) * width],
                weight[9 * a + at],
                (((1,), (1,)), ((), ())),
                preferred_element_type=jnp.float32,
            )
    return jnp.where(wide(mask), total, 0.0).astype(jnp.bfloat16)


def backward_inner_kernel(grad, mask, weight, grad_feats, cols):
    planes = [grad[128 * (z - 1) : 128 * z, :] for z in range(1, 7)]
    done = backward_rows(planes, mask[256:768, :], weight, cols, 0)
    for z in range(2, 6):
        for b in range(2):
            start = 128 * (z - 2) + 64 * b
            grad_feats[b, z] = done[start : start + 64]


def backward_inner(grad, mask, weight):
    width = grad.shape[1]
    return pl.pallas_call(
        backward_inner_kernel,
        in_specs=[WHOLE] * 3,
        out_specs=WHOLE,
        out_shape=jax.ShapeDtypeStruct((2, 8, 64, width), jnp.bfloat16),
        scratch_shapes=[pltpu.VMEM((768, 9 * width), jnp.bfloat16)],
        compiler_params=params(10),
        cost_estimate=cost(1024, 1024),
        name="backward_inner",
    )(near(grad), near(mask), near(weight))


def backward_outer_kernel(table, grad, parcel, mask, weight, done, *refs):
    arrived, (grad_feats, bias_sum, cols, planes, near_weight, fetched, sent) = refs[:-7], refs[-7:]
    fetch_taps(weight, near_weight, fetched)
    for side in range(2):
        halo = jnp.concatenate([chosen(table, 2 * side + b, arrived) for b in range(2)], axis=0)
        rim = parcel[128 * side : 128 * side + 128, :]
        if side == 0:
            around = [halo, rim, grad[:128, :], grad[128:256, :]]
        else:
            around = [grad[512:640, :], grad[640:768, :], rim, halo]
        first = 6 * side
        await_now = (lambda: await_taps(0, weight.shape[0], weight, near_weight, fetched)) if side == 0 else None
        keep = mask[128 * first : 128 * first + 256, :]
        rows = backward_rows(around, keep, near_weight, cols, 4 * side, await_now)
        for z in range(2):
            for b in range(2):
                start = 128 * z + 64 * b
                planes[side, b, z] = rows[start : start + 64]
        pltpu.make_async_copy(planes.at[side], grad_feats.at[:, pl.ds(first, 2)], sent.at[side]).start()
    bias_sum[...] = sum(read_extra(ref) for ref in arrived)
    for side in range(2):
        pltpu.make_async_copy(planes.at[side], grad_feats.at[:, pl.ds(6 * side, 2)], sent.at[side]).wait()


def backward_outer(table, grad, parcel, mask, weight, done, arrived):
    width = grad.shape[1]
    return pl.pallas_call(
        backward_outer_kernel,
        in_specs=[SCALARS] + [WHOLE] * 3 + [FAR, FAR] + [WHOLE] * len(arrived),
        out_specs=(FAR, WHOLE),
        out_shape=(jax.ShapeDtypeStruct(done.shape, done.dtype), jax.ShapeDtypeStruct((1, width), jnp.float32)),
        scratch_shapes=[
            pltpu.VMEM((1024, 9 * width), jnp.bfloat16),
            pltpu.VMEM((2, 2, 2, 64, width), jnp.bfloat16),
            pltpu.VMEM(weight.shape, jnp.bfloat16),
            pltpu.SemaphoreType.DMA((weight.shape[0],)),
            pltpu.SemaphoreType.DMA((2,)),
        ],
        input_output_aliases={5: 0},
        compiler_params=params(12),
        cost_estimate=cost(1024, 1024),
        name="backward_outer",
    )(table, near(grad), near(parcel), near(mask), far(weight), done, *[near(x) for x in arrived])


def assemble_kernel(first, size, *refs):
    parts, (out, done) = refs[:4], refs[-2:]
    count = parts[0].shape[0]
    core = lax.axis_index("zslab") % 2
    mine = stage_half(size, 0)
    places = (2 * core + mine, 2 * core + 1 - mine, 2 - 2 * core + mine, 3 - 2 * core - mine)
    copies = [
        pltpu.make_async_copy(ref, out.at[pl.ds(first, count), place], done.at[index])
        for index, (ref, place) in enumerate(zip(parts, places))
    ]
    for copy in copies:
        copy.start()
    for copy in copies:
        copy.wait()


def assemble(first, size, parts, shape, done):
    given = [] if done is None else [done]
    return pl.pallas_call(
        functools.partial(assemble_kernel, first, size),
        in_specs=[WHOLE] * 4 + [FAR] * len(given),
        out_specs=FAR,
        out_shape=jax.ShapeDtypeStruct(shape, jnp.bfloat16),
        scratch_shapes=[pltpu.SemaphoreType.DMA((4,))],
        input_output_aliases={4: 0} if given else {},
        compiler_params=params(),
        cost_estimate=cost(1024, 1024),
        name="assemble",
    )(*[near(x) for x in parts], *given)


def gather_group(parcel, size, before=()):
    inner, *before = lax.optimization_barrier((swap(parcel, size, 2), *before))
    return [parcel, inner, swap(parcel, size, 1), swap(inner, size, 1)], *before


def per_device(size, feats, voxmask, links, weight, bias, cotangent):
    width = feats.shape[3]
    outer = size // 4

    mask, rows, give, turned, taps, ends = prepare(feats, voxmask, weight, cotangent)
    parcels, rows = gather_group(rims(links, feats, voxmask), size, (rows,))
    out, grad, edge, bias_local = forward_inside(rows, mask, taps, bias.reshape(1, width), ends)
    *parcels, grad = lax.optimization_barrier((*parcels, grad))
    table, picks = route(parcels, outer)

    *picks, give = lax.optimization_barrier((*picks, give))
    arrived = [rotate(pick, size, steps) if steps else pick for steps, pick in enumerate(picks)]
    their_turned = turn(swap(give, size, 1))
    inner = inner_terms(turned, their_turned, grad, swap(grad, size, 1))

    grad_feats = backward_inner(grad, mask, taps)
    *arrived, inner, grad_feats = lax.optimization_barrier((*arrived, inner, grad_feats))
    out, parcel, halos, give = forward_edges(table, mask, taps, edge, ends, bias_local, out, arrived)
    their_halos = swap(give, size, 1)
    parcels, halos = gather_group(parcel, size, (halos,))

    stages = stage_count(size)
    halves = [stage_half(size, stage) for stage in range(stages)]
    count = weight.shape[0]
    cuts = [(count * k // 3, count * (k + 1) // 3) for k in range(3)]
    sums = []
    for cut in cuts:
        give, stay = outer_terms(cut, size, turned, their_turned, halos, their_halos, parcel, parcels[2], inner)
        if len(sums) == 2:
            arrived_first, give = lax.optimization_barrier((sums[0][1], give))
            sums[0] = (sums[0][0], arrived_first)
        sums.append((stay, swap_stage(give, size, 0)))

    picks = repeat_route(table, parcels, outer)
    (stay, got), *others = sums
    stay, *picks = lax.optimization_barrier((stay, *picks))
    sums = [(stay, got), *others]
    arrived = [rotate(pick, size, steps) if steps else pick for steps, pick in enumerate(picks)]
    for stage in range(1, stages):
        for index, (stay, got) in enumerate(sums):
            give, stay = halve(stay, got, halves[stage])
            sums[index] = (stay, swap_stage(give, size, stage))
    parts = [(stay + got.astype(jnp.float32)).astype(jnp.bfloat16) for stay, got in sums]
    parts[0], *arrived = lax.optimization_barrier((parts[0], *arrived))
    grad_feats, grad_bias = backward_outer(table, grad, parcel, mask, weight, grad_feats, arrived)
    for stage in reversed(range(1, stages)):
        gathered = [swap_stage(part, size, stage) for part in parts]
        if stage == 1:
            gathered[0], grad_feats, grad_bias = lax.optimization_barrier((gathered[0], grad_feats, grad_bias))
        parts = [join(part, got, halves[stage]) for part, got in zip(parts, gathered)]

    grad_weight = None
    for cut, part in zip(cuts, parts):
        last = swap_stage(part, size, 0)
        other = swap(part, size, 1)
        pieces = [x.reshape(cut[1] - cut[0], width // 4, width) for x in (part, last, other, swap(last, size, 1))]
        grad_weight = assemble(cut[0], size, pieces, (count, 4, width // 4, width), grad_weight)
    return out, grad_feats, grad_weight.reshape(count, width, width), grad_bias.reshape(width)


def solution(mesh):
    return jax.shard_map(
        functools.partial(per_device, mesh.shape["zslab"]),
        mesh=mesh,
        in_specs=(
            P(("groups", "zslab"), None, None, None),
            P(("groups", "zslab"), None),
            P(("groups", "zslab"), None),
            P(),
            P(),
            P(("groups", "zslab"), None, None, None),
        ),
        out_specs=(
            P(("groups", "zslab"), None, None, None),
            P(("groups", "zslab"), None, None, None),
            P("groups", None, None),
            P("groups"),
        ),
        check_vma=False,
    )
```

```python
import functools

import jax
import jax.numpy as jnp
from jax import lax
from jax.experimental import pallas as pl
from jax.experimental.pallas import tpu as pltpu
from jax.sharding import PartitionSpec as P

EXTRA = 16


def params(mebibytes=6):
    return pltpu.CompilerParams(vmem_limit_bytes=mebibytes * 1024 * 1024)


def cost(flops, bytes_accessed):
    return pl.CostEstimate(flops=flops, bytes_accessed=bytes_accessed, transcendentals=0)


def near(x):
    return pltpu.with_memory_space_constraint(x, pltpu.VMEM)


def far(x):
    return pltpu.with_memory_space_constraint(x, pltpu.HBM)


SCALARS = pl.BlockSpec(memory_space=pltpu.SMEM)
WHOLE = pl.BlockSpec(memory_space=pltpu.VMEM)
FAR = pl.BlockSpec(memory_space=pl.ANY)


def swap(x, size, bit):
    return lax.ppermute(x, "zslab", [(i, i ^ bit) for i in range(size)])


def rotate(x, size, steps):
    return lax.ppermute(x, "zslab", [(i, (i + 4 * steps) % size) for i in range(size)])


def me():
    return lax.axis_index("zslab")


def units(outer):
    return -(-108 // outer)


def mask_rows(voxmask, z):
    lanes = slice(64 * z, 64 * z + 64)
    line = jnp.concatenate([voxmask[0:1, lanes], voxmask[1:2, lanes]], axis=1)
    return jnp.broadcast_to((line == 1).astype(jnp.float32), (128, 128)).T


def wide(mask):
    return jnp.concatenate([mask, mask], axis=1) > 0


def both(ref, z):
    return jnp.concatenate([ref[0, z], ref[1, z]], axis=0)


def inside(shape, dim, rows, cols):
    index = lax.broadcasted_iota(jnp.int32, shape, dim)
    row = (index // 8) % 8 + rows
    col = index % 8 + cols
    return (row >= 0) & (row < 8) & (col >= 0) & (col < 8)


def windows(shape, dim):
    return [inside(shape, dim, p, q) for p in (-1, 0, 1) for q in (-1, 0, 1)]


def shifts(x, dim, valid, sign=1):
    count = x.shape[dim]
    moved = []
    for place in range(9):
        at = place if sign == 1 else 8 - place
        move = 8 * (at // 3 - 1) + at % 3 - 1
        turned = pltpu.roll(x, (-move) % count, dim) if move else x
        moved.append(jnp.where(valid[at], turned, 0.0).astype(jnp.bfloat16))
    return moved


def activate(pre, cotangent, keep):
    sigma = 1.0 / (1.0 + jnp.exp(-pre))
    out = jnp.where(keep, pre * sigma, 0.0)
    grad = jnp.where(keep, cotangent * sigma * (1.0 + pre * (1.0 - sigma)), 0.0)
    return out.astype(jnp.bfloat16), grad.astype(jnp.bfloat16)


def write_exact(rows, ref):
    high = rows.astype(jnp.bfloat16)
    left = rows - high.astype(jnp.float32)
    middle = left.astype(jnp.bfloat16)
    low = (left - middle.astype(jnp.float32)).astype(jnp.bfloat16)
    zeros = jnp.zeros((EXTRA - 3, rows.shape[1]), jnp.float32)
    terms = [term.astype(jnp.float32) for term in (high, middle, low)]
    ref[256:272, :] = jnp.concatenate(terms + [zeros], axis=0).astype(jnp.bfloat16)


def read_extra(ref):
    return jnp.sum(ref[256:272, :].astype(jnp.float32), axis=0, keepdims=True)


def rims_kernel(links, feats, voxmask, parcel, planes, masks, codes, done):
    width = feats.shape[3]
    copies = [
        pltpu.make_async_copy(feats.at[:, pl.ds(0, 1)], planes.at[0], done.at[0]),
        pltpu.make_async_copy(feats.at[:, pl.ds(7, 1)], planes.at[1], done.at[1]),
        pltpu.make_async_copy(voxmask, masks, done.at[2]),
        pltpu.make_async_copy(links, codes, done.at[3]),
    ]
    for copy in copies:
        copy.start()
    for copy in copies:
        copy.wait()
    for side in range(2):
        keep = wide(mask_rows(masks, 7 * side))
        plane = jnp.concatenate([planes[side, 0, 0], planes[side, 1, 0]], axis=0).astype(jnp.float32)
        parcel[128 * side : 128 * side + 128, :] = jnp.where(keep, plane, 0.0).astype(jnp.bfloat16)
    lane = lax.broadcasted_iota(jnp.int32, (EXTRA, width), 1)
    row = jnp.zeros((EXTRA, width), jnp.float32)
    for place in range(4):
        row = jnp.where(lane == place, codes[place // 2, place % 2].astype(jnp.float32), row)
    parcel[256:272, :] = row.astype(jnp.bfloat16)


def rims(links, feats, voxmask):
    width = feats.shape[3]
    return pl.pallas_call(
        rims_kernel,
        in_specs=[FAR] * 3,
        out_specs=WHOLE,
        out_shape=pltpu.VMEM((256 + EXTRA, width), jnp.bfloat16),
        scratch_shapes=[
            pltpu.VMEM((2, 2, 1, 64, width), jnp.bfloat16),
            pltpu.VMEM(voxmask.shape, jnp.int32),
            pltpu.SMEM(links.shape, jnp.int32),
            pltpu.SemaphoreType.DMA((4,)),
        ],
        compiler_params=params(),
        cost_estimate=cost(1024, 1024),
        name="rims",
    )(far(links), far(feats), far(voxmask))


def fetch_taps(weight, near_weight, done):
    for tap in range(weight.shape[0]):
        pltpu.make_async_copy(weight.at[tap], near_weight.at[tap], done.at[tap]).start()


def await_taps(first, last, weight, near_weight, done):
    for tap in range(first, last):
        pltpu.make_async_copy(weight.at[tap], near_weight.at[tap], done.at[tap]).wait()


def aligned(index, rows):
    return pl.ds(pl.multiple_of(index * rows, rows), rows)


def quarters(flip, own, give_inner, give_core):
    position = me() % 4
    rows = flip.shape[0] // 4
    if own is not None:
        own[...] = flip[aligned(position, rows), :].astype(own.dtype)
    give_inner[...] = flip[aligned(1 - position // 2, 2 * rows), :].astype(jnp.bfloat16)
    give_core[...] = flip[aligned(position // 2 * 2 + 1 - position % 2, rows), :].astype(jnp.bfloat16)


def turn_rows(flip, lanes, valid, turned, first):
    rows = flip.shape[0]
    for place, moved in enumerate(shifts(flip[:, lanes].astype(jnp.float32), 1, valid)):
        turned[first + place * rows : first + (place + 1) * rows, lanes] = moved


def prepare_kernel(
    feats, voxmask, weight, cotangent, mask, rows, give_inner, give_core, turned, taps, slopes, planes, masks, flip, own, done, fetched
):
    count = weight.shape[0]
    pltpu.make_async_copy(voxmask, masks, done.at[8]).start()
    for z in range(8):
        pltpu.make_async_copy(feats.at[:, pl.ds(z, 1)], planes.at[:, pl.ds(z, 1)], done.at[z]).start()
    fetch_taps(weight, taps, fetched)
    for z in range(8):
        pltpu.make_async_copy(cotangent.at[:, pl.ds(z, 1)], slopes.at[:, pl.ds(z, 1)], fetched.at[count + z]).start()
    valid = windows((own.shape[0], 128), 1)
    pltpu.make_async_copy(voxmask, masks, done.at[8]).wait()
    for z in range(8):
        pltpu.make_async_copy(feats.at[:, pl.ds(z, 1)], planes.at[:, pl.ds(z, 1)], done.at[z]).wait()
        span = slice(128 * z, 128 * z + 128)
        keep = mask_rows(masks, z)
        mask[span, :] = keep
        plane = jnp.where(wide(keep), both(planes, z).astype(jnp.float32), 0.0)
        rows[span, :] = plane.astype(jnp.bfloat16)
        flip[:, span] = plane.T
    quarters(flip, own, give_inner, give_core)
    for z in range(8):
        turn_rows(own, slice(128 * z, 128 * z + 128), valid, turned, 0)
    await_taps(0, count, weight, taps, fetched)
    for z in range(8):
        pltpu.make_async_copy(cotangent.at[:, pl.ds(z, 1)], slopes.at[:, pl.ds(z, 1)], fetched.at[count + z]).wait()


def prepare(feats, voxmask, weight, cotangent):
    width = feats.shape[3]
    quarter = width // 4
    return pl.pallas_call(
        prepare_kernel,
        in_specs=[FAR] * 4,
        out_specs=(WHOLE,) * 7,
        out_shape=(
            pltpu.VMEM((1024, 128), jnp.float32),
            pltpu.VMEM((1024, width), jnp.bfloat16),
            pltpu.VMEM((2 * quarter, 1024), jnp.bfloat16),
            pltpu.VMEM((quarter, 1024), jnp.bfloat16),
            pltpu.VMEM((9 * quarter, 1024), jnp.bfloat16),
            pltpu.VMEM(weight.shape, jnp.bfloat16),
            pltpu.VMEM(cotangent.shape, jnp.bfloat16),
        ),
        scratch_shapes=[
            pltpu.VMEM(feats.shape, jnp.bfloat16),
            pltpu.VMEM(voxmask.shape, jnp.int32),
            pltpu.VMEM((width, 1024), jnp.float32),
            pltpu.VMEM((quarter, 1024), jnp.float32),
            pltpu.SemaphoreType.DMA((9,)),
            pltpu.SemaphoreType.DMA((weight.shape[0] + 8,)),
        ],
        compiler_params=params(12),
        cost_estimate=cost(1024, 1024),
        name="prepare",
    )(far(feats), far(voxmask), far(weight), far(cotangent))


def turn_kernel(inner, core, both_changed, turned):
    quarter = core.shape[0]
    valid = windows((quarter, 128), 1)
    mine = aligned(me() % 2, quarter)
    for z in range(8):
        lanes = slice(128 * z, 128 * z + 128)
        for index, rows in enumerate((inner[mine, lanes], core[:, lanes], both_changed[mine, lanes])):
            first = 9 * quarter * index
            for place, moved in enumerate(shifts(rows.astype(jnp.float32), 1, valid)):
                turned[first + place * quarter : first + (place + 1) * quarter, lanes] = moved


def turn(inner, core, both_changed):
    quarter = core.shape[0]
    return pl.pallas_call(
        turn_kernel,
        in_specs=[WHOLE] * 3,
        out_specs=WHOLE,
        out_shape=pltpu.VMEM((27 * quarter, 1024), jnp.bfloat16),
        compiler_params=params(10),
        cost_estimate=cost(1024, 1024),
        name="turn",
    )(near(inner), near(core), near(both_changed))


def copy_picks(outer, table, parcels, picks, planes):
    for dev in range(4):
        planes[256 * dev : 256 * dev + 256, :] = parcels[dev][:256, :]
    for steps in range(outer):
        for slot in range(4):
            start = pl.multiple_of(table[steps * 4 + slot] * 64, 64)
            picks[steps][64 * slot : 64 * slot + 64, :] = planes[pl.ds(start, 64), :]


def route_kernel(outer, *refs):
    position = me()
    parcels, (table, *picks), (codes, links, planes, done) = refs[:4], refs[4:-4], refs[-4:]
    for dev in range(4):
        row = parcels[dev][256:272, :128].astype(jnp.float32)
        codes[8 * dev : 8 * dev + 8, :] = row[:8, :].astype(jnp.int32)
    copy = pltpu.make_async_copy(codes, links, done)
    copy.start()
    copy.wait()
    for place in range(outer * 4):
        table[place] = 0
    for plane in range(16):
        dev, side, brick = plane // 4, plane // 2 % 2, plane % 2
        dest = links[dev * 8, brick * 2 + side]

        @pl.when((dest >= 0) & ((dest // 2) % 4 == position % 4))
        def _():
            steps = lax.rem(dest // 8 - position // 4 + outer, outer)
            table[steps * 4 + dest % 2 + (0 if side == 1 else 2)] = plane

    for brick in range(2):
        for side in range(2):
            dest = links[0, brick * 2 + side]
            steps = lax.rem(position // 4 - dest // 8 + outer, outer)
            table[outer * 4 + 2 * side + brick] = jnp.where(dest >= 0, steps, -1)

    copy_picks(outer, table, parcels, picks, planes)


def route(parcels, outer):
    width = parcels[0].shape[1]
    results = pl.pallas_call(
        functools.partial(route_kernel, outer),
        in_specs=[WHOLE] * 4,
        out_specs=[SCALARS] + [WHOLE] * outer,
        out_shape=[jax.ShapeDtypeStruct((outer * 4 + 4,), jnp.int32)]
        + [pltpu.VMEM((256, width), jnp.bfloat16)] * outer,
        scratch_shapes=[
            pltpu.VMEM((32, 128), jnp.int32),
            pltpu.SMEM((32, 128), jnp.int32),
            pltpu.VMEM((1024, width), jnp.bfloat16),
            pltpu.SemaphoreType.DMA(()),
        ],
        compiler_params=params(),
        cost_estimate=cost(1024, 1024),
        name="route",
    )(*[near(x) for x in parcels])
    return results[0], results[1:]


def repeat_kernel(outer, table, *refs):
    parcels, picks, planes = refs[:4], refs[4:-1], refs[-1]
    copy_picks(outer, table, parcels, picks, planes)
    total = sum(read_extra(ref) for ref in parcels)
    for ref in picks:
        write_exact(total, ref)


def repeat_route(table, parcels, outer):
    width = parcels[0].shape[1]
    return pl.pallas_call(
        functools.partial(repeat_kernel, outer),
        in_specs=[SCALARS] + [WHOLE] * 4,
        out_specs=[WHOLE] * outer,
        out_shape=[pltpu.VMEM((256 + EXTRA, width), jnp.bfloat16)] * outer,
        scratch_shapes=[pltpu.VMEM((1024, width), jnp.bfloat16)],
        compiler_params=params(),
        cost_estimate=cost(1024, 1024),
        name="repeat_route",
    )(table, *[near(x) for x in parcels])


def chosen(table, slot, arrived):
    rows = slice(64 * slot, 64 * slot + 64)
    plane = jnp.zeros((64, arrived[0].shape[1]), jnp.float32)
    for steps, ref in enumerate(arrived):
        plane = jnp.where(table[4 * len(arrived) + slot] == steps, ref[rows, :].astype(jnp.float32), plane)
    return plane


def forward_kernel(rows, mask, weight, bias, slopes, out, grad, edge, bias_sum, cols, pre):
    width = rows.shape[1]
    valid = windows((128, width), 0)
    for z in range(8):
        span = slice(128 * z, 128 * z + 128)
        for place, moved in enumerate(shifts(rows[span, :].astype(jnp.float32), 0, valid)):
            cols[span, place * width : (place + 1) * width] = moved

    def taps(a):
        return weight[9 * a : 9 * a + 9].reshape(9 * width, width)

    pre[...] = jnp.dot(cols[...], taps(1), preferred_element_type=jnp.float32) + bias[...]
    pre[128:, :] += jnp.dot(cols[:896, :], taps(0), preferred_element_type=jnp.float32)
    pre[:896, :] += jnp.dot(cols[128:, :], taps(2), preferred_element_type=jnp.float32)
    for side in range(2):
        edge[side] = pre[896 * side : 896 * side + 128, :]
    total = jnp.zeros((1, width), jnp.float32)
    for z in range(1, 7):
        span = slice(128 * z, 128 * z + 128)
        act, slope = activate(pre[span, :], both(slopes, z).astype(jnp.float32), wide(mask[span, :]))
        for b in range(2):
            out[b, z] = act[64 * b : 64 * b + 64]
        grad[128 * (z - 1) : 128 * z, :] = slope
        total += jnp.sum(slope.astype(jnp.float32), axis=0, keepdims=True)
    bias_sum[...] = total


def forward_inside(rows, mask, weight, bias, cotangent):
    width = rows.shape[1]
    return pl.pallas_call(
        forward_kernel,
        in_specs=[WHOLE] * 5,
        out_specs=(WHOLE,) * 4,
        out_shape=(
            jax.ShapeDtypeStruct(cotangent.shape, jnp.bfloat16),
            pltpu.VMEM((768, width), jnp.bfloat16),
            pltpu.VMEM((2, 128, width), jnp.float32),
            pltpu.VMEM((1, width), jnp.float32),
        ),
        scratch_shapes=[
            pltpu.VMEM((1024, 9 * width), jnp.bfloat16),
            pltpu.VMEM((1024, width), jnp.float32),
        ],
        compiler_params=params(12),
        cost_estimate=cost(1024, 1024),
        name="forward_inside",
    )(near(rows), near(mask), near(weight), bias, near(cotangent))


def inner_terms_kernel(mine, others, *refs):
    grads, terms = refs[:4], refs[4]
    rows = mine.shape[0]
    for a in range(3):
        lanes = slice(128 * a, 128 * a + 768)
        total = jnp.dot(mine[:, lanes], grads[0][...], preferred_element_type=jnp.float32)
        for index in range(3):
            total += jnp.dot(
                others[index * rows : (index + 1) * rows, lanes], grads[index + 1][...], preferred_element_type=jnp.float32
            )
        terms[a * rows : (a + 1) * rows, :] = total


def inner_terms(mine, others, grads):
    rows, width = mine.shape[0], grads[0].shape[1]
    return pl.pallas_call(
        inner_terms_kernel,
        in_specs=[WHOLE] * 6,
        out_specs=WHOLE,
        out_shape=pltpu.VMEM((3 * rows, width), jnp.float32),
        compiler_params=params(10),
        cost_estimate=cost(1024, 1024),
        name="inner_terms",
    )(near(mine), near(others), *[near(x) for x in grads])


def edge_kernel(table, mask, weight, edge, ends, inner, out_in, *refs):
    arrived, (out, to_inner, to_core, own, planes, flip, done) = refs[:-7], refs[-7:]
    width = edge.shape[2]
    valid = windows((128, width), 0)
    total = inner[...]
    for side in range(2):
        rows = slice(128 * side, 128 * side + 128)
        halo = jnp.concatenate([chosen(table, 2 * side + b, arrived) for b in range(2)], axis=0)
        flip[:, rows] = halo.T
        cols = jnp.concatenate(shifts(halo, 0, valid), axis=1)
        taps = weight[18 * side : 18 * side + 9].reshape(9 * width, width)
        pre = edge[side] + jnp.dot(cols, taps, preferred_element_type=jnp.float32)
        z = 7 * side
        keep = wide(mask[128 * z : 128 * z + 128, :])
        act, slope = activate(pre, both(ends, z).astype(jnp.float32), keep)
        for b in range(2):
            planes[side, b, 0] = act[64 * b : 64 * b + 64]
        pltpu.make_async_copy(planes.at[side], out.at[:, pl.ds(z, 1)], done.at[side]).start()
        to_inner[rows, :] = slope
        to_core[rows, :] = slope
        total += jnp.sum(slope.astype(jnp.float32), axis=0, keepdims=True)
    write_exact(total, to_inner)
    write_exact(total, to_core)
    quarters(flip, own, to_inner.at[272:], to_core.at[272:])
    for side in range(2):
        pltpu.make_async_copy(planes.at[side], out.at[:, pl.ds(7 * side, 1)], done.at[side]).wait()


def forward_edges(table, mask, weight, edge, ends, inner, out, arrived):
    width = edge.shape[2]
    quarter = width // 4
    return pl.pallas_call(
        edge_kernel,
        in_specs=[SCALARS] + [WHOLE] * 5 + [FAR] + [WHOLE] * len(arrived),
        out_specs=(FAR, WHOLE, WHOLE, WHOLE),
        out_shape=(
            jax.ShapeDtypeStruct(out.shape, out.dtype),
            pltpu.VMEM((256 + EXTRA + 2 * quarter, width), jnp.bfloat16),
            pltpu.VMEM((256 + EXTRA + quarter, width), jnp.bfloat16),
            pltpu.VMEM((quarter, 256), jnp.bfloat16),
        ),
        scratch_shapes=[
            pltpu.VMEM((2, 2, 1, 64, width), jnp.bfloat16),
            pltpu.VMEM((width, 256), jnp.float32),
            pltpu.SemaphoreType.DMA((2,)),
        ],
        input_output_aliases={6: 0},
        compiler_params=params(10),
        cost_estimate=cost(1024, 1024),
        name="forward_edges",
    )(
        table,
        near(mask),
        near(weight),
        near(edge),
        near(ends),
        near(inner),
        out,
        *[near(x) for x in arrived],
    )


def outer_terms_kernel(outer, mine, others, halos, *refs):
    parcels, inner = refs[:4], refs[4]
    gives, stay, cols, total = refs[5 : 4 + outer], refs[4 + outer], refs[5 + outer], refs[6 + outer]
    quarter = halos.shape[0]
    rows = 9 * quarter
    valid = windows((quarter, 128), 1)
    half = aligned(me() % 2, quarter)
    ends = (
        halos,
        parcels[1].at[272 : 272 + 2 * quarter].at[half],
        parcels[2].at[272 : 272 + quarter],
        parcels[3].at[272 : 272 + 2 * quarter].at[half],
    )
    facing = jnp.concatenate(
        [parcel[128 * side : 128 * side + 128, :] for side in range(2) for parcel in parcels], axis=0
    )
    for a in range(3):
        for side in range(2):
            plane = a - 1 + 7 * side
            for who in range(4):
                lanes = slice(128 * (4 * side + who), 128 * (4 * side + who) + 128)
                if 0 <= plane < 8:
                    ref, first = (mine, 0) if who == 0 else (others, rows * (who - 1))
                    cols[:, lanes] = ref[first : first + rows, 128 * plane : 128 * plane + 128]
                else:
                    moved = shifts(ends[who][:, 128 * side : 128 * side + 128].astype(jnp.float32), 1, valid)
                    for place in range(9):
                        cols[place * quarter : (place + 1) * quarter, lanes] = moved[place]
        span = slice(a * rows, (a + 1) * rows)
        total[span, :] = inner[span, :] + jnp.dot(cols[...], facing, preferred_element_type=jnp.float32)
    if total.shape[0] > 3 * rows:
        total[3 * rows :, :] = jnp.zeros((total.shape[0] - 3 * rows, total.shape[1]), jnp.float32)
    z = me() // 4
    for steps in range(outer):
        block = lax.rem(z + steps, outer)
        for unit in range(units(outer)):
            piece = total[aligned(block + outer * unit, 16), :]
            if steps:
                gives[steps - 1][16 * unit : 16 * unit + 16, :] = piece.astype(jnp.bfloat16)
            else:
                stay[16 * unit : 16 * unit + 16, :] = piece


def outer_terms(outer, mine, others, halos, parcels, inner):
    width = inner.shape[1]
    rows = 16 * units(outer)
    results = pl.pallas_call(
        functools.partial(outer_terms_kernel, outer),
        in_specs=[WHOLE] * 8,
        out_specs=[WHOLE] * outer,
        out_shape=[pltpu.VMEM((rows, width), jnp.bfloat16)] * (outer - 1) + [pltpu.VMEM((rows, width), jnp.float32)],
        scratch_shapes=[
            pltpu.VMEM((inner.shape[0] // 3, 1024), jnp.bfloat16),
            pltpu.VMEM((outer * rows, width), jnp.float32),
        ],
        compiler_params=params(12),
        cost_estimate=cost(1024, 1024),
        name="outer_terms",
    )(*[near(x) for x in (mine, others, halos, *parcels, inner)])
    return results[:-1], results[-1]


def backward_kernel(grad, parcel, mask, weight, grad_feats, partial, cols, total, near_weight, fetched):
    width = grad.shape[1]
    fetch_taps(weight, near_weight, fetched)
    valid = windows((128, width), 0)
    planes = [parcel[:128, :]] + [grad[128 * z : 128 * z + 128, :] for z in range(6)] + [parcel[128:256, :]]
    for z, plane in enumerate(planes):
        for at, moved in enumerate(shifts(plane.astype(jnp.float32), 0, valid, -1)):
            cols[128 * z : 128 * z + 128, at * width : (at + 1) * width] = moved
    for a in (1, 0, 2):
        await_taps(9 * a, 9 * a + 9, weight, near_weight, fetched)
        first, start, count = ((128, 0, 896), (0, 0, 1024), (0, 128, 896))[a]
        for at in range(9):
            piece = lax.dot_general(
                cols[first : first + count, at * width : (at + 1) * width],
                near_weight[9 * a + at],
                (((1,), (1,)), ((), ())),
                preferred_element_type=jnp.float32,
            )
            if a == 1 and at == 0:
                total[...] = piece
            else:
                total[start : start + count, :] += piece
    for z in range(1, 7):
        rows = slice(128 * z, 128 * z + 128)
        done = jnp.where(wide(mask[rows, :]), total[rows, :], 0.0).astype(jnp.bfloat16)
        for b in range(2):
            grad_feats[b, z] = done[64 * b : 64 * b + 64]
    for side in range(2):
        partial[side] = total[896 * side : 896 * side + 128, :]


def backward(grad, parcel, mask, weight):
    width = grad.shape[1]
    return pl.pallas_call(
        backward_kernel,
        in_specs=[WHOLE] * 3 + [FAR],
        out_specs=(WHOLE, WHOLE),
        out_shape=(jax.ShapeDtypeStruct((2, 8, 64, width), jnp.bfloat16), pltpu.VMEM((2, 128, width), jnp.float32)),
        scratch_shapes=[
            pltpu.VMEM((1024, 9 * width), jnp.bfloat16),
            pltpu.VMEM((1024, width), jnp.float32),
            pltpu.VMEM(weight.shape, jnp.bfloat16),
            pltpu.SemaphoreType.DMA((weight.shape[0],)),
        ],
        compiler_params=params(16),
        cost_estimate=cost(1024, 1024),
        name="backward",
    )(near(grad), near(parcel), near(mask), far(weight))


def backward_halos_kernel(table, partial, mask, weight, done, *refs):
    arrived, (grad_feats, bias_sum, planes, near_weight, fetched, sent) = refs[:-6], refs[-6:]
    width = weight.shape[1]
    fetch_taps(weight, near_weight, fetched)
    valid = windows((128, width), 0)
    await_taps(0, weight.shape[0], weight, near_weight, fetched)
    for side in range(2):
        halo = jnp.concatenate([chosen(table, 2 * side + b, arrived) for b in range(2)], axis=0)
        total = partial[side]
        for at, moved in enumerate(shifts(halo, 0, valid, -1)):
            total += lax.dot_general(
                moved,
                near_weight[18 * (1 - side) + at],
                (((1,), (1,)), ((), ())),
                preferred_element_type=jnp.float32,
            )
        rows = slice(896 * side, 896 * side + 128)
        done_rows = jnp.where(wide(mask[rows, :]), total, 0.0).astype(jnp.bfloat16)
        for b in range(2):
            planes[side, b, 0] = done_rows[64 * b : 64 * b + 64]
        pltpu.make_async_copy(planes.at[side], grad_feats.at[:, pl.ds(7 * side, 1)], sent.at[side]).start()
    bias_sum[...] = sum(read_extra(ref) for ref in arrived)
    for side in range(2):
        pltpu.make_async_copy(planes.at[side], grad_feats.at[:, pl.ds(7 * side, 1)], sent.at[side]).wait()


def backward_halos(table, partial, mask, weight, done, arrived):
    width = weight.shape[1]
    return pl.pallas_call(
        backward_halos_kernel,
        in_specs=[SCALARS, WHOLE, WHOLE, FAR, FAR] + [WHOLE] * len(arrived),
        out_specs=(FAR, WHOLE),
        out_shape=(jax.ShapeDtypeStruct(done.shape, done.dtype), jax.ShapeDtypeStruct((1, width), jnp.float32)),
        scratch_shapes=[
            pltpu.VMEM((2, 2, 1, 64, width), jnp.bfloat16),
            pltpu.VMEM(weight.shape, jnp.bfloat16),
            pltpu.SemaphoreType.DMA((weight.shape[0],)),
            pltpu.SemaphoreType.DMA((2,)),
        ],
        input_output_aliases={4: 0},
        compiler_params=params(10),
        cost_estimate=cost(1024, 1024),
        name="backward_halos",
    )(table, near(partial), near(mask), far(weight), done, *[near(x) for x in arrived])


def assemble_kernel(outer, places, *refs):
    parts, (out, done) = refs[: len(places)], refs[-2:]
    position = me()
    copies = []
    for index, (ref, (steps, inner, core)) in enumerate(zip(parts, places)):
        block = lax.rem(position // 4 - steps + outer, outer)
        quarter = 4 * ((position % 4) ^ (2 * inner + core))
        if outer == 4:
            copies.append((None, pltpu.make_async_copy(ref, out.at[:, quarter + block], done.at[index, 0])))
            continue
        for unit in range(units(outer)):
            place = block + outer * unit
            here = jnp.minimum(place, 107)
            target = out.at[here // 4, quarter + here % 4]
            copies.append((place < 108, pltpu.make_async_copy(ref.at[unit], target, done.at[index, unit])))
    for wait in (False, True):
        for condition, copy in copies:
            act = copy.wait if wait else copy.start
            if condition is None:
                act()
            else:
                pl.when(condition)(act)


def assemble(outer, places, parts, shape, given):
    before = [] if given is None else [given]
    rows = units(outer)
    return pl.pallas_call(
        functools.partial(assemble_kernel, outer, places),
        in_specs=[WHOLE] * len(parts) + [FAR] * len(before),
        out_specs=FAR,
        out_shape=jax.ShapeDtypeStruct(shape, jnp.bfloat16),
        scratch_shapes=[pltpu.SemaphoreType.DMA((len(parts), rows))],
        input_output_aliases={len(parts): 0} if before else {},
        compiler_params=params(),
        cost_estimate=cost(1024, 1024),
        name="assemble",
    )(*[near(x.reshape(rows, 16, shape[-1])) for x in parts], *before)


def per_device(size, feats, voxmask, links, weight, bias, cotangent):
    width = feats.shape[3]
    outer = size // 4

    parcel = rims(links, feats, voxmask)
    mask, rows, give_inner, give_core, turned, taps, ends = prepare(feats, voxmask, weight, cotangent)
    inner, rows = lax.optimization_barrier((swap(parcel, size, 2), rows))
    parcels = [parcel, inner, swap(parcel, size, 1), swap(inner, size, 1)]
    out, grad, edge, bias_local = forward_inside(rows, mask, taps, bias.reshape(1, width), ends)
    *parcels, grad = lax.optimization_barrier((*parcels, grad))
    table, picks = route(parcels, outer)

    *picks, give_inner, give_core = lax.optimization_barrier((*picks, give_inner, give_core))
    arrived = [rotate(pick, size, steps) if steps else pick for steps, pick in enumerate(picks)]
    got_inner, grad_inner = swap(give_inner, size, 2), swap(grad, size, 2)
    *arrived, got_inner, grad_inner = lax.optimization_barrier((*arrived, got_inner, grad_inner))
    others = turn(got_inner, swap(give_core, size, 1), swap(got_inner, size, 1))
    grads = [grad, grad_inner, swap(grad, size, 1), swap(grad_inner, size, 1)]

    out, to_inner, to_core, halos = forward_edges(table, mask, taps, edge, ends, bias_local, out, arrived)
    inner = swap(to_inner, size, 2)
    terms = inner_terms(turned, others, grads)
    inner, terms = lax.optimization_barrier((inner, terms))
    parcels = [to_inner, inner, swap(to_core, size, 1), swap(inner, size, 1)]

    gives, stay = outer_terms(outer, turned, others, halos, parcels, terms)
    gots = [rotate(give, size, steps + 1) for steps, give in enumerate(gives)]
    grad_feats, partial = backward(grad, to_inner, mask, weight)
    picks = repeat_route(table, parcels, outer)
    stay, partial, *picks = lax.optimization_barrier((stay, partial, *picks))
    part = (stay + sum(got.astype(jnp.float32) for got in gots)).astype(jnp.bfloat16)

    blocks = {(0, 0): part, (0, 1): swap(part, size, 2)}
    later, blocks[0, 1] = lax.optimization_barrier((part, blocks[0, 1]))
    for steps in [k for k in range(1, outer) if k in (1, outer - 1)] + list(range(2, outer - 1)):
        blocks[steps, 0] = rotate(part if steps in (1, outer - 1) else later, size, steps)
        blocks[steps, 1] = swap(blocks[steps, 0], size, 2)
    blocks[1, 1], *picks = lax.optimization_barrier((blocks[1, 1], *picks))
    arrived = [rotate(pick, size, steps) if steps else pick for steps, pick in enumerate(picks)]
    grad_feats, grad_bias = backward_halos(table, partial, mask, weight, grad_feats, arrived)

    early = [(0, 0), (0, 1), (1, 0), (outer - 1, 0)]
    grad_weight = None
    for chosen_blocks in (early, [key for key in blocks if key not in early]):
        places = [(steps, bit, core) for core in range(2) for steps, bit in chosen_blocks]
        parts = [blocks[key] for key in chosen_blocks]
        parts += [swap(x, size, 1) for x in parts]
        grad_weight = assemble(outer, places, parts, (27, 16, width // 16, width), grad_weight)
    return out, grad_feats, grad_weight.reshape(weight.shape), grad_bias.reshape(width)


def solution(mesh):
    return jax.shard_map(
        functools.partial(per_device, mesh.shape["zslab"]),
        mesh=mesh,
        in_specs=(
            P(("groups", "zslab"), None, None, None),
            P(("groups", "zslab"), None),
            P(("groups", "zslab"), None),
            P(),
            P(),
            P(("groups", "zslab"), None, None, None),
        ),
        out_specs=(
            P(("groups", "zslab"), None, None, None),
            P(("groups", "zslab"), None, None, None),
            P("groups", None, None),
            P("groups"),
        ),
        check_vma=False,
    )
```

```python
import functools

import jax
import jax.numpy as jnp
from jax import lax
from jax.experimental import pallas as pl
from jax.experimental.pallas import tpu as pltpu
from jax.sharding import PartitionSpec as P

EXTRA = 16


def params(mebibytes=6):
    return pltpu.CompilerParams(vmem_limit_bytes=mebibytes * 1024 * 1024)


def cost(flops, bytes_accessed):
    return pl.CostEstimate(flops=flops, bytes_accessed=bytes_accessed, transcendentals=0)


def near(x):
    return pltpu.with_memory_space_constraint(x, pltpu.VMEM)


def far(x):
    return pltpu.with_memory_space_constraint(x, pltpu.HBM)


SCALARS = pl.BlockSpec(memory_space=pltpu.SMEM)
WHOLE = pl.BlockSpec(memory_space=pltpu.VMEM)
FAR = pl.BlockSpec(memory_space=pl.ANY)


def swap(x, size, bit):
    return lax.ppermute(x, "zslab", [(i, i ^ bit) for i in range(size)])


def rotate(x, size, steps):
    return lax.ppermute(x, "zslab", [(i, (i + 4 * steps) % size) for i in range(size)])


def me():
    return lax.axis_index("zslab")


def units(outer):
    return -(-108 // outer)


def mask_rows(voxmask, z):
    lanes = slice(64 * z, 64 * z + 64)
    line = jnp.concatenate([voxmask[0:1, lanes], voxmask[1:2, lanes]], axis=1)
    return jnp.broadcast_to((line == 1).astype(jnp.float32), (128, 128)).T


def wide(mask):
    return jnp.concatenate([mask, mask], axis=1) > 0


def both(ref, z):
    return jnp.concatenate([ref[0, z], ref[1, z]], axis=0)


def inside(shape, dim, rows, cols):
    index = lax.broadcasted_iota(jnp.int32, shape, dim)
    row = (index // 8) % 8 + rows
    col = index % 8 + cols
    return (row >= 0) & (row < 8) & (col >= 0) & (col < 8)


def windows(shape, dim):
    return [inside(shape, dim, p, q) for p in (-1, 0, 1) for q in (-1, 0, 1)]


def shifts(x, dim, valid, sign=1):
    count = x.shape[dim]
    moved = []
    for place in range(9):
        at = place if sign == 1 else 8 - place
        move = 8 * (at // 3 - 1) + at % 3 - 1
        turned = pltpu.roll(x, (-move) % count, dim) if move else x
        moved.append(jnp.where(valid[at], turned, 0.0).astype(jnp.bfloat16))
    return moved


def activate(pre, cotangent, keep):
    sigma = 1.0 / (1.0 + jnp.exp(-pre))
    out = jnp.where(keep, pre * sigma, 0.0)
    grad = jnp.where(keep, cotangent * sigma * (1.0 + pre * (1.0 - sigma)), 0.0)
    return out.astype(jnp.bfloat16), grad.astype(jnp.bfloat16)


def write_exact(rows, ref):
    high = rows.astype(jnp.bfloat16)
    left = rows - high.astype(jnp.float32)
    middle = left.astype(jnp.bfloat16)
    low = (left - middle.astype(jnp.float32)).astype(jnp.bfloat16)
    zeros = jnp.zeros((EXTRA - 3, rows.shape[1]), jnp.float32)
    terms = [term.astype(jnp.float32) for term in (high, middle, low)]
    ref[256:272, :] = jnp.concatenate(terms + [zeros], axis=0).astype(jnp.bfloat16)


def read_extra(ref):
    return jnp.sum(ref[256:272, :].astype(jnp.float32), axis=0, keepdims=True)


def rims_kernel(links, feats, voxmask, parcel, planes, masks, codes, done):
    width = feats.shape[3]
    copies = [
        pltpu.make_async_copy(feats.at[:, pl.ds(0, 1)], planes.at[0], done.at[0]),
        pltpu.make_async_copy(feats.at[:, pl.ds(7, 1)], planes.at[1], done.at[1]),
        pltpu.make_async_copy(voxmask, masks, done.at[2]),
        pltpu.make_async_copy(links, codes, done.at[3]),
    ]
    for copy in copies:
        copy.start()
    for copy in copies:
        copy.wait()
    for side in range(2):
        keep = wide(mask_rows(masks, 7 * side))
        plane = jnp.concatenate([planes[side, 0, 0], planes[side, 1, 0]], axis=0).astype(jnp.float32)
        parcel[128 * side : 128 * side + 128, :] = jnp.where(keep, plane, 0.0).astype(jnp.bfloat16)
    lane = lax.broadcasted_iota(jnp.int32, (EXTRA, width), 1)
    row = jnp.zeros((EXTRA, width), jnp.float32)
    for place in range(4):
        row = jnp.where(lane == place, codes[place // 2, place % 2].astype(jnp.float32), row)
    parcel[256:272, :] = row.astype(jnp.bfloat16)


def rims(links, feats, voxmask):
    width = feats.shape[3]
    return pl.pallas_call(
        rims_kernel,
        in_specs=[FAR] * 3,
        out_specs=WHOLE,
        out_shape=pltpu.VMEM((256 + EXTRA, width), jnp.bfloat16),
        scratch_shapes=[
            pltpu.VMEM((2, 2, 1, 64, width), jnp.bfloat16),
            pltpu.VMEM(voxmask.shape, jnp.int32),
            pltpu.SMEM(links.shape, jnp.int32),
            pltpu.SemaphoreType.DMA((4,)),
        ],
        compiler_params=params(),
        cost_estimate=cost(1024, 1024),
        name="rims",
    )(far(links), far(feats), far(voxmask))


def fetch_taps(weight, near_weight, done):
    for tap in range(weight.shape[0]):
        pltpu.make_async_copy(weight.at[tap], near_weight.at[tap], done.at[tap]).start()


def await_taps(first, last, weight, near_weight, done):
    for tap in range(first, last):
        pltpu.make_async_copy(weight.at[tap], near_weight.at[tap], done.at[tap]).wait()


def aligned(index, rows):
    return pl.ds(pl.multiple_of(index * rows, rows), rows)


def quarters(flip, own, give_inner, give_core):
    position = me() % 4
    rows = flip.shape[0] // 4
    if own is not None:
        own[...] = flip[aligned(position, rows), :].astype(own.dtype)
    give_inner[...] = flip[aligned(1 - position // 2, 2 * rows), :].astype(jnp.bfloat16)
    give_core[...] = flip[aligned(position // 2 * 2 + 1 - position % 2, rows), :].astype(jnp.bfloat16)


def turn_rows(flip, lanes, valid, turned, first):
    rows = flip.shape[0]
    for place, moved in enumerate(shifts(flip[:, lanes].astype(jnp.float32), 1, valid)):
        turned[first + place * rows : first + (place + 1) * rows, lanes] = moved


def prepare_kernel(
    feats, voxmask, weight, cotangent, mask, rows, give_inner, give_core, turned, taps, slopes, planes, masks, flip, own, done, fetched
):
    count = weight.shape[0]
    pltpu.make_async_copy(voxmask, masks, done.at[8]).start()
    for z in range(8):
        pltpu.make_async_copy(feats.at[:, pl.ds(z, 1)], planes.at[:, pl.ds(z, 1)], done.at[z]).start()
    fetch_taps(weight, taps, fetched)
    for z in range(8):
        pltpu.make_async_copy(cotangent.at[:, pl.ds(z, 1)], slopes.at[:, pl.ds(z, 1)], fetched.at[count + z]).start()
    valid = windows((own.shape[0], 128), 1)
    pltpu.make_async_copy(voxmask, masks, done.at[8]).wait()
    for z in range(8):
        pltpu.make_async_copy(feats.at[:, pl.ds(z, 1)], planes.at[:, pl.ds(z, 1)], done.at[z]).wait()
        span = slice(128 * z, 128 * z + 128)
        keep = mask_rows(masks, z)
        mask[span, :] = keep
        plane = jnp.where(wide(keep), both(planes, z).astype(jnp.float32), 0.0)
        rows[span, :] = plane.astype(jnp.bfloat16)
        flip[:, span] = plane.T
    quarters(flip, own, give_inner, give_core)
    for z in range(8):
        turn_rows(own, slice(128 * z, 128 * z + 128), valid, turned, 0)
    await_taps(0, count, weight, taps, fetched)
    for z in range(8):
        pltpu.make_async_copy(cotangent.at[:, pl.ds(z, 1)], slopes.at[:, pl.ds(z, 1)], fetched.at[count + z]).wait()


def prepare(feats, voxmask, weight, cotangent):
    width = feats.shape[3]
    quarter = width // 4
    return pl.pallas_call(
        prepare_kernel,
        in_specs=[FAR] * 4,
        out_specs=(WHOLE,) * 7,
        out_shape=(
            pltpu.VMEM((1024, 128), jnp.float32),
            pltpu.VMEM((1024, width), jnp.bfloat16),
            pltpu.VMEM((2 * quarter, 1024), jnp.bfloat16),
            pltpu.VMEM((quarter, 1024), jnp.bfloat16),
            pltpu.VMEM((9 * quarter, 1024), jnp.bfloat16),
            pltpu.VMEM(weight.shape, jnp.bfloat16),
            pltpu.VMEM(cotangent.shape, jnp.bfloat16),
        ),
        scratch_shapes=[
            pltpu.VMEM(feats.shape, jnp.bfloat16),
            pltpu.VMEM(voxmask.shape, jnp.int32),
            pltpu.VMEM((width, 1024), jnp.float32),
            pltpu.VMEM((quarter, 1024), jnp.float32),
            pltpu.SemaphoreType.DMA((9,)),
            pltpu.SemaphoreType.DMA((weight.shape[0] + 8,)),
        ],
        compiler_params=params(12),
        cost_estimate=cost(1024, 1024),
        name="prepare",
    )(far(feats), far(voxmask), far(weight), far(cotangent))


def turn_kernel(inner, core, both_changed, turned):
    quarter = core.shape[0]
    valid = windows((quarter, 128), 1)
    mine = aligned(me() % 2, quarter)
    for z in range(8):
        lanes = slice(128 * z, 128 * z + 128)
        for index, rows in enumerate((inner[mine, lanes], core[:, lanes], both_changed[mine, lanes])):
            first = 9 * quarter * index
            for place, moved in enumerate(shifts(rows.astype(jnp.float32), 1, valid)):
                turned[first + place * quarter : first + (place + 1) * quarter, lanes] = moved


def turn(inner, core, both_changed):
    quarter = core.shape[0]
    return pl.pallas_call(
        turn_kernel,
        in_specs=[WHOLE] * 3,
        out_specs=WHOLE,
        out_shape=pltpu.VMEM((27 * quarter, 1024), jnp.bfloat16),
        compiler_params=params(10),
        cost_estimate=cost(1024, 1024),
        name="turn",
    )(near(inner), near(core), near(both_changed))


def copy_picks(outer, table, parcels, picks, planes):
    for dev in range(4):
        planes[256 * dev : 256 * dev + 256, :] = parcels[dev][:256, :]
    for steps in range(outer):
        for slot in range(4):
            start = pl.multiple_of(table[steps * 4 + slot] * 64, 64)
            picks[steps][64 * slot : 64 * slot + 64, :] = planes[pl.ds(start, 64), :]


def route_kernel(outer, *refs):
    position = me()
    parcels, (table, *picks), (codes, links, planes, done) = refs[:4], refs[4:-4], refs[-4:]
    for dev in range(4):
        row = parcels[dev][256:272, :128].astype(jnp.float32)
        codes[8 * dev : 8 * dev + 8, :] = row[:8, :].astype(jnp.int32)
    copy = pltpu.make_async_copy(codes, links, done)
    copy.start()
    copy.wait()
    for place in range(outer * 4):
        table[place] = 0
    for plane in range(16):
        dev, side, brick = plane // 4, plane // 2 % 2, plane % 2
        dest = links[dev * 8, brick * 2 + side]

        @pl.when((dest >= 0) & ((dest // 2) % 4 == position % 4))
        def _():
            steps = lax.rem(dest // 8 - position // 4 + outer, outer)
            table[steps * 4 + dest % 2 + (0 if side == 1 else 2)] = plane

    for brick in range(2):
        for side in range(2):
            dest = links[0, brick * 2 + side]
            steps = lax.rem(position // 4 - dest // 8 + outer, outer)
            table[outer * 4 + 2 * side + brick] = jnp.where(dest >= 0, steps, -1)

    copy_picks(outer, table, parcels, picks, planes)


def route(parcels, outer):
    width = parcels[0].shape[1]
    results = pl.pallas_call(
        functools.partial(route_kernel, outer),
        in_specs=[WHOLE] * 4,
        out_specs=[SCALARS] + [WHOLE] * outer,
        out_shape=[jax.ShapeDtypeStruct((outer * 4 + 4,), jnp.int32)]
        + [pltpu.VMEM((256, width), jnp.bfloat16)] * outer,
        scratch_shapes=[
            pltpu.VMEM((32, 128), jnp.int32),
            pltpu.SMEM((32, 128), jnp.int32),
            pltpu.VMEM((1024, width), jnp.bfloat16),
            pltpu.SemaphoreType.DMA(()),
        ],
        compiler_params=params(),
        cost_estimate=cost(1024, 1024),
        name="route",
    )(*[near(x) for x in parcels])
    return results[0], results[1:]


def repeat_kernel(outer, table, *refs):
    parcels, picks, planes = refs[:4], refs[4:-1], refs[-1]
    copy_picks(outer, table, parcels, picks, planes)
    total = sum(read_extra(ref) for ref in parcels)
    for ref in picks:
        write_exact(total, ref)


def repeat_route(table, parcels, outer):
    width = parcels[0].shape[1]
    return pl.pallas_call(
        functools.partial(repeat_kernel, outer),
        in_specs=[SCALARS] + [WHOLE] * 4,
        out_specs=[WHOLE] * outer,
        out_shape=[pltpu.VMEM((256 + EXTRA, width), jnp.bfloat16)] * outer,
        scratch_shapes=[pltpu.VMEM((1024, width), jnp.bfloat16)],
        compiler_params=params(),
        cost_estimate=cost(1024, 1024),
        name="repeat_route",
    )(table, *[near(x) for x in parcels])


def chosen(table, slot, arrived):
    rows = slice(64 * slot, 64 * slot + 64)
    plane = jnp.zeros((64, arrived[0].shape[1]), jnp.float32)
    for steps, ref in enumerate(arrived):
        plane = jnp.where(table[4 * len(arrived) + slot] == steps, ref[rows, :].astype(jnp.float32), plane)
    return plane


def forward_kernel(rows, mask, weight, bias, slopes, out, grad, edge, bias_sum, cols, pre):
    width = rows.shape[1]
    valid = windows((128, width), 0)
    for z in range(8):
        span = slice(128 * z, 128 * z + 128)
        for place, moved in enumerate(shifts(rows[span, :].astype(jnp.float32), 0, valid)):
            cols[span, place * width : (place + 1) * width] = moved

    def taps(a):
        return weight[9 * a : 9 * a + 9].reshape(9 * width, width)

    pre[...] = jnp.dot(cols[...], taps(1), preferred_element_type=jnp.float32) + bias[...]
    pre[128:, :] += jnp.dot(cols[:896, :], taps(0), preferred_element_type=jnp.float32)
    pre[:896, :] += jnp.dot(cols[128:, :], taps(2), preferred_element_type=jnp.float32)
    for side in range(2):
        edge[side] = pre[896 * side : 896 * side + 128, :]
    total = jnp.zeros((1, width), jnp.float32)
    for z in range(1, 7):
        span = slice(128 * z, 128 * z + 128)
        act, slope = activate(pre[span, :], both(slopes, z).astype(jnp.float32), wide(mask[span, :]))
        for b in range(2):
            out[b, z] = act[64 * b : 64 * b + 64]
        grad[128 * (z - 1) : 128 * z, :] = slope
        total += jnp.sum(slope.astype(jnp.float32), axis=0, keepdims=True)
    bias_sum[...] = total


def forward_inside(rows, mask, weight, bias, cotangent):
    width = rows.shape[1]
    return pl.pallas_call(
        forward_kernel,
        in_specs=[WHOLE] * 5,
        out_specs=(WHOLE,) * 4,
        out_shape=(
            jax.ShapeDtypeStruct(cotangent.shape, jnp.bfloat16),
            pltpu.VMEM((768, width), jnp.bfloat16),
            pltpu.VMEM((2, 128, width), jnp.float32),
            pltpu.VMEM((1, width), jnp.float32),
        ),
        scratch_shapes=[
            pltpu.VMEM((1024, 9 * width), jnp.bfloat16),
            pltpu.VMEM((1024, width), jnp.float32),
        ],
        compiler_params=params(12),
        cost_estimate=cost(1024, 1024),
        name="forward_inside",
    )(near(rows), near(mask), near(weight), bias, near(cotangent))


def inner_terms_kernel(mine, others, *refs):
    grads, terms = refs[:4], refs[4]
    rows = mine.shape[0]
    for a in range(3):
        lanes = slice(128 * a, 128 * a + 768)
        total = jnp.dot(mine[:, lanes], grads[0][...], preferred_element_type=jnp.float32)
        for index in range(3):
            total += jnp.dot(
                others[index * rows : (index + 1) * rows, lanes], grads[index + 1][...], preferred_element_type=jnp.float32
            )
        terms[a * rows : (a + 1) * rows, :] = total


def inner_terms(mine, others, grads):
    rows, width = mine.shape[0], grads[0].shape[1]
    return pl.pallas_call(
        inner_terms_kernel,
        in_specs=[WHOLE] * 6,
        out_specs=WHOLE,
        out_shape=pltpu.VMEM((3 * rows, width), jnp.float32),
        compiler_params=params(10),
        cost_estimate=cost(1024, 1024),
        name="inner_terms",
    )(near(mine), near(others), *[near(x) for x in grads])


def edge_kernel(table, mask, weight, edge, ends, inner, out_in, *refs):
    arrived, (out, to_inner, to_core, own, planes, flip, done) = refs[:-7], refs[-7:]
    width = edge.shape[2]
    valid = windows((128, width), 0)
    total = inner[...]
    for side in range(2):
        rows = slice(128 * side, 128 * side + 128)
        halo = jnp.concatenate([chosen(table, 2 * side + b, arrived) for b in range(2)], axis=0)
        flip[:, rows] = halo.T
        cols = jnp.concatenate(shifts(halo, 0, valid), axis=1)
        taps = weight[18 * side : 18 * side + 9].reshape(9 * width, width)
        pre = edge[side] + jnp.dot(cols, taps, preferred_element_type=jnp.float32)
        z = 7 * side
        keep = wide(mask[128 * z : 128 * z + 128, :])
        act, slope = activate(pre, both(ends, z).astype(jnp.float32), keep)
        for b in range(2):
            planes[side, b, 0] = act[64 * b : 64 * b + 64]
        pltpu.make_async_copy(planes.at[side], out.at[:, pl.ds(z, 1)], done.at[side]).start()
        to_inner[rows, :] = slope
        to_core[rows, :] = slope
        total += jnp.sum(slope.astype(jnp.float32), axis=0, keepdims=True)
    write_exact(total, to_inner)
    write_exact(total, to_core)
    quarters(flip, own, to_inner.at[272:], to_core.at[272:])
    for side in range(2):
        pltpu.make_async_copy(planes.at[side], out.at[:, pl.ds(7 * side, 1)], done.at[side]).wait()


def forward_edges(table, mask, weight, edge, ends, inner, out, arrived):
    width = edge.shape[2]
    quarter = width // 4
    return pl.pallas_call(
        edge_kernel,
        in_specs=[SCALARS] + [WHOLE] * 5 + [FAR] + [WHOLE] * len(arrived),
        out_specs=(FAR, WHOLE, WHOLE, WHOLE),
        out_shape=(
            jax.ShapeDtypeStruct(out.shape, out.dtype),
            pltpu.VMEM((256 + EXTRA + 2 * quarter, width), jnp.bfloat16),
            pltpu.VMEM((256 + EXTRA + quarter, width), jnp.bfloat16),
            pltpu.VMEM((quarter, 256), jnp.bfloat16),
        ),
        scratch_shapes=[
            pltpu.VMEM((2, 2, 1, 64, width), jnp.bfloat16),
            pltpu.VMEM((width, 256), jnp.float32),
            pltpu.SemaphoreType.DMA((2,)),
        ],
        input_output_aliases={6: 0},
        compiler_params=params(10),
        cost_estimate=cost(1024, 1024),
        name="forward_edges",
    )(
        table,
        near(mask),
        near(weight),
        near(edge),
        near(ends),
        near(inner),
        out,
        *[near(x) for x in arrived],
    )


def outer_terms_kernel(outer, mine, others, halos, *refs):
    parcels, inner = refs[:4], refs[4]
    gives, stay, cols, total = refs[5 : 4 + outer], refs[4 + outer], refs[5 + outer], refs[6 + outer]
    quarter = halos.shape[0]
    rows = 9 * quarter
    valid = windows((quarter, 128), 1)
    half = aligned(me() % 2, quarter)
    ends = (
        halos,
        parcels[1].at[272 : 272 + 2 * quarter].at[half],
        parcels[2].at[272 : 272 + quarter],
        parcels[3].at[272 : 272 + 2 * quarter].at[half],
    )
    facing = jnp.concatenate(
        [parcel[128 * side : 128 * side + 128, :] for side in range(2) for parcel in parcels], axis=0
    )
    for a in range(3):
        for side in range(2):
            plane = a - 1 + 7 * side
            for who in range(4):
                lanes = slice(128 * (4 * side + who), 128 * (4 * side + who) + 128)
                if 0 <= plane < 8:
                    ref, first = (mine, 0) if who == 0 else (others, rows * (who - 1))
                    cols[:, lanes] = ref[first : first + rows, 128 * plane : 128 * plane + 128]
                else:
                    moved = shifts(ends[who][:, 128 * side : 128 * side + 128].astype(jnp.float32), 1, valid)
                    for place in range(9):
                        cols[place * quarter : (place + 1) * quarter, lanes] = moved[place]
        span = slice(a * rows, (a + 1) * rows)
        total[span, :] = inner[span, :] + jnp.dot(cols[...], facing, preferred_element_type=jnp.float32)
    if total.shape[0] > 3 * rows:
        total[3 * rows :, :] = jnp.zeros((total.shape[0] - 3 * rows, total.shape[1]), jnp.float32)
    z = me() // 4
    for steps in range(outer):
        block = lax.rem(z + steps, outer)
        for unit in range(units(outer)):
            piece = total[aligned(block + outer * unit, 16), :]
            if steps:
                gives[steps - 1][16 * unit : 16 * unit + 16, :] = piece.astype(jnp.bfloat16)
            else:
                stay[16 * unit : 16 * unit + 16, :] = piece


def outer_terms(outer, mine, others, halos, parcels, inner):
    width = inner.shape[1]
    rows = 16 * units(outer)
    results = pl.pallas_call(
        functools.partial(outer_terms_kernel, outer),
        in_specs=[WHOLE] * 8,
        out_specs=[WHOLE] * outer,
        out_shape=[pltpu.VMEM((rows, width), jnp.bfloat16)] * (outer - 1) + [pltpu.VMEM((rows, width), jnp.float32)],
        scratch_shapes=[
            pltpu.VMEM((inner.shape[0] // 3, 1024), jnp.bfloat16),
            pltpu.VMEM((outer * rows, width), jnp.float32),
        ],
        compiler_params=params(12),
        cost_estimate=cost(1024, 1024),
        name="outer_terms",
    )(*[near(x) for x in (mine, others, halos, *parcels, inner)])
    return results[:-1], results[-1]


def backward_kernel(grad, parcel, mask, weight, grad_feats, partial, near_weight, cols, total, fetched):
    width = grad.shape[1]
    fetch_taps(weight, near_weight, fetched)
    valid = windows((128, width), 0)
    planes = [parcel[:128, :]] + [grad[128 * z : 128 * z + 128, :] for z in range(6)] + [parcel[128:256, :]]
    for z, plane in enumerate(planes):
        for at, moved in enumerate(shifts(plane.astype(jnp.float32), 0, valid, -1)):
            cols[128 * z : 128 * z + 128, at * width : (at + 1) * width] = moved
    for a in (1, 0, 2):
        await_taps(9 * a, 9 * a + 9, weight, near_weight, fetched)
        first, start, count = ((128, 0, 896), (0, 0, 1024), (0, 128, 896))[a]
        for at in range(9):
            piece = lax.dot_general(
                cols[first : first + count, at * width : (at + 1) * width],
                near_weight[9 * a + at],
                (((1,), (1,)), ((), ())),
                preferred_element_type=jnp.float32,
            )
            if a == 1 and at == 0:
                total[...] = piece
            else:
                total[start : start + count, :] += piece
    for z in range(1, 7):
        rows = slice(128 * z, 128 * z + 128)
        done = jnp.where(wide(mask[rows, :]), total[rows, :], 0.0).astype(jnp.bfloat16)
        for b in range(2):
            grad_feats[b, z] = done[64 * b : 64 * b + 64]
    for side in range(2):
        partial[side] = total[896 * side : 896 * side + 128, :]


def backward(grad, parcel, mask, weight):
    width = grad.shape[1]
    return pl.pallas_call(
        backward_kernel,
        in_specs=[WHOLE] * 3 + [FAR],
        out_specs=(WHOLE,) * 3,
        out_shape=(
            jax.ShapeDtypeStruct((2, 8, 64, width), jnp.bfloat16),
            pltpu.VMEM((2, 128, width), jnp.float32),
            pltpu.VMEM(weight.shape, jnp.bfloat16),
        ),
        scratch_shapes=[
            pltpu.VMEM((1024, 9 * width), jnp.bfloat16),
            pltpu.VMEM((1024, width), jnp.float32),
            pltpu.SemaphoreType.DMA((weight.shape[0],)),
        ],
        compiler_params=params(16),
        cost_estimate=cost(1024, 1024),
        name="backward",
    )(near(grad), near(parcel), near(mask), far(weight))


def backward_halos_kernel(table, partial, mask, weight, done, *refs):
    arrived, (grad_feats, bias_sum, planes, sent) = refs[:-4], refs[-4:]
    width = weight.shape[1]
    valid = windows((128, width), 0)
    for side in range(2):
        halo = jnp.concatenate([chosen(table, 2 * side + b, arrived) for b in range(2)], axis=0)
        total = partial[side]
        for at, moved in enumerate(shifts(halo, 0, valid, -1)):
            total += lax.dot_general(
                moved,
                weight[18 * (1 - side) + at],
                (((1,), (1,)), ((), ())),
                preferred_element_type=jnp.float32,
            )
        rows = slice(896 * side, 896 * side + 128)
        done_rows = jnp.where(wide(mask[rows, :]), total, 0.0).astype(jnp.bfloat16)
        for b in range(2):
            planes[side, b, 0] = done_rows[64 * b : 64 * b + 64]
        pltpu.make_async_copy(planes.at[side], grad_feats.at[:, pl.ds(7 * side, 1)], sent.at[side]).start()
    bias_sum[...] = sum(read_extra(ref) for ref in arrived)
    for side in range(2):
        pltpu.make_async_copy(planes.at[side], grad_feats.at[:, pl.ds(7 * side, 1)], sent.at[side]).wait()


def backward_halos(table, partial, mask, weight, done, arrived):
    width = weight.shape[1]
    return pl.pallas_call(
        backward_halos_kernel,
        in_specs=[SCALARS] + [WHOLE] * 3 + [FAR] + [WHOLE] * len(arrived),
        out_specs=(FAR, WHOLE),
        out_shape=(jax.ShapeDtypeStruct(done.shape, done.dtype), jax.ShapeDtypeStruct((1, width), jnp.float32)),
        scratch_shapes=[
            pltpu.VMEM((2, 2, 1, 64, width), jnp.bfloat16),
            pltpu.SemaphoreType.DMA((2,)),
        ],
        input_output_aliases={4: 0},
        compiler_params=params(10),
        cost_estimate=cost(1024, 1024),
        name="backward_halos",
    )(table, near(partial), near(mask), near(weight), done, *[near(x) for x in arrived])


def assemble_kernel(outer, places, parts, *refs):
    out, done = refs[-2:]
    position = me()
    blocks = [ref.at[index] for ref, count in zip(refs, parts) for index in range(count)]
    copies = []
    for index, (ref, (flip, inner, core)) in enumerate(zip(blocks, places)):
        block = (position // 4) ^ flip
        quarter = 4 * ((position % 4) ^ (2 * inner + core))
        if outer == 4:
            copies.append((None, pltpu.make_async_copy(ref, out.at[:, quarter + block], done.at[index, 0])))
            continue
        for unit in range(units(outer)):
            place = block + outer * unit
            here = jnp.minimum(place, 107)
            target = out.at[here // 4, quarter + here % 4]
            copies.append((place < 108, pltpu.make_async_copy(ref.at[unit], target, done.at[index, unit])))
    for wait in (False, True):
        for condition, copy in copies:
            act = copy.wait if wait else copy.start
            if condition is None:
                act()
            else:
                pl.when(condition)(act)


def assemble(outer, places, stacks, shape, given):
    before = [] if given is None else [given]
    rows = units(outer)
    return pl.pallas_call(
        functools.partial(assemble_kernel, outer, places, [x.shape[0] for x in stacks]),
        in_specs=[WHOLE] * len(stacks) + [FAR] * len(before),
        out_specs=FAR,
        out_shape=jax.ShapeDtypeStruct(shape, jnp.bfloat16),
        scratch_shapes=[pltpu.SemaphoreType.DMA((len(places), rows))],
        input_output_aliases={len(stacks): 0} if before else {},
        compiler_params=params(),
        cost_estimate=cost(1024, 1024),
        name="assemble",
    )(*[near(x.reshape(x.shape[0], rows, 16, shape[-1])) for x in stacks], *before)


def per_device(size, feats, voxmask, links, weight, bias, cotangent):
    width = feats.shape[3]
    outer = size // 4

    parcel = rims(links, feats, voxmask)
    mask, rows, give_inner, give_core, turned, taps, ends = prepare(feats, voxmask, weight, cotangent)
    inner, rows = lax.optimization_barrier((swap(parcel, size, 2), rows))
    parcels = [parcel, inner, swap(parcel, size, 1), swap(inner, size, 1)]
    out, grad, edge, bias_local = forward_inside(rows, mask, taps, bias.reshape(1, width), ends)
    got_inner = swap(give_inner, size, 2)
    *parcels, grad, got_inner = lax.optimization_barrier((*parcels, grad, got_inner))
    table, picks = route(parcels, outer)

    *picks, give_core = lax.optimization_barrier((*picks, give_core))
    arrived = [rotate(pick, size, steps) if steps else pick for steps, pick in enumerate(picks)]
    grad_inner = swap(grad, size, 2)
    *arrived, got_inner, grad_inner = lax.optimization_barrier((*arrived, got_inner, grad_inner))
    others = turn(got_inner, swap(give_core, size, 1), swap(got_inner, size, 1))
    grads = [grad, grad_inner, swap(grad, size, 1), swap(grad_inner, size, 1)]

    out, to_inner, to_core, halos = forward_edges(table, mask, taps, edge, ends, bias_local, out, arrived)
    inner = swap(to_inner, size, 2)
    terms = inner_terms(turned, others, grads)
    inner, terms = lax.optimization_barrier((inner, terms))
    parcels = [to_inner, inner, swap(to_core, size, 1), swap(inner, size, 1)]

    gives, stay = outer_terms(outer, turned, others, halos, parcels, terms)
    gots = [rotate(give, size, steps + 1) for steps, give in enumerate(gives)]
    grad_feats, partial, taps = backward(grad, to_inner, mask, weight)
    picks = repeat_route(table, parcels, outer)
    stay, partial, *picks = lax.optimization_barrier((stay, partial, *picks))
    part = (stay + sum(got.astype(jnp.float32) for got in gots)).astype(jnp.bfloat16)

    def stack(*blocks):
        return jnp.concatenate([x.reshape(-1, *part.shape) for x in blocks])

    def place_blocks(keys, blocks, given):
        places = [(flip, bit, core) for core in range(2) for flip, bit in keys]
        return assemble(outer, places, [blocks, swap(blocks, size, 1)], (27, 16, width // 16, width), given)

    last = outer - 1
    flips = list(range(1, last))
    blocks = [part]
    for flip in flips:
        blocks.append(swap(blocks[flip & (flip - 1)], size, 4 * (flip & -flip)))
    first_inner = swap(part, size, 2)
    middle = stack(*blocks[1:])
    farthest = swap(blocks[last & (last - 1)], size, 4)
    middle, *picks = lax.optimization_barrier((middle, *picks))
    middle_inner = swap(middle, size, 2)
    arrived = [rotate(pick, size, steps) if steps else pick for steps, pick in enumerate(picks)]
    grad_weight = place_blocks([(0, 0), (0, 1)] + [(flip, 0) for flip in flips], stack(part, first_inner, middle), None)
    farthest_inner = swap(farthest, size, 2)
    middle_inner, farthest_inner, grad_weight, *arrived = lax.optimization_barrier(
        (middle_inner, farthest_inner, grad_weight, *arrived)
    )
    keys = [(flip, 1) for flip in flips] + [(last, 0), (last, 1)]
    grad_weight = place_blocks(keys, stack(middle_inner, farthest, farthest_inner), grad_weight)
    grad_feats, grad_bias = backward_halos(table, partial, mask, taps, grad_feats, arrived)
    return out, grad_feats, grad_weight.reshape(weight.shape), grad_bias.reshape(width)


def solution(mesh):
    return jax.shard_map(
        functools.partial(per_device, mesh.shape["zslab"]),
        mesh=mesh,
        in_specs=(
            P(("groups", "zslab"), None, None, None),
            P(("groups", "zslab"), None),
            P(("groups", "zslab"), None),
            P(),
            P(),
            P(("groups", "zslab"), None, None, None),
        ),
        out_specs=(
            P(("groups", "zslab"), None, None, None),
            P(("groups", "zslab"), None, None, None),
            P("groups", None, None),
            P("groups"),
        ),
        check_vma=False,
    )
```

```python
import functools

import jax
import jax.numpy as jnp
from jax import lax
from jax.experimental import pallas as pl
from jax.experimental.pallas import tpu as pltpu
from jax.sharding import PartitionSpec as P

EXTRA = 16


def params(mebibytes=6):
    return pltpu.CompilerParams(vmem_limit_bytes=mebibytes * 1024 * 1024)


def cost(flops, bytes_accessed):
    return pl.CostEstimate(flops=flops, bytes_accessed=bytes_accessed, transcendentals=0)


def near(x):
    return pltpu.with_memory_space_constraint(x, pltpu.VMEM)


def far(x):
    return pltpu.with_memory_space_constraint(x, pltpu.HBM)


SCALARS = pl.BlockSpec(memory_space=pltpu.SMEM)
WHOLE = pl.BlockSpec(memory_space=pltpu.VMEM)
FAR = pl.BlockSpec(memory_space=pl.ANY)


def swap(x, size, bit):
    return lax.ppermute(x, "zslab", [(i, i ^ bit) for i in range(size)])


def rotate(x, size, steps):
    return lax.ppermute(x, "zslab", [(i, (i + 4 * steps) % size) for i in range(size)])


def me():
    return lax.axis_index("zslab")


def units(outer):
    return -(-108 // outer)


def mask_rows(voxmask, z):
    lanes = slice(64 * z, 64 * z + 64)
    line = jnp.concatenate([voxmask[0:1, lanes], voxmask[1:2, lanes]], axis=1)
    return jnp.broadcast_to((line == 1).astype(jnp.float32), (128, 128)).T


def wide(mask):
    return jnp.concatenate([mask, mask], axis=1) > 0


def both(ref, z):
    return jnp.concatenate([ref[0, z], ref[1, z]], axis=0)


def inside(shape, dim, rows, cols):
    index = lax.broadcasted_iota(jnp.int32, shape, dim)
    row = (index // 8) % 8 + rows
    col = index % 8 + cols
    return (row >= 0) & (row < 8) & (col >= 0) & (col < 8)


def windows(shape, dim):
    return [inside(shape, dim, p, q) for p in (-1, 0, 1) for q in (-1, 0, 1)]


def shifts(x, dim, valid, sign=1):
    count = x.shape[dim]
    moved = []
    for place in range(9):
        at = place if sign == 1 else 8 - place
        move = 8 * (at // 3 - 1) + at % 3 - 1
        turned = pltpu.roll(x, (-move) % count, dim) if move else x
        moved.append(jnp.where(valid[at], turned, 0.0).astype(jnp.bfloat16))
    return moved


def activate(pre, cotangent, keep):
    sigma = 1.0 / (1.0 + jnp.exp(-pre))
    out = jnp.where(keep, pre * sigma, 0.0)
    grad = jnp.where(keep, cotangent * sigma * (1.0 + pre * (1.0 - sigma)), 0.0)
    return out.astype(jnp.bfloat16), grad.astype(jnp.bfloat16)


def write_exact(rows, ref):
    high = rows.astype(jnp.bfloat16)
    left = rows - high.astype(jnp.float32)
    middle = left.astype(jnp.bfloat16)
    low = (left - middle.astype(jnp.float32)).astype(jnp.bfloat16)
    zeros = jnp.zeros((EXTRA - 3, rows.shape[1]), jnp.float32)
    terms = [term.astype(jnp.float32) for term in (high, middle, low)]
    ref[256:272, :] = jnp.concatenate(terms + [zeros], axis=0).astype(jnp.bfloat16)


def read_extra(ref):
    return jnp.sum(ref[256:272, :].astype(jnp.float32), axis=0, keepdims=True)


def rims_kernel(links, feats, voxmask, parcel, planes, masks, codes, done):
    width = feats.shape[3]
    copies = [
        pltpu.make_async_copy(feats.at[:, pl.ds(0, 1)], planes.at[0], done.at[0]),
        pltpu.make_async_copy(feats.at[:, pl.ds(7, 1)], planes.at[1], done.at[1]),
        pltpu.make_async_copy(voxmask, masks, done.at[2]),
        pltpu.make_async_copy(links, codes, done.at[3]),
    ]
    for copy in copies:
        copy.start()
    for copy in copies:
        copy.wait()
    for side in range(2):
        keep = wide(mask_rows(masks, 7 * side))
        plane = jnp.concatenate([planes[side, 0, 0], planes[side, 1, 0]], axis=0).astype(jnp.float32)
        parcel[128 * side : 128 * side + 128, :] = jnp.where(keep, plane, 0.0).astype(jnp.bfloat16)
    lane = lax.broadcasted_iota(jnp.int32, (EXTRA, width), 1)
    row = jnp.zeros((EXTRA, width), jnp.float32)
    for place in range(4):
        row = jnp.where(lane == place, codes[place // 2, place % 2].astype(jnp.float32), row)
    parcel[256:272, :] = row.astype(jnp.bfloat16)


def rims(links, feats, voxmask):
    width = feats.shape[3]
    return pl.pallas_call(
        rims_kernel,
        in_specs=[FAR] * 3,
        out_specs=WHOLE,
        out_shape=pltpu.VMEM((256 + EXTRA, width), jnp.bfloat16),
        scratch_shapes=[
            pltpu.VMEM((2, 2, 1, 64, width), jnp.bfloat16),
            pltpu.VMEM(voxmask.shape, jnp.int32),
            pltpu.SMEM(links.shape, jnp.int32),
            pltpu.SemaphoreType.DMA((4,)),
        ],
        compiler_params=params(),
        cost_estimate=cost(1024, 1024),
        name="rims",
    )(far(links), far(feats), far(voxmask))


def fetch_taps(weight, near_weight, done):
    for tap in range(weight.shape[0]):
        pltpu.make_async_copy(weight.at[tap], near_weight.at[tap], done.at[tap]).start()


def await_taps(first, last, weight, near_weight, done):
    for tap in range(first, last):
        pltpu.make_async_copy(weight.at[tap], near_weight.at[tap], done.at[tap]).wait()


def aligned(index, rows):
    return pl.ds(pl.multiple_of(index * rows, rows), rows)


def quarters(flip, own, give_inner, give_core):
    position = me() % 4
    rows = flip.shape[0] // 4
    if own is not None:
        own[...] = flip[aligned(position, rows), :].astype(own.dtype)
    give_inner[...] = flip[aligned(1 - position // 2, 2 * rows), :].astype(jnp.bfloat16)
    give_core[...] = flip[aligned(position // 2 * 2 + 1 - position % 2, rows), :].astype(jnp.bfloat16)


def turn_rows(flip, lanes, valid, turned, first):
    rows = flip.shape[0]
    for place, moved in enumerate(shifts(flip[:, lanes].astype(jnp.float32), 1, valid)):
        turned[first + place * rows : first + (place + 1) * rows, lanes] = moved


def prepare_kernel(
    feats, voxmask, weight, cotangent, mask, rows, give_inner, give_core, turned, taps, slopes, planes, masks, flip, own, done, fetched
):
    count = weight.shape[0]
    pltpu.make_async_copy(voxmask, masks, done.at[8]).start()
    for z in range(8):
        pltpu.make_async_copy(feats.at[:, pl.ds(z, 1)], planes.at[:, pl.ds(z, 1)], done.at[z]).start()
    fetch_taps(weight, taps, fetched)
    for z in range(8):
        pltpu.make_async_copy(cotangent.at[:, pl.ds(z, 1)], slopes.at[:, pl.ds(z, 1)], fetched.at[count + z]).start()
    valid = windows((own.shape[0], 128), 1)
    pltpu.make_async_copy(voxmask, masks, done.at[8]).wait()
    for z in range(8):
        pltpu.make_async_copy(feats.at[:, pl.ds(z, 1)], planes.at[:, pl.ds(z, 1)], done.at[z]).wait()
        span = slice(128 * z, 128 * z + 128)
        keep = mask_rows(masks, z)
        mask[span, :] = keep
        plane = jnp.where(wide(keep), both(planes, z).astype(jnp.float32), 0.0)
        rows[span, :] = plane.astype(jnp.bfloat16)
        flip[:, span] = plane.T
    quarters(flip, own, give_inner, give_core)
    for z in range(8):
        turn_rows(own, slice(128 * z, 128 * z + 128), valid, turned, 0)
    await_taps(0, count, weight, taps, fetched)
    for z in range(8):
        pltpu.make_async_copy(cotangent.at[:, pl.ds(z, 1)], slopes.at[:, pl.ds(z, 1)], fetched.at[count + z]).wait()


def prepare(feats, voxmask, weight, cotangent):
    width = feats.shape[3]
    quarter = width // 4
    return pl.pallas_call(
        prepare_kernel,
        in_specs=[FAR] * 4,
        out_specs=(WHOLE,) * 7,
        out_shape=(
            pltpu.VMEM((1024, 128), jnp.float32),
            pltpu.VMEM((1024, width), jnp.bfloat16),
            pltpu.VMEM((2 * quarter, 1024), jnp.bfloat16),
            pltpu.VMEM((quarter, 1024), jnp.bfloat16),
            pltpu.VMEM((9 * quarter, 1024), jnp.bfloat16),
            pltpu.VMEM(weight.shape, jnp.bfloat16),
            pltpu.VMEM(cotangent.shape, jnp.bfloat16),
        ),
        scratch_shapes=[
            pltpu.VMEM(feats.shape, jnp.bfloat16),
            pltpu.VMEM(voxmask.shape, jnp.int32),
            pltpu.VMEM((width, 1024), jnp.float32),
            pltpu.VMEM((quarter, 1024), jnp.float32),
            pltpu.SemaphoreType.DMA((9,)),
            pltpu.SemaphoreType.DMA((weight.shape[0] + 8,)),
        ],
        compiler_params=params(12),
        cost_estimate=cost(1024, 1024),
        name="prepare",
    )(far(feats), far(voxmask), far(weight), far(cotangent))


def turn_kernel(inner, core, both_changed, turned):
    quarter = core.shape[0]
    valid = windows((quarter, 128), 1)
    mine = aligned(me() % 2, quarter)
    for z in range(8):
        lanes = slice(128 * z, 128 * z + 128)
        for index, rows in enumerate((inner[mine, lanes], core[:, lanes], both_changed[mine, lanes])):
            first = 9 * quarter * index
            for place, moved in enumerate(shifts(rows.astype(jnp.float32), 1, valid)):
                turned[first + place * quarter : first + (place + 1) * quarter, lanes] = moved


def turn(inner, core, both_changed):
    quarter = core.shape[0]
    return pl.pallas_call(
        turn_kernel,
        in_specs=[WHOLE] * 3,
        out_specs=WHOLE,
        out_shape=pltpu.VMEM((27 * quarter, 1024), jnp.bfloat16),
        compiler_params=params(10),
        cost_estimate=cost(1024, 1024),
        name="turn",
    )(near(inner), near(core), near(both_changed))


def copy_picks(outer, table, parcels, picks, planes):
    for dev in range(4):
        planes[256 * dev : 256 * dev + 256, :] = parcels[dev][:256, :]
    for steps in range(outer):
        for slot in range(4):
            start = pl.multiple_of(table[steps * 4 + slot] * 64, 64)
            picks[steps][64 * slot : 64 * slot + 64, :] = planes[pl.ds(start, 64), :]


def route_kernel(outer, *refs):
    position = me()
    parcels, (table, *picks), (codes, links, planes, done) = refs[:4], refs[4:-4], refs[-4:]
    for dev in range(4):
        row = parcels[dev][256:272, :128].astype(jnp.float32)
        codes[8 * dev : 8 * dev + 8, :] = row[:8, :].astype(jnp.int32)
    copy = pltpu.make_async_copy(codes, links, done)
    copy.start()
    copy.wait()
    for place in range(outer * 4):
        table[place] = 0
        table[outer * 4 + 4 + place] = -1
    for plane in range(16):
        dev, side, brick = plane // 4, plane // 2 % 2, plane % 2
        dest = links[dev * 8, brick * 2 + side]

        @pl.when((dest >= 0) & ((dest // 2) % 4 == position % 4))
        def _():
            steps = lax.rem(dest // 8 - position // 4 + outer, outer)
            slot = dest % 2 + (0 if side == 1 else 2)
            table[steps * 4 + slot] = plane
            table[outer * 4 + 4 + ((dest // 8) ^ (position // 4)) * 4 + slot] = plane

    for brick in range(2):
        for side in range(2):
            dest = links[0, brick * 2 + side]
            steps = lax.rem(position // 4 - dest // 8 + outer, outer)
            table[outer * 4 + 2 * side + brick] = jnp.where(dest >= 0, steps, -1)

    copy_picks(outer, table, parcels, picks, planes)


def route(parcels, outer):
    width = parcels[0].shape[1]
    results = pl.pallas_call(
        functools.partial(route_kernel, outer),
        in_specs=[WHOLE] * 4,
        out_specs=[SCALARS] + [WHOLE] * outer,
        out_shape=[jax.ShapeDtypeStruct((outer * 8 + 4,), jnp.int32)]
        + [pltpu.VMEM((256, width), jnp.bfloat16)] * outer,
        scratch_shapes=[
            pltpu.VMEM((32, 128), jnp.int32),
            pltpu.SMEM((32, 128), jnp.int32),
            pltpu.VMEM((1024, width), jnp.bfloat16),
            pltpu.SemaphoreType.DMA(()),
        ],
        compiler_params=params(),
        cost_estimate=cost(1024, 1024),
        name="route",
    )(*[near(x) for x in parcels])
    return results[0], results[1:]


def deal_kernel(outer, table, *refs):
    parcels, (give, keep, planes) = refs[:4], refs[4:]
    for dev in range(4):
        planes[256 * dev : 256 * dev + 256, :] = parcels[dev][:256, :]
    for flip in range(outer):
        target = (give if flip % 2 else keep).at[flip // 2]
        for slot in range(4):
            plane = table[outer * 4 + 4 + flip * 4 + slot]
            rows = planes[aligned(jnp.maximum(plane, 0), 64), :]
            target[64 * slot : 64 * slot + 64, :] = jnp.where(plane >= 0, rows.astype(jnp.float32), 0.0).astype(jnp.bfloat16)
    total = sum(read_extra(ref) for ref in parcels)
    for ref in (give, keep):
        write_exact(total, ref.at[0])
        for index in range(1, outer // 2):
            ref[index, 256:272, :] = jnp.zeros((EXTRA, planes.shape[1]), jnp.bfloat16)


def deal(table, parcels, outer):
    width = parcels[0].shape[1]
    shape = pltpu.VMEM((outer // 2, 256 + EXTRA, width), jnp.bfloat16)
    return pl.pallas_call(
        functools.partial(deal_kernel, outer),
        in_specs=[SCALARS] + [WHOLE] * 4,
        out_specs=(WHOLE, WHOLE),
        out_shape=(shape, shape),
        scratch_shapes=[pltpu.VMEM((1024, width), jnp.bfloat16)],
        compiler_params=params(8),
        cost_estimate=cost(1024, 1024),
        name="deal",
    )(table, *[near(x) for x in parcels])


def merged(keep, got, index):
    planes = keep[index, :256, :].astype(jnp.float32) + got[index, :256, :].astype(jnp.float32)
    return planes


def merge_kernel(kept, got, give, keep):
    total = read_extra(kept.at[0]) + read_extra(got.at[0])
    for index in range(kept.shape[0]):
        target = (give if index % 2 else keep).at[index // 2]
        target[:256, :] = merged(kept, got, index).astype(jnp.bfloat16)
        target[256:272, :] = jnp.zeros((EXTRA, kept.shape[2]), jnp.bfloat16)
    for ref in (give, keep):
        write_exact(total, ref.at[0])


def merge(kept, got):
    shape = pltpu.VMEM((kept.shape[0] // 2, *kept.shape[1:]), jnp.bfloat16)
    return pl.pallas_call(
        merge_kernel,
        in_specs=[WHOLE, WHOLE],
        out_specs=(WHOLE, WHOLE),
        out_shape=(shape, shape),
        compiler_params=params(8),
        cost_estimate=cost(1024, 1024),
        name="merge",
    )(near(kept), near(got))


def chosen(table, slot, arrived):
    rows = slice(64 * slot, 64 * slot + 64)
    plane = jnp.zeros((64, arrived[0].shape[1]), jnp.float32)
    for steps, ref in enumerate(arrived):
        plane = jnp.where(table[4 * len(arrived) + slot] == steps, ref[rows, :].astype(jnp.float32), plane)
    return plane


def forward_kernel(rows, mask, weight, bias, slopes, out, grad, edge, bias_sum, cols, pre):
    width = rows.shape[1]
    valid = windows((128, width), 0)
    for z in range(8):
        span = slice(128 * z, 128 * z + 128)
        for place, moved in enumerate(shifts(rows[span, :].astype(jnp.float32), 0, valid)):
            cols[span, place * width : (place + 1) * width] = moved

    def taps(a):
        return weight[9 * a : 9 * a + 9].reshape(9 * width, width)

    pre[...] = jnp.dot(cols[...], taps(1), preferred_element_type=jnp.float32) + bias[...]
    pre[128:, :] += jnp.dot(cols[:896, :], taps(0), preferred_element_type=jnp.float32)
    pre[:896, :] += jnp.dot(cols[128:, :], taps(2), preferred_element_type=jnp.float32)
    for side in range(2):
        edge[side] = pre[896 * side : 896 * side + 128, :]
    total = jnp.zeros((1, width), jnp.float32)
    for z in range(1, 7):
        span = slice(128 * z, 128 * z + 128)
        act, slope = activate(pre[span, :], both(slopes, z).astype(jnp.float32), wide(mask[span, :]))
        for b in range(2):
            out[b, z] = act[64 * b : 64 * b + 64]
        grad[128 * (z - 1) : 128 * z, :] = slope
        total += jnp.sum(slope.astype(jnp.float32), axis=0, keepdims=True)
    bias_sum[...] = total


def forward_inside(rows, mask, weight, bias, cotangent):
    width = rows.shape[1]
    return pl.pallas_call(
        forward_kernel,
        in_specs=[WHOLE] * 5,
        out_specs=(WHOLE,) * 4,
        out_shape=(
            jax.ShapeDtypeStruct(cotangent.shape, jnp.bfloat16),
            pltpu.VMEM((768, width), jnp.bfloat16),
            pltpu.VMEM((2, 128, width), jnp.float32),
            pltpu.VMEM((1, width), jnp.float32),
        ),
        scratch_shapes=[
            pltpu.VMEM((1024, 9 * width), jnp.bfloat16),
            pltpu.VMEM((1024, width), jnp.float32),
        ],
        compiler_params=params(12),
        cost_estimate=cost(1024, 1024),
        name="forward_inside",
    )(near(rows), near(mask), near(weight), bias, near(cotangent))


def inner_terms_kernel(mine, others, *refs):
    grads, terms = refs[:4], refs[4]
    rows = mine.shape[0]
    for a in range(3):
        lanes = slice(128 * a, 128 * a + 768)
        total = jnp.dot(mine[:, lanes], grads[0][...], preferred_element_type=jnp.float32)
        for index in range(3):
            total += jnp.dot(
                others[index * rows : (index + 1) * rows, lanes], grads[index + 1][...], preferred_element_type=jnp.float32
            )
        terms[a * rows : (a + 1) * rows, :] = total


def inner_terms(mine, others, grads):
    rows, width = mine.shape[0], grads[0].shape[1]
    return pl.pallas_call(
        inner_terms_kernel,
        in_specs=[WHOLE] * 6,
        out_specs=WHOLE,
        out_shape=pltpu.VMEM((3 * rows, width), jnp.float32),
        compiler_params=params(10),
        cost_estimate=cost(1024, 1024),
        name="inner_terms",
    )(near(mine), near(others), *[near(x) for x in grads])


def edge_kernel(table, mask, weight, edge, ends, inner, out_in, *refs):
    arrived, (out, to_inner, to_core, own, planes, flip, done) = refs[:-7], refs[-7:]
    width = edge.shape[2]
    valid = windows((128, width), 0)
    total = inner[...]
    for side in range(2):
        rows = slice(128 * side, 128 * side + 128)
        halo = jnp.concatenate([chosen(table, 2 * side + b, arrived) for b in range(2)], axis=0)
        flip[:, rows] = halo.T
        cols = jnp.concatenate(shifts(halo, 0, valid), axis=1)
        taps = weight[18 * side : 18 * side + 9].reshape(9 * width, width)
        pre = edge[side] + jnp.dot(cols, taps, preferred_element_type=jnp.float32)
        z = 7 * side
        keep = wide(mask[128 * z : 128 * z + 128, :])
        act, slope = activate(pre, both(ends, z).astype(jnp.float32), keep)
        for b in range(2):
            planes[side, b, 0] = act[64 * b : 64 * b + 64]
        pltpu.make_async_copy(planes.at[side], out.at[:, pl.ds(z, 1)], done.at[side]).start()
        to_inner[rows, :] = slope
        to_core[rows, :] = slope
        total += jnp.sum(slope.astype(jnp.float32), axis=0, keepdims=True)
    write_exact(total, to_inner)
    write_exact(total, to_core)
    quarters(flip, own, to_inner.at[272:], to_core.at[272:])
    for side in range(2):
        pltpu.make_async_copy(planes.at[side], out.at[:, pl.ds(7 * side, 1)], done.at[side]).wait()


def forward_edges(table, mask, weight, edge, ends, inner, out, arrived):
    width = edge.shape[2]
    quarter = width // 4
    return pl.pallas_call(
        edge_kernel,
        in_specs=[SCALARS] + [WHOLE] * 5 + [FAR] + [WHOLE] * len(arrived),
        out_specs=(FAR, WHOLE, WHOLE, WHOLE),
        out_shape=(
            jax.ShapeDtypeStruct(out.shape, out.dtype),
            pltpu.VMEM((256 + EXTRA + 2 * quarter, width), jnp.bfloat16),
            pltpu.VMEM((256 + EXTRA + quarter, width), jnp.bfloat16),
            pltpu.VMEM((quarter, 256), jnp.bfloat16),
        ),
        scratch_shapes=[
            pltpu.VMEM((2, 2, 1, 64, width), jnp.bfloat16),
            pltpu.VMEM((width, 256), jnp.float32),
            pltpu.SemaphoreType.DMA((2,)),
        ],
        input_output_aliases={6: 0},
        compiler_params=params(10),
        cost_estimate=cost(1024, 1024),
        name="forward_edges",
    )(
        table,
        near(mask),
        near(weight),
        near(edge),
        near(ends),
        near(inner),
        out,
        *[near(x) for x in arrived],
    )


def outer_terms_kernel(outer, mine, others, halos, *refs):
    parcels, inner = refs[:4], refs[4]
    gives, stay, cols, total = refs[5 : 4 + outer], refs[4 + outer], refs[5 + outer], refs[6 + outer]
    quarter = halos.shape[0]
    rows = 9 * quarter
    valid = windows((quarter, 128), 1)
    half = aligned(me() % 2, quarter)
    ends = (
        halos,
        parcels[1].at[272 : 272 + 2 * quarter].at[half],
        parcels[2].at[272 : 272 + quarter],
        parcels[3].at[272 : 272 + 2 * quarter].at[half],
    )
    facing = jnp.concatenate(
        [parcel[128 * side : 128 * side + 128, :] for side in range(2) for parcel in parcels], axis=0
    )
    for a in range(3):
        for side in range(2):
            plane = a - 1 + 7 * side
            for who in range(4):
                lanes = slice(128 * (4 * side + who), 128 * (4 * side + who) + 128)
                if 0 <= plane < 8:
                    ref, first = (mine, 0) if who == 0 else (others, rows * (who - 1))
                    cols[:, lanes] = ref[first : first + rows, 128 * plane : 128 * plane + 128]
                else:
                    moved = shifts(ends[who][:, 128 * side : 128 * side + 128].astype(jnp.float32), 1, valid)
                    for place in range(9):
                        cols[place * quarter : (place + 1) * quarter, lanes] = moved[place]
        span = slice(a * rows, (a + 1) * rows)
        total[span, :] = inner[span, :] + jnp.dot(cols[...], facing, preferred_element_type=jnp.float32)
    if total.shape[0] > 3 * rows:
        total[3 * rows :, :] = jnp.zeros((total.shape[0] - 3 * rows, total.shape[1]), jnp.float32)
    z = me() // 4
    for steps in range(outer):
        block = lax.rem(z + steps, outer)
        for unit in range(units(outer)):
            piece = total[aligned(block + outer * unit, 16), :]
            if steps:
                gives[steps - 1][16 * unit : 16 * unit + 16, :] = piece.astype(jnp.bfloat16)
            else:
                stay[16 * unit : 16 * unit + 16, :] = piece


def outer_terms(outer, mine, others, halos, parcels, inner):
    width = inner.shape[1]
    rows = 16 * units(outer)
    results = pl.pallas_call(
        functools.partial(outer_terms_kernel, outer),
        in_specs=[WHOLE] * 8,
        out_specs=[WHOLE] * outer,
        out_shape=[pltpu.VMEM((rows, width), jnp.bfloat16)] * (outer - 1) + [pltpu.VMEM((rows, width), jnp.float32)],
        scratch_shapes=[
            pltpu.VMEM((inner.shape[0] // 3, 1024), jnp.bfloat16),
            pltpu.VMEM((outer * rows, width), jnp.float32),
        ],
        compiler_params=params(12),
        cost_estimate=cost(1024, 1024),
        name="outer_terms",
    )(*[near(x) for x in (mine, others, halos, *parcels, inner)])
    return results[:-1], results[-1]


def backward_kernel(grad, parcel, mask, weight, grad_feats, partial, near_weight, cols, total, fetched):
    width = grad.shape[1]
    fetch_taps(weight, near_weight, fetched)
    valid = windows((128, width), 0)
    planes = [parcel[:128, :]] + [grad[128 * z : 128 * z + 128, :] for z in range(6)] + [parcel[128:256, :]]
    for z, plane in enumerate(planes):
        for at, moved in enumerate(shifts(plane.astype(jnp.float32), 0, valid, -1)):
            cols[128 * z : 128 * z + 128, at * width : (at + 1) * width] = moved
    for a in (1, 0, 2):
        await_taps(9 * a, 9 * a + 9, weight, near_weight, fetched)
        first, start, count = ((128, 0, 896), (0, 0, 1024), (0, 128, 896))[a]
        for at in range(9):
            piece = lax.dot_general(
                cols[first : first + count, at * width : (at + 1) * width],
                near_weight[9 * a + at],
                (((1,), (1,)), ((), ())),
                preferred_element_type=jnp.float32,
            )
            if a == 1 and at == 0:
                total[...] = piece
            else:
                total[start : start + count, :] += piece
    for z in range(1, 7):
        rows = slice(128 * z, 128 * z + 128)
        done = jnp.where(wide(mask[rows, :]), total[rows, :], 0.0).astype(jnp.bfloat16)
        for b in range(2):
            grad_feats[b, z] = done[64 * b : 64 * b + 64]
    for side in range(2):
        partial[side] = total[896 * side : 896 * side + 128, :]


def backward(grad, parcel, mask, weight):
    width = grad.shape[1]
    return pl.pallas_call(
        backward_kernel,
        in_specs=[WHOLE] * 3 + [FAR],
        out_specs=(WHOLE,) * 3,
        out_shape=(
            jax.ShapeDtypeStruct((2, 8, 64, width), jnp.bfloat16),
            pltpu.VMEM((2, 128, width), jnp.float32),
            pltpu.VMEM(weight.shape, jnp.bfloat16),
        ),
        scratch_shapes=[
            pltpu.VMEM((1024, 9 * width), jnp.bfloat16),
            pltpu.VMEM((1024, width), jnp.float32),
            pltpu.SemaphoreType.DMA((weight.shape[0],)),
        ],
        compiler_params=params(16),
        cost_estimate=cost(1024, 1024),
        name="backward",
    )(near(grad), near(parcel), near(mask), far(weight))


def block_copies(outer, places, stacks, out, done):
    position = me()
    blocks = [ref.at[index] for ref in stacks for index in range(ref.shape[0])]
    copies = []
    for index, (ref, (flip, inner, core)) in enumerate(zip(blocks, places)):
        block = (position // 4) ^ flip
        quarter = 4 * ((position % 4) ^ (2 * inner + core))
        if outer == 4:
            copies.append((None, pltpu.make_async_copy(ref, out.at[:, quarter + block], done.at[index, 0])))
            continue
        for unit in range(units(outer)):
            place = block + outer * unit
            here = jnp.minimum(place, 107)
            target = out.at[here // 4, quarter + here % 4]
            copies.append((place < 108, pltpu.make_async_copy(ref.at[unit], target, done.at[index, unit])))
    return copies


def for_each(copies, wait):
    for condition, copy in copies:
        act = copy.wait if wait else copy.start
        if condition is None:
            act()
        else:
            pl.when(condition)(act)


def assemble_kernel(outer, places, count, *refs):
    out, done = refs[-2:]
    copies = block_copies(outer, places, refs[:count], out, done)
    for_each(copies, False)
    for_each(copies, True)


def in_units(stack, outer):
    return near(stack.reshape(stack.shape[0], units(outer), 16, stack.shape[-1]))


def assemble(outer, places, stacks, shape, given):
    before = [] if given is None else [given]
    return pl.pallas_call(
        functools.partial(assemble_kernel, outer, places, len(stacks)),
        in_specs=[WHOLE] * len(stacks) + [FAR] * len(before),
        out_specs=FAR,
        out_shape=jax.ShapeDtypeStruct(shape, jnp.bfloat16),
        scratch_shapes=[pltpu.SemaphoreType.DMA((len(places), units(outer)))],
        input_output_aliases={len(stacks): 0} if before else {},
        compiler_params=params(),
        cost_estimate=cost(1024, 1024),
        name="assemble",
    )(*[in_units(x, outer) for x in stacks], *before)


def finish_kernel(outer, places, partial, mask, weight, kept, got, stack, feats_in, weight_in, *refs):
    grad_feats, grad_weight, bias_sum, planes, sent, done = refs
    copies = block_copies(outer, places, [stack], grad_weight, done)
    for_each(copies, False)
    width = weight.shape[1]
    valid = windows((128, width), 0)
    halos = merged(kept, got, 0)
    for side in range(2):
        total = partial[side]
        for at, moved in enumerate(shifts(halos[128 * side : 128 * side + 128, :], 0, valid, -1)):
            total += lax.dot_general(
                moved,
                weight[18 * (1 - side) + at],
                (((1,), (1,)), ((), ())),
                preferred_element_type=jnp.float32,
            )
        rows = slice(896 * side, 896 * side + 128)
        done_rows = jnp.where(wide(mask[rows, :]), total, 0.0).astype(jnp.bfloat16)
        for b in range(2):
            planes[side, b, 0] = done_rows[64 * b : 64 * b + 64]
        pltpu.make_async_copy(planes.at[side], grad_feats.at[:, pl.ds(7 * side, 1)], sent.at[side]).start()
    bias_sum[...] = read_extra(kept.at[0]) + read_extra(got.at[0])
    for side in range(2):
        pltpu.make_async_copy(planes.at[side], grad_feats.at[:, pl.ds(7 * side, 1)], sent.at[side]).wait()
    for_each(copies, True)


def finish(outer, places, partial, mask, weight, kept, got, stack, grad_feats, grad_weight):
    width = weight.shape[1]
    return pl.pallas_call(
        functools.partial(finish_kernel, outer, places),
        in_specs=[WHOLE] * 6 + [FAR, FAR],
        out_specs=(FAR, FAR, WHOLE),
        out_shape=(
            jax.ShapeDtypeStruct(grad_feats.shape, grad_feats.dtype),
            jax.ShapeDtypeStruct(grad_weight.shape, grad_weight.dtype),
            jax.ShapeDtypeStruct((1, width), jnp.float32),
        ),
        scratch_shapes=[
            pltpu.VMEM((2, 2, 1, 64, width), jnp.bfloat16),
            pltpu.SemaphoreType.DMA((2,)),
            pltpu.SemaphoreType.DMA((len(places), units(outer))),
        ],
        input_output_aliases={6: 0, 7: 1},
        compiler_params=params(10),
        cost_estimate=cost(1024, 1024),
        name="finish",
    )(*[near(x) for x in (partial, mask, weight, kept, got)], in_units(stack, outer), grad_feats, grad_weight)


def per_device(size, feats, voxmask, links, weight, bias, cotangent):
    width = feats.shape[3]
    outer = size // 4

    parcel = rims(links, feats, voxmask)
    mask, rows, give_inner, give_core, turned, taps, ends = prepare(feats, voxmask, weight, cotangent)
    inner, rows = lax.optimization_barrier((swap(parcel, size, 2), rows))
    parcels = [parcel, inner, swap(parcel, size, 1), swap(inner, size, 1)]
    out, grad, edge, bias_local = forward_inside(rows, mask, taps, bias.reshape(1, width), ends)
    *parcels, grad = lax.optimization_barrier((*parcels, grad))
    table, picks = route(parcels, outer)

    *picks, give_core, grad = lax.optimization_barrier((*picks, give_core, grad))
    arrived = [rotate(pick, size, steps) if steps else pick for steps, pick in enumerate(picks)]
    got_inner = swap(give_inner, size, 2)
    got_inner, grad = lax.optimization_barrier((got_inner, grad))
    grad_inner = swap(grad, size, 2)
    *arrived, got_inner, grad_inner = lax.optimization_barrier((*arrived, got_inner, grad_inner))
    others = turn(got_inner, swap(give_core, size, 1), swap(got_inner, size, 1))
    grads = [grad, grad_inner, swap(grad, size, 1), swap(grad_inner, size, 1)]

    out, to_inner, to_core, halos = forward_edges(table, mask, taps, edge, ends, bias_local, out, arrived)
    inner = swap(to_inner, size, 2)
    terms = inner_terms(turned, others, grads)
    inner, terms = lax.optimization_barrier((inner, terms))
    parcels = [to_inner, inner, swap(to_core, size, 1), swap(inner, size, 1)]

    gives, stay = outer_terms(outer, turned, others, halos, parcels, terms)
    gots = [rotate(give, size, steps + 1) for steps, give in enumerate(gives)]
    give, kept = deal(table, parcels, outer)
    got = swap(give, size, 4)
    grad_feats, partial, taps = backward(grad, to_inner, mask, weight)
    bits = outer.bit_length() - 1
    for bit in range(1, bits):
        give, kept = merge(kept, got)
        if bit < bits - 1:
            got = swap(give, size, 4 << bit)
    stay, partial, give, kept = lax.optimization_barrier((stay, partial, give, kept))
    part = (stay + sum(got.astype(jnp.float32) for got in gots)).astype(jnp.bfloat16)

    def stack(*blocks):
        return jnp.concatenate([x.reshape(-1, *part.shape) for x in blocks])

    def place_blocks(keys, blocks, given):
        places = [(*key, core) for core in range(2) for key in keys]
        return assemble(outer, places, [blocks, swap(blocks, size, 1)], (27, 16, width // 16, width), given)

    last = outer - 1
    flips = list(range(1, last))
    blocks = [part]
    for flip in flips:
        blocks.append(swap(blocks[flip & (flip - 1)], size, 4 * (flip & -flip)))
    first_inner = swap(part, size, 2)
    middle = stack(*blocks[1:])
    farthest = swap(blocks[last & (last - 1)], size, 4)
    middle, give = lax.optimization_barrier((middle, give))
    middle_inner = swap(middle, size, 2)
    got = swap(give, size, 4 << (bits - 1))
    grad_weight = place_blocks([(0, 0), (0, 1)] + [(flip, 0) for flip in flips], stack(part, first_inner, middle), None)
    farthest_inner = swap(farthest, size, 2)
    middle_inner, farthest_inner, grad_weight, got = lax.optimization_barrier(
        (middle_inner, farthest_inner, grad_weight, got)
    )
    keys = [(flip, 1) for flip in flips] + [(last, 0), (last, 1)]
    rest = stack(middle_inner, farthest, farthest_inner)
    theirs = swap(rest, size, 1)
    grad_feats, grad_weight, grad_bias = finish(
        outer, [(*key, 0) for key in keys], partial, mask, taps, kept, got, rest, grad_feats, grad_weight
    )
    grad_weight = assemble(outer, [(*key, 1) for key in keys], [theirs], grad_weight.shape, grad_weight)
    return out, grad_feats, grad_weight.reshape(weight.shape), grad_bias.reshape(width)


def solution(mesh):
    return jax.shard_map(
        functools.partial(per_device, mesh.shape["zslab"]),
        mesh=mesh,
        in_specs=(
            P(("groups", "zslab"), None, None, None),
            P(("groups", "zslab"), None),
            P(("groups", "zslab"), None),
            P(),
            P(),
            P(("groups", "zslab"), None, None, None),
        ),
        out_specs=(
            P(("groups", "zslab"), None, None, None),
            P(("groups", "zslab"), None, None, None),
            P("groups", None, None),
            P("groups"),
        ),
        check_vma=False,
    )
```

```python
import functools

import jax
import jax.numpy as jnp
from jax import lax
from jax.experimental import pallas as pl
from jax.experimental.pallas import tpu as pltpu
from jax.sharding import PartitionSpec as P

EXTRA = 16


def params(mebibytes=6):
    return pltpu.CompilerParams(vmem_limit_bytes=mebibytes * 1024 * 1024)


def cost(flops, bytes_accessed):
    return pl.CostEstimate(flops=flops, bytes_accessed=bytes_accessed, transcendentals=0)


def near(x):
    return pltpu.with_memory_space_constraint(x, pltpu.VMEM)


def far(x):
    return pltpu.with_memory_space_constraint(x, pltpu.HBM)


SCALARS = pl.BlockSpec(memory_space=pltpu.SMEM)
WHOLE = pl.BlockSpec(memory_space=pltpu.VMEM)
FAR = pl.BlockSpec(memory_space=pl.ANY)


def swap(x, size, bit):
    return lax.ppermute(x, "zslab", [(i, i ^ bit) for i in range(size)])


def me():
    return lax.axis_index("zslab")


def units(outer):
    return -(-108 // outer)


def mask_rows(voxmask, z):
    lanes = slice(64 * z, 64 * z + 64)
    line = jnp.concatenate([voxmask[0:1, lanes], voxmask[1:2, lanes]], axis=1)
    return jnp.broadcast_to((line == 1).astype(jnp.float32), (128, 128)).T


def wide(mask):
    return jnp.concatenate([mask, mask], axis=1) > 0


def both(ref, z):
    return jnp.concatenate([ref[0, z], ref[1, z]], axis=0)


def inside(shape, dim, rows, cols):
    index = lax.broadcasted_iota(jnp.int32, shape, dim)
    row = (index // 8) % 8 + rows
    col = index % 8 + cols
    return (row >= 0) & (row < 8) & (col >= 0) & (col < 8)


def windows(shape, dim):
    return [inside(shape, dim, p, q) for p in (-1, 0, 1) for q in (-1, 0, 1)]


def shifts(x, dim, valid, sign=1):
    count = x.shape[dim]
    moved = []
    for place in range(9):
        at = place if sign == 1 else 8 - place
        move = 8 * (at // 3 - 1) + at % 3 - 1
        turned = pltpu.roll(x, (-move) % count, dim) if move else x
        moved.append(jnp.where(valid[at], turned, 0.0).astype(jnp.bfloat16))
    return moved


def activate(pre, cotangent, keep):
    sigma = 1.0 / (1.0 + jnp.exp(-pre))
    out = jnp.where(keep, pre * sigma, 0.0)
    grad = jnp.where(keep, cotangent * sigma * (1.0 + pre * (1.0 - sigma)), 0.0)
    return out.astype(jnp.bfloat16), grad.astype(jnp.bfloat16)


def write_exact(rows, ref):
    high = rows.astype(jnp.bfloat16)
    left = rows - high.astype(jnp.float32)
    middle = left.astype(jnp.bfloat16)
    low = (left - middle.astype(jnp.float32)).astype(jnp.bfloat16)
    zeros = jnp.zeros((EXTRA - 3, rows.shape[1]), jnp.float32)
    terms = [term.astype(jnp.float32) for term in (high, middle, low)]
    ref[256:272, :] = jnp.concatenate(terms + [zeros], axis=0).astype(jnp.bfloat16)


def read_extra(ref):
    return jnp.sum(ref[256:272, :].astype(jnp.float32), axis=0, keepdims=True)


def rims_kernel(links, feats, voxmask, parcel, planes, masks, codes, done):
    width = feats.shape[3]
    copies = [
        pltpu.make_async_copy(feats.at[:, pl.ds(0, 1)], planes.at[0], done.at[0]),
        pltpu.make_async_copy(feats.at[:, pl.ds(7, 1)], planes.at[1], done.at[1]),
        pltpu.make_async_copy(voxmask, masks, done.at[2]),
        pltpu.make_async_copy(links, codes, done.at[3]),
    ]
    for copy in copies:
        copy.start()
    for copy in copies:
        copy.wait()
    for side in range(2):
        keep = wide(mask_rows(masks, 7 * side))
        plane = jnp.concatenate([planes[side, 0, 0], planes[side, 1, 0]], axis=0).astype(jnp.float32)
        parcel[128 * side : 128 * side + 128, :] = jnp.where(keep, plane, 0.0).astype(jnp.bfloat16)
    lane = lax.broadcasted_iota(jnp.int32, (EXTRA, width), 1)
    row = jnp.zeros((EXTRA, width), jnp.float32)
    for place in range(4):
        row = jnp.where(lane == place, codes[place // 2, place % 2].astype(jnp.float32), row)
    parcel[256:272, :] = row.astype(jnp.bfloat16)


def rims(links, feats, voxmask):
    width = feats.shape[3]
    return pl.pallas_call(
        rims_kernel,
        in_specs=[FAR] * 3,
        out_specs=WHOLE,
        out_shape=pltpu.VMEM((256 + EXTRA, width), jnp.bfloat16),
        scratch_shapes=[
            pltpu.VMEM((2, 2, 1, 64, width), jnp.bfloat16),
            pltpu.VMEM(voxmask.shape, jnp.int32),
            pltpu.SMEM(links.shape, jnp.int32),
            pltpu.SemaphoreType.DMA((4,)),
        ],
        compiler_params=params(),
        cost_estimate=cost(1024, 1024),
        name="rims",
    )(far(links), far(feats), far(voxmask))


def fetch_taps(weight, near_weight, done):
    for tap in range(weight.shape[0]):
        pltpu.make_async_copy(weight.at[tap], near_weight.at[tap], done.at[tap]).start()


def await_taps(first, last, weight, near_weight, done):
    for tap in range(first, last):
        pltpu.make_async_copy(weight.at[tap], near_weight.at[tap], done.at[tap]).wait()


def aligned(index, rows):
    return pl.ds(pl.multiple_of(index * rows, rows), rows)


def quarters(flip, own, give_inner, give_core):
    position = me() % 4
    rows = flip.shape[0] // 4
    if own is not None:
        own[...] = flip[aligned(position, rows), :].astype(own.dtype)
    give_inner[...] = flip[aligned(1 - position // 2, 2 * rows), :].astype(jnp.bfloat16)
    give_core[...] = flip[aligned(position // 2 * 2 + 1 - position % 2, rows), :].astype(jnp.bfloat16)


def turn_rows(flip, lanes, valid, turned, first):
    rows = flip.shape[0]
    for place, moved in enumerate(shifts(flip[:, lanes].astype(jnp.float32), 1, valid)):
        turned[first + place * rows : first + (place + 1) * rows, lanes] = moved


def prepare_kernel(
    feats, voxmask, weight, cotangent, mask, rows, give_inner, give_core, turned, taps, slopes, planes, masks, flip, own, done, fetched
):
    count = weight.shape[0]
    pltpu.make_async_copy(voxmask, masks, done.at[8]).start()
    for z in range(8):
        pltpu.make_async_copy(feats.at[:, pl.ds(z, 1)], planes.at[:, pl.ds(z, 1)], done.at[z]).start()
    fetch_taps(weight, taps, fetched)
    for z in range(8):
        pltpu.make_async_copy(cotangent.at[:, pl.ds(z, 1)], slopes.at[:, pl.ds(z, 1)], fetched.at[count + z]).start()
    valid = windows((own.shape[0], 128), 1)
    pltpu.make_async_copy(voxmask, masks, done.at[8]).wait()
    for z in range(8):
        pltpu.make_async_copy(feats.at[:, pl.ds(z, 1)], planes.at[:, pl.ds(z, 1)], done.at[z]).wait()
        span = slice(128 * z, 128 * z + 128)
        keep = mask_rows(masks, z)
        mask[span, :] = keep
        plane = jnp.where(wide(keep), both(planes, z).astype(jnp.float32), 0.0)
        rows[span, :] = plane.astype(jnp.bfloat16)
        flip[:, span] = plane.T
    quarters(flip, own, give_inner, give_core)
    for z in range(8):
        turn_rows(own, slice(128 * z, 128 * z + 128), valid, turned, 0)
    await_taps(0, count, weight, taps, fetched)
    for z in range(8):
        pltpu.make_async_copy(cotangent.at[:, pl.ds(z, 1)], slopes.at[:, pl.ds(z, 1)], fetched.at[count + z]).wait()


def prepare(feats, voxmask, weight, cotangent):
    width = feats.shape[3]
    quarter = width // 4
    return pl.pallas_call(
        prepare_kernel,
        in_specs=[FAR] * 4,
        out_specs=(WHOLE,) * 7,
        out_shape=(
            pltpu.VMEM((1024, 128), jnp.float32),
            pltpu.VMEM((1024, width), jnp.bfloat16),
            pltpu.VMEM((2 * quarter, 1024), jnp.bfloat16),
            pltpu.VMEM((quarter, 1024), jnp.bfloat16),
            pltpu.VMEM((9 * quarter, 1024), jnp.bfloat16),
            pltpu.VMEM(weight.shape, jnp.bfloat16),
            pltpu.VMEM(cotangent.shape, jnp.bfloat16),
        ),
        scratch_shapes=[
            pltpu.VMEM(feats.shape, jnp.bfloat16),
            pltpu.VMEM(voxmask.shape, jnp.int32),
            pltpu.VMEM((width, 1024), jnp.float32),
            pltpu.VMEM((quarter, 1024), jnp.float32),
            pltpu.SemaphoreType.DMA((9,)),
            pltpu.SemaphoreType.DMA((weight.shape[0] + 8,)),
        ],
        compiler_params=params(12),
        cost_estimate=cost(1024, 1024),
        name="prepare",
    )(far(feats), far(voxmask), far(weight), far(cotangent))


def turn_kernel(inner, core, both_changed, turned):
    quarter = core.shape[0]
    valid = windows((quarter, 128), 1)
    mine = aligned(me() % 2, quarter)
    for z in range(8):
        lanes = slice(128 * z, 128 * z + 128)
        for index, rows in enumerate((inner[mine, lanes], core[:, lanes], both_changed[mine, lanes])):
            first = 9 * quarter * index
            for place, moved in enumerate(shifts(rows.astype(jnp.float32), 1, valid)):
                turned[first + place * quarter : first + (place + 1) * quarter, lanes] = moved


def turn(inner, core, both_changed):
    quarter = core.shape[0]
    return pl.pallas_call(
        turn_kernel,
        in_specs=[WHOLE] * 3,
        out_specs=WHOLE,
        out_shape=pltpu.VMEM((27 * quarter, 1024), jnp.bfloat16),
        compiler_params=params(10),
        cost_estimate=cost(1024, 1024),
        name="turn",
    )(near(inner), near(core), near(both_changed))


def route_kernel(outer, *refs):
    position = me()
    parcels, (table, *picks), (codes, links, planes, done) = refs[:4], refs[4:-4], refs[-4:]
    for dev in range(4):
        row = parcels[dev][256:272, :128].astype(jnp.float32)
        codes[8 * dev : 8 * dev + 8, :] = row[:8, :].astype(jnp.int32)
    copy = pltpu.make_async_copy(codes, links, done)
    copy.start()
    for dev in range(4):
        planes[256 * dev : 256 * dev + 256, :] = parcels[dev][:256, :]
    for place in range(outer * 4):
        table[place] = -1
    copy.wait()
    for plane in range(16):
        dev, side, brick = plane // 4, plane // 2 % 2, plane % 2
        dest = links[dev * 8, brick * 2 + side]

        @pl.when((dest >= 0) & ((dest // 2) % 4 == position % 4))
        def _():
            flip = (dest // 8) ^ (position // 4)
            table[flip * 4 + dest % 2 + (0 if side == 1 else 2)] = plane

    for brick in range(2):
        for side in range(2):
            dest = links[0, brick * 2 + side]
            table[outer * 4 + 2 * side + brick] = jnp.where(dest >= 0, (dest // 8) ^ (position // 4), -1)
    for flip in range(outer):
        for slot in range(4):
            plane = jnp.maximum(table[flip * 4 + slot], 0)
            picks[flip][64 * slot : 64 * slot + 64, :] = planes[aligned(plane, 64), :]


def route(parcels, outer):
    width = parcels[0].shape[1]
    results = pl.pallas_call(
        functools.partial(route_kernel, outer),
        in_specs=[WHOLE] * 4,
        out_specs=[SCALARS] + [WHOLE] * outer,
        out_shape=[jax.ShapeDtypeStruct((outer * 4 + 4,), jnp.int32)]
        + [pltpu.VMEM((256, width), jnp.bfloat16)] * outer,
        scratch_shapes=[
            pltpu.VMEM((32, 128), jnp.int32),
            pltpu.SMEM((32, 128), jnp.int32),
            pltpu.VMEM((1024, width), jnp.bfloat16),
            pltpu.SemaphoreType.DMA(()),
        ],
        compiler_params=params(),
        cost_estimate=cost(1024, 1024),
        name="route",
    )(*[near(x) for x in parcels])
    return results[0], results[1:]


def deal_kernel(outer, table, *refs):
    parcels, (give, keep, planes) = refs[:4], refs[4:]
    for dev in range(4):
        planes[256 * dev : 256 * dev + 256, :] = parcels[dev][:256, :]
    for flip in range(outer):
        target = (give if flip % 2 else keep).at[flip // 2]
        for slot in range(4):
            plane = table[flip * 4 + slot]
            rows = planes[aligned(jnp.maximum(plane, 0), 64), :]
            target[64 * slot : 64 * slot + 64, :] = jnp.where(plane >= 0, rows.astype(jnp.float32), 0.0).astype(jnp.bfloat16)
    total = sum(read_extra(ref) for ref in parcels)
    for ref in (give, keep):
        write_exact(total, ref.at[0])
        for index in range(1, outer // 2):
            ref[index, 256:272, :] = jnp.zeros((EXTRA, planes.shape[1]), jnp.bfloat16)


def deal(table, parcels, outer):
    width = parcels[0].shape[1]
    shape = pltpu.VMEM((outer // 2, 256 + EXTRA, width), jnp.bfloat16)
    return pl.pallas_call(
        functools.partial(deal_kernel, outer),
        in_specs=[SCALARS] + [WHOLE] * 4,
        out_specs=(WHOLE, WHOLE),
        out_shape=(shape, shape),
        scratch_shapes=[pltpu.VMEM((1024, width), jnp.bfloat16)],
        compiler_params=params(8),
        cost_estimate=cost(1024, 1024),
        name="deal",
    )(table, *[near(x) for x in parcels])


def merged(keep, got, index):
    planes = keep[index, :256, :].astype(jnp.float32) + got[index, :256, :].astype(jnp.float32)
    return planes


def merge_kernel(kept, got, give, keep):
    total = read_extra(kept.at[0]) + read_extra(got.at[0])
    for index in range(kept.shape[0]):
        target = (give if index % 2 else keep).at[index // 2]
        target[:256, :] = merged(kept, got, index).astype(jnp.bfloat16)
        target[256:272, :] = jnp.zeros((EXTRA, kept.shape[2]), jnp.bfloat16)
    for ref in (give, keep):
        write_exact(total, ref.at[0])


def merge(kept, got):
    shape = pltpu.VMEM((kept.shape[0] // 2, *kept.shape[1:]), jnp.bfloat16)
    return pl.pallas_call(
        merge_kernel,
        in_specs=[WHOLE, WHOLE],
        out_specs=(WHOLE, WHOLE),
        out_shape=(shape, shape),
        compiler_params=params(8),
        cost_estimate=cost(1024, 1024),
        name="merge",
    )(near(kept), near(got))


def chosen(table, slot, arrived):
    rows = slice(64 * slot, 64 * slot + 64)
    plane = jnp.zeros((64, arrived[0].shape[1]), jnp.float32)
    for flip, ref in enumerate(arrived):
        plane = jnp.where(table[4 * len(arrived) + slot] == flip, ref[rows, :].astype(jnp.float32), plane)
    return plane


def forward_kernel(rows, mask, weight, bias, slopes, out, grad, edge, bias_sum, cols, pre):
    width = rows.shape[1]
    valid = windows((128, width), 0)
    for z in range(8):
        span = slice(128 * z, 128 * z + 128)
        for place, moved in enumerate(shifts(rows[span, :].astype(jnp.float32), 0, valid)):
            cols[span, place * width : (place + 1) * width] = moved

    def taps(a):
        return weight[9 * a : 9 * a + 9].reshape(9 * width, width)

    pre[...] = jnp.dot(cols[...], taps(1), preferred_element_type=jnp.float32) + bias[...]
    pre[128:, :] += jnp.dot(cols[:896, :], taps(0), preferred_element_type=jnp.float32)
    pre[:896, :] += jnp.dot(cols[128:, :], taps(2), preferred_element_type=jnp.float32)
    for side in range(2):
        edge[side] = pre[896 * side : 896 * side + 128, :]
    total = jnp.zeros((1, width), jnp.float32)
    for z in range(1, 7):
        span = slice(128 * z, 128 * z + 128)
        act, slope = activate(pre[span, :], both(slopes, z).astype(jnp.float32), wide(mask[span, :]))
        for b in range(2):
            out[b, z] = act[64 * b : 64 * b + 64]
        grad[128 * (z - 1) : 128 * z, :] = slope
        total += jnp.sum(slope.astype(jnp.float32), axis=0, keepdims=True)
    bias_sum[...] = total


def forward_inside(rows, mask, weight, bias, cotangent):
    width = rows.shape[1]
    return pl.pallas_call(
        forward_kernel,
        in_specs=[WHOLE] * 5,
        out_specs=(WHOLE,) * 4,
        out_shape=(
            jax.ShapeDtypeStruct(cotangent.shape, jnp.bfloat16),
            pltpu.VMEM((768, width), jnp.bfloat16),
            pltpu.VMEM((2, 128, width), jnp.float32),
            pltpu.VMEM((1, width), jnp.float32),
        ),
        scratch_shapes=[
            pltpu.VMEM((1024, 9 * width), jnp.bfloat16),
            pltpu.VMEM((1024, width), jnp.float32),
        ],
        compiler_params=params(12),
        cost_estimate=cost(1024, 1024),
        name="forward_inside",
    )(near(rows), near(mask), near(weight), bias, near(cotangent))


def inner_terms_kernel(mine, others, *refs):
    grads, terms = refs[:4], refs[4]
    rows = mine.shape[0]
    for a in range(3):
        lanes = slice(128 * a, 128 * a + 768)
        total = jnp.dot(mine[:, lanes], grads[0][...], preferred_element_type=jnp.float32)
        for index in range(3):
            total += jnp.dot(
                others[index * rows : (index + 1) * rows, lanes], grads[index + 1][...], preferred_element_type=jnp.float32
            )
        terms[a * rows : (a + 1) * rows, :] = total


def inner_terms(mine, others, grads):
    rows, width = mine.shape[0], grads[0].shape[1]
    return pl.pallas_call(
        inner_terms_kernel,
        in_specs=[WHOLE] * 6,
        out_specs=WHOLE,
        out_shape=pltpu.VMEM((3 * rows, width), jnp.float32),
        compiler_params=params(10),
        cost_estimate=cost(1024, 1024),
        name="inner_terms",
    )(near(mine), near(others), *[near(x) for x in grads])


def edge_kernel(table, mask, weight, edge, ends, inner, out_in, *refs):
    arrived, (out, to_inner, to_core, own, planes, flip, done) = refs[:-7], refs[-7:]
    width = edge.shape[2]
    valid = windows((128, width), 0)
    total = inner[...]
    for side in range(2):
        rows = slice(128 * side, 128 * side + 128)
        halo = jnp.concatenate([chosen(table, 2 * side + b, arrived) for b in range(2)], axis=0)
        flip[:, rows] = halo.T
        cols = jnp.concatenate(shifts(halo, 0, valid), axis=1)
        taps = weight[18 * side : 18 * side + 9].reshape(9 * width, width)
        pre = edge[side] + jnp.dot(cols, taps, preferred_element_type=jnp.float32)
        z = 7 * side
        keep = wide(mask[128 * z : 128 * z + 128, :])
        act, slope = activate(pre, both(ends, z).astype(jnp.float32), keep)
        for b in range(2):
            planes[side, b, 0] = act[64 * b : 64 * b + 64]
        pltpu.make_async_copy(planes.at[side], out.at[:, pl.ds(z, 1)], done.at[side]).start()
        to_inner[rows, :] = slope
        to_core[rows, :] = slope
        total += jnp.sum(slope.astype(jnp.float32), axis=0, keepdims=True)
    write_exact(total, to_inner)
    write_exact(total, to_core)
    quarters(flip, own, to_inner.at[272:], to_core.at[272:])
    for side in range(2):
        pltpu.make_async_copy(planes.at[side], out.at[:, pl.ds(7 * side, 1)], done.at[side]).wait()


def forward_edges(table, mask, weight, edge, ends, inner, out, arrived):
    width = edge.shape[2]
    quarter = width // 4
    return pl.pallas_call(
        edge_kernel,
        in_specs=[SCALARS] + [WHOLE] * 5 + [FAR] + [WHOLE] * len(arrived),
        out_specs=(FAR, WHOLE, WHOLE, WHOLE),
        out_shape=(
            jax.ShapeDtypeStruct(out.shape, out.dtype),
            pltpu.VMEM((256 + EXTRA + 2 * quarter, width), jnp.bfloat16),
            pltpu.VMEM((256 + EXTRA + quarter, width), jnp.bfloat16),
            pltpu.VMEM((quarter, 256), jnp.bfloat16),
        ),
        scratch_shapes=[
            pltpu.VMEM((2, 2, 1, 64, width), jnp.bfloat16),
            pltpu.VMEM((width, 256), jnp.float32),
            pltpu.SemaphoreType.DMA((2,)),
        ],
        input_output_aliases={6: 0},
        compiler_params=params(10),
        cost_estimate=cost(1024, 1024),
        name="forward_edges",
    )(
        table,
        near(mask),
        near(weight),
        near(edge),
        near(ends),
        near(inner),
        out,
        *[near(x) for x in arrived],
    )


def outer_terms_kernel(outer, mine, others, halos, *refs):
    parcels, inner = refs[:4], refs[4]
    gives, stay, cols, total = refs[5 : 4 + outer], refs[4 + outer], refs[5 + outer], refs[6 + outer]
    quarter = halos.shape[0]
    rows = 9 * quarter
    valid = windows((quarter, 128), 1)
    half = aligned(me() % 2, quarter)
    ends = (
        halos,
        parcels[1].at[272 : 272 + 2 * quarter].at[half],
        parcels[2].at[272 : 272 + quarter],
        parcels[3].at[272 : 272 + 2 * quarter].at[half],
    )
    facing = jnp.concatenate(
        [parcel[128 * side : 128 * side + 128, :] for side in range(2) for parcel in parcels], axis=0
    )
    for a in range(3):
        for side in range(2):
            plane = a - 1 + 7 * side
            for who in range(4):
                lanes = slice(128 * (4 * side + who), 128 * (4 * side + who) + 128)
                if 0 <= plane < 8:
                    ref, first = (mine, 0) if who == 0 else (others, rows * (who - 1))
                    cols[:, lanes] = ref[first : first + rows, 128 * plane : 128 * plane + 128]
                else:
                    moved = shifts(ends[who][:, 128 * side : 128 * side + 128].astype(jnp.float32), 1, valid)
                    for place in range(9):
                        cols[place * quarter : (place + 1) * quarter, lanes] = moved[place]
        span = slice(a * rows, (a + 1) * rows)
        total[span, :] = inner[span, :] + jnp.dot(cols[...], facing, preferred_element_type=jnp.float32)
    if total.shape[0] > 3 * rows:
        total[3 * rows :, :] = jnp.zeros((total.shape[0] - 3 * rows, total.shape[1]), jnp.float32)
    for flip in range(outer):
        block = (me() // 4) ^ flip
        for unit in range(units(outer)):
            piece = total[aligned(block + outer * unit, 16), :]
            if flip:
                gives[flip - 1][16 * unit : 16 * unit + 16, :] = piece.astype(jnp.bfloat16)
            else:
                stay[16 * unit : 16 * unit + 16, :] = piece


def outer_terms(outer, mine, others, halos, parcels, inner):
    width = inner.shape[1]
    rows = 16 * units(outer)
    results = pl.pallas_call(
        functools.partial(outer_terms_kernel, outer),
        in_specs=[WHOLE] * 8,
        out_specs=[WHOLE] * outer,
        out_shape=[pltpu.VMEM((rows, width), jnp.bfloat16)] * (outer - 1) + [pltpu.VMEM((rows, width), jnp.float32)],
        scratch_shapes=[
            pltpu.VMEM((inner.shape[0] // 3, 1024), jnp.bfloat16),
            pltpu.VMEM((outer * rows, width), jnp.float32),
        ],
        compiler_params=params(12),
        cost_estimate=cost(1024, 1024),
        name="outer_terms",
    )(*[near(x) for x in (mine, others, halos, *parcels, inner)])
    return results[:-1], results[-1]


def backward_kernel(grad, parcel, mask, weight, grad_feats, partial, near_weight, cols, total, fetched):
    width = grad.shape[1]
    fetch_taps(weight, near_weight, fetched)
    valid = windows((128, width), 0)
    planes = [parcel[:128, :]] + [grad[128 * z : 128 * z + 128, :] for z in range(6)] + [parcel[128:256, :]]
    for z, plane in enumerate(planes):
        for at, moved in enumerate(shifts(plane.astype(jnp.float32), 0, valid, -1)):
            cols[128 * z : 128 * z + 128, at * width : (at + 1) * width] = moved
    for a in (1, 0, 2):
        await_taps(9 * a, 9 * a + 9, weight, near_weight, fetched)
        first, start, count = ((128, 0, 896), (0, 0, 1024), (0, 128, 896))[a]
        for at in range(9):
            piece = lax.dot_general(
                cols[first : first + count, at * width : (at + 1) * width],
                near_weight[9 * a + at],
                (((1,), (1,)), ((), ())),
                preferred_element_type=jnp.float32,
            )
            if a == 1 and at == 0:
                total[...] = piece
            else:
                total[start : start + count, :] += piece
    for z in range(1, 7):
        rows = slice(128 * z, 128 * z + 128)
        done = jnp.where(wide(mask[rows, :]), total[rows, :], 0.0).astype(jnp.bfloat16)
        for b in range(2):
            grad_feats[b, z] = done[64 * b : 64 * b + 64]
    for side in range(2):
        partial[side] = total[896 * side : 896 * side + 128, :]


def backward(grad, parcel, mask, weight):
    width = grad.shape[1]
    return pl.pallas_call(
        backward_kernel,
        in_specs=[WHOLE] * 3 + [FAR],
        out_specs=(WHOLE,) * 3,
        out_shape=(
            jax.ShapeDtypeStruct((2, 8, 64, width), jnp.bfloat16),
            pltpu.VMEM((2, 128, width), jnp.float32),
            pltpu.VMEM(weight.shape, jnp.bfloat16),
        ),
        scratch_shapes=[
            pltpu.VMEM((1024, 9 * width), jnp.bfloat16),
            pltpu.VMEM((1024, width), jnp.float32),
            pltpu.SemaphoreType.DMA((weight.shape[0],)),
        ],
        compiler_params=params(16),
        cost_estimate=cost(1024, 1024),
        name="backward",
    )(near(grad), near(parcel), near(mask), far(weight))


def block_copies(outer, places, stacks, out, done):
    position = me()
    blocks = [ref.at[index] for ref in stacks for index in range(ref.shape[0])]
    copies = []
    for index, (ref, (flip, inner, core)) in enumerate(zip(blocks, places)):
        block = (position // 4) ^ flip
        quarter = 4 * ((position % 4) ^ (2 * inner + core))
        if outer == 4:
            copies.append((None, pltpu.make_async_copy(ref, out.at[:, quarter + block], done.at[index, 0])))
            continue
        for unit in range(units(outer)):
            place = block + outer * unit
            here = jnp.minimum(place, 107)
            target = out.at[here // 4, quarter + here % 4]
            copies.append((place < 108, pltpu.make_async_copy(ref.at[unit], target, done.at[index, unit])))
    return copies


def for_each(copies, wait):
    for condition, copy in copies:
        act = copy.wait if wait else copy.start
        if condition is None:
            act()
        else:
            pl.when(condition)(act)


def assemble_kernel(outer, places, count, *refs):
    out, done = refs[-2:]
    copies = block_copies(outer, places, refs[:count], out, done)
    for_each(copies, False)
    for_each(copies, True)


def in_units(stack, outer):
    return near(stack.reshape(stack.shape[0], units(outer), 16, stack.shape[-1]))


def assemble(outer, places, stacks, shape, given):
    before = [] if given is None else [given]
    return pl.pallas_call(
        functools.partial(assemble_kernel, outer, places, len(stacks)),
        in_specs=[WHOLE] * len(stacks) + [FAR] * len(before),
        out_specs=FAR,
        out_shape=jax.ShapeDtypeStruct(shape, jnp.bfloat16),
        scratch_shapes=[pltpu.SemaphoreType.DMA((len(places), units(outer)))],
        input_output_aliases={len(stacks): 0} if before else {},
        compiler_params=params(),
        cost_estimate=cost(1024, 1024),
        name="assemble",
    )(*[in_units(x, outer) for x in stacks], *before)


def finish_kernel(outer, places, partial, mask, weight, kept, got, stack, feats_in, weight_in, *refs):
    grad_feats, grad_weight, bias_sum, planes, sent, done = refs
    copies = block_copies(outer, places, [stack], grad_weight, done)
    for_each(copies, False)
    width = weight.shape[1]
    valid = windows((128, width), 0)
    halos = merged(kept, got, 0)
    for side in range(2):
        total = partial[side]
        for at, moved in enumerate(shifts(halos[128 * side : 128 * side + 128, :], 0, valid, -1)):
            total += lax.dot_general(
                moved,
                weight[18 * (1 - side) + at],
                (((1,), (1,)), ((), ())),
                preferred_element_type=jnp.float32,
            )
        rows = slice(896 * side, 896 * side + 128)
        done_rows = jnp.where(wide(mask[rows, :]), total, 0.0).astype(jnp.bfloat16)
        for b in range(2):
            planes[side, b, 0] = done_rows[64 * b : 64 * b + 64]
        pltpu.make_async_copy(planes.at[side], grad_feats.at[:, pl.ds(7 * side, 1)], sent.at[side]).start()
    bias_sum[...] = read_extra(kept.at[0]) + read_extra(got.at[0])
    for side in range(2):
        pltpu.make_async_copy(planes.at[side], grad_feats.at[:, pl.ds(7 * side, 1)], sent.at[side]).wait()
    for_each(copies, True)


def finish(outer, places, partial, mask, weight, kept, got, stack, grad_feats, grad_weight):
    width = weight.shape[1]
    return pl.pallas_call(
        functools.partial(finish_kernel, outer, places),
        in_specs=[WHOLE] * 6 + [FAR, FAR],
        out_specs=(FAR, FAR, WHOLE),
        out_shape=(
            jax.ShapeDtypeStruct(grad_feats.shape, grad_feats.dtype),
            jax.ShapeDtypeStruct(grad_weight.shape, grad_weight.dtype),
            jax.ShapeDtypeStruct((1, width), jnp.float32),
        ),
        scratch_shapes=[
            pltpu.VMEM((2, 2, 1, 64, width), jnp.bfloat16),
            pltpu.SemaphoreType.DMA((2,)),
            pltpu.SemaphoreType.DMA((len(places), units(outer))),
        ],
        input_output_aliases={6: 0, 7: 1},
        compiler_params=params(10),
        cost_estimate=cost(1024, 1024),
        name="finish",
    )(*[near(x) for x in (partial, mask, weight, kept, got)], in_units(stack, outer), grad_feats, grad_weight)


def per_device(size, feats, voxmask, links, weight, bias, cotangent):
    width = feats.shape[3]
    outer = size // 4

    parcel = rims(links, feats, voxmask)
    mask, rows, give_inner, give_core, turned, taps, ends = prepare(feats, voxmask, weight, cotangent)
    inner, rows = lax.optimization_barrier((swap(parcel, size, 2), rows))
    parcels = [parcel, inner, swap(parcel, size, 1), swap(inner, size, 1)]
    out, grad, edge, bias_local = forward_inside(rows, mask, taps, bias.reshape(1, width), ends)
    *parcels, grad = lax.optimization_barrier((*parcels, grad))
    table, picks = route(parcels, outer)

    *picks, give_core, grad = lax.optimization_barrier((*picks, give_core, grad))
    arrived = [swap(pick, size, 4 * flip) if flip else pick for flip, pick in enumerate(picks)]
    got_inner = swap(give_inner, size, 2)
    got_inner, grad = lax.optimization_barrier((got_inner, grad))
    grad_inner = swap(grad, size, 2)
    *arrived, got_inner, grad_inner = lax.optimization_barrier((*arrived, got_inner, grad_inner))
    others = turn(got_inner, swap(give_core, size, 1), swap(got_inner, size, 1))
    grads = [grad, grad_inner, swap(grad, size, 1), swap(grad_inner, size, 1)]

    out, to_inner, to_core, halos = forward_edges(table, mask, taps, edge, ends, bias_local, out, arrived)
    inner = swap(to_inner, size, 2)
    terms = inner_terms(turned, others, grads)
    inner, terms = lax.optimization_barrier((inner, terms))
    parcels = [to_inner, inner, swap(to_core, size, 1), swap(inner, size, 1)]

    gives, stay = outer_terms(outer, turned, others, halos, parcels, terms)
    give, kept = deal(table, parcels, outer)
    give, *gives = lax.optimization_barrier((give, *gives))
    gots = [swap(x, size, 4 * flip) for flip, x in enumerate(gives, 1)]
    got = swap(give, size, 4)
    grad_feats, partial, taps = backward(grad, to_inner, mask, weight)
    bits = outer.bit_length() - 1
    for bit in range(1, bits):
        give, kept = merge(kept, got)
        if bit < bits - 1:
            got = swap(give, size, 4 << bit)
    stay, partial, give, kept = lax.optimization_barrier((stay, partial, give, kept))
    part = (stay + sum(got.astype(jnp.float32) for got in gots)).astype(jnp.bfloat16)

    def stack(*blocks):
        return jnp.concatenate([x.reshape(-1, *part.shape) for x in blocks])

    def place_blocks(keys, blocks, given):
        places = [(*key, core) for core in range(2) for key in keys]
        return assemble(outer, places, [blocks, swap(blocks, size, 1)], (27, 16, width // 16, width), given)

    last = outer - 1
    flips = list(range(1, last))
    blocks = [part]
    for flip in flips:
        blocks.append(swap(blocks[flip & (flip - 1)], size, 4 * (flip & -flip)))
    first_inner = swap(part, size, 2)
    near_inner = swap(first_inner, size, 4)
    upper, give = lax.optimization_barrier((stack(*blocks[2:]), give))
    upper_inner = swap(upper, size, 2)
    farthest = swap(blocks[last & (last - 1)], size, 4)
    got = swap(give, size, 4 << (bits - 1))
    farthest, got = lax.optimization_barrier((farthest, got))
    farthest_inner = swap(farthest, size, 2)
    grad_weight = place_blocks([(0, 0), (0, 1)] + [(flip, 0) for flip in flips], stack(part, first_inner, *blocks[1:]), None)
    keys = [(1, 1)] + [(flip, 1) for flip in flips[1:]] + [(last, 0)]
    grad_weight = place_blocks(keys, stack(near_inner, upper_inner, farthest), grad_weight)
    farthest_inner, grad_weight = lax.optimization_barrier((farthest_inner, grad_weight))
    rest = stack(farthest_inner)
    theirs = swap(rest, size, 1)
    grad_feats, grad_weight, grad_bias = finish(
        outer, [(last, 1, 0)], partial, mask, taps, kept, got, rest, grad_feats, grad_weight
    )
    grad_weight = assemble(outer, [(last, 1, 1)], [theirs], grad_weight.shape, grad_weight)
    return out, grad_feats, grad_weight.reshape(weight.shape), grad_bias.reshape(width)


def solution(mesh):
    return jax.shard_map(
        functools.partial(per_device, mesh.shape["zslab"]),
        mesh=mesh,
        in_specs=(
            P(("groups", "zslab"), None, None, None),
            P(("groups", "zslab"), None),
            P(("groups", "zslab"), None),
            P(),
            P(),
            P(("groups", "zslab"), None, None, None),
        ),
        out_specs=(
            P(("groups", "zslab"), None, None, None),
            P(("groups", "zslab"), None, None, None),
            P("groups", None, None),
            P("groups"),
        ),
        check_vma=False,
    )
```

```python
import functools

import jax
import jax.numpy as jnp
from jax import lax
from jax.experimental import pallas as pl
from jax.experimental.pallas import tpu as pltpu
from jax.sharding import PartitionSpec as P

EXTRA = 16


def params(mebibytes=6):
    return pltpu.CompilerParams(vmem_limit_bytes=mebibytes * 1024 * 1024)


def cost(flops, bytes_accessed):
    return pl.CostEstimate(flops=flops, bytes_accessed=bytes_accessed, transcendentals=0)


def near(x):
    return pltpu.with_memory_space_constraint(x, pltpu.VMEM)


def far(x):
    return pltpu.with_memory_space_constraint(x, pltpu.HBM)


SCALARS = pl.BlockSpec(memory_space=pltpu.SMEM)
WHOLE = pl.BlockSpec(memory_space=pltpu.VMEM)
FAR = pl.BlockSpec(memory_space=pl.ANY)


def swap(x, size, bit):
    return lax.ppermute(x, "zslab", [(i, i ^ bit) for i in range(size)])


def rotate(x, size, steps):
    return lax.ppermute(x, "zslab", [(i, (i + 4 * steps) % size) for i in range(size)])


def me():
    return lax.axis_index("zslab")


def units(outer):
    return -(-108 // outer)


def mask_rows(voxmask, z):
    lanes = slice(64 * z, 64 * z + 64)
    line = jnp.concatenate([voxmask[0:1, lanes], voxmask[1:2, lanes]], axis=1)
    return jnp.broadcast_to((line == 1).astype(jnp.float32), (128, 128)).T


def wide(mask):
    return jnp.concatenate([mask, mask], axis=1) > 0


def both(ref, z):
    return jnp.concatenate([ref[0, z], ref[1, z]], axis=0)


def inside(shape, dim, rows, cols):
    index = lax.broadcasted_iota(jnp.int32, shape, dim)
    row = (index // 8) % 8 + rows
    col = index % 8 + cols
    return (row >= 0) & (row < 8) & (col >= 0) & (col < 8)


def windows(shape, dim):
    return [inside(shape, dim, p, q) for p in (-1, 0, 1) for q in (-1, 0, 1)]


def shifts(x, dim, valid, sign=1):
    count = x.shape[dim]
    moved = []
    for place in range(9):
        at = place if sign == 1 else 8 - place
        move = 8 * (at // 3 - 1) + at % 3 - 1
        turned = pltpu.roll(x, (-move) % count, dim) if move else x
        moved.append(jnp.where(valid[at], turned, 0.0).astype(jnp.bfloat16))
    return moved


def activate(pre, cotangent, keep):
    sigma = 1.0 / (1.0 + jnp.exp(-pre))
    out = jnp.where(keep, pre * sigma, 0.0)
    grad = jnp.where(keep, cotangent * sigma * (1.0 + pre * (1.0 - sigma)), 0.0)
    return out.astype(jnp.bfloat16), grad.astype(jnp.bfloat16)


def write_exact(rows, ref):
    high = rows.astype(jnp.bfloat16)
    left = rows - high.astype(jnp.float32)
    middle = left.astype(jnp.bfloat16)
    low = (left - middle.astype(jnp.float32)).astype(jnp.bfloat16)
    zeros = jnp.zeros((EXTRA - 3, rows.shape[1]), jnp.float32)
    terms = [term.astype(jnp.float32) for term in (high, middle, low)]
    ref[256:272, :] = jnp.concatenate(terms + [zeros], axis=0).astype(jnp.bfloat16)


def read_extra(ref):
    return jnp.sum(ref[256:272, :].astype(jnp.float32), axis=0, keepdims=True)


def rims_kernel(links, feats, voxmask, parcel, planes, masks, codes, done):
    width = feats.shape[3]
    copies = [
        pltpu.make_async_copy(feats.at[:, pl.ds(0, 1)], planes.at[0], done.at[0]),
        pltpu.make_async_copy(feats.at[:, pl.ds(7, 1)], planes.at[1], done.at[1]),
        pltpu.make_async_copy(voxmask, masks, done.at[2]),
        pltpu.make_async_copy(links, codes, done.at[3]),
    ]
    for copy in copies:
        copy.start()
    for copy in copies:
        copy.wait()
    for side in range(2):
        keep = wide(mask_rows(masks, 7 * side))
        plane = jnp.concatenate([planes[side, 0, 0], planes[side, 1, 0]], axis=0).astype(jnp.float32)
        parcel[128 * side : 128 * side + 128, :] = jnp.where(keep, plane, 0.0).astype(jnp.bfloat16)
    lane = lax.broadcasted_iota(jnp.int32, (EXTRA, width), 1)
    row = jnp.zeros((EXTRA, width), jnp.float32)
    for place in range(4):
        row = jnp.where(lane == place, codes[place // 2, place % 2].astype(jnp.float32), row)
    parcel[256:272, :] = row.astype(jnp.bfloat16)


def rims(links, feats, voxmask):
    width = feats.shape[3]
    return pl.pallas_call(
        rims_kernel,
        in_specs=[FAR] * 3,
        out_specs=WHOLE,
        out_shape=pltpu.VMEM((256 + EXTRA, width), jnp.bfloat16),
        scratch_shapes=[
            pltpu.VMEM((2, 2, 1, 64, width), jnp.bfloat16),
            pltpu.VMEM(voxmask.shape, jnp.int32),
            pltpu.SMEM(links.shape, jnp.int32),
            pltpu.SemaphoreType.DMA((4,)),
        ],
        compiler_params=params(),
        cost_estimate=cost(1024, 1024),
        name="rims",
    )(far(links), far(feats), far(voxmask))


def fetch_taps(weight, near_weight, done, skip=0):
    for tap in range(near_weight.shape[0]):
        pltpu.make_async_copy(weight.at[skip + tap], near_weight.at[tap], done.at[tap]).start()


def await_taps(first, last, weight, near_weight, done):
    for tap in range(first, last):
        pltpu.make_async_copy(weight.at[tap], near_weight.at[tap], done.at[tap]).wait()


def aligned(index, rows):
    return pl.ds(pl.multiple_of(index * rows, rows), rows)


def quarters(flip, own, give_inner, give_core):
    position = me() % 4
    rows = flip.shape[0] // 4
    if own is not None:
        own[...] = flip[aligned(position, rows), :].astype(own.dtype)
    give_inner[...] = flip[aligned(1 - position // 2, 2 * rows), :].astype(jnp.bfloat16)
    give_core[...] = flip[aligned(position // 2 * 2 + 1 - position % 2, rows), :].astype(jnp.bfloat16)


def turn_rows(flip, lanes, valid, turned, first):
    rows = flip.shape[0]
    for place, moved in enumerate(shifts(flip[:, lanes].astype(jnp.float32), 1, valid)):
        turned[first + place * rows : first + (place + 1) * rows, lanes] = moved


def prepare_kernel(
    feats, voxmask, weight, mask, rows, give_inner, give_core, turned, taps, planes, masks, flip, own, done, fetched
):
    pltpu.make_async_copy(voxmask, masks, done.at[8]).start()
    for z in range(8):
        pltpu.make_async_copy(feats.at[:, pl.ds(z, 1)], planes.at[:, pl.ds(z, 1)], done.at[z]).start()
    fetch_taps(weight, taps, fetched)
    valid = windows((own.shape[0], 128), 1)
    pltpu.make_async_copy(voxmask, masks, done.at[8]).wait()
    for z in range(8):
        pltpu.make_async_copy(feats.at[:, pl.ds(z, 1)], planes.at[:, pl.ds(z, 1)], done.at[z]).wait()
        span = slice(128 * z, 128 * z + 128)
        keep = mask_rows(masks, z)
        mask[span, :] = keep
        plane = jnp.where(wide(keep), both(planes, z).astype(jnp.float32), 0.0)
        rows[span, :] = plane.astype(jnp.bfloat16)
        flip[:, span] = plane.T
    quarters(flip, own, give_inner, give_core)
    for z in range(8):
        turn_rows(own, slice(128 * z, 128 * z + 128), valid, turned, 0)
    await_taps(0, taps.shape[0], weight, taps, fetched)


def prepare(feats, voxmask, weight):
    width = feats.shape[3]
    quarter = width // 4
    return pl.pallas_call(
        prepare_kernel,
        in_specs=[FAR] * 3,
        out_specs=(WHOLE,) * 6,
        out_shape=(
            pltpu.VMEM((1024, 128), jnp.float32),
            pltpu.VMEM((1024, width), jnp.bfloat16),
            pltpu.VMEM((2 * quarter, 1024), jnp.bfloat16),
            pltpu.VMEM((quarter, 1024), jnp.bfloat16),
            pltpu.VMEM((9 * quarter, 1024), jnp.bfloat16),
            pltpu.VMEM((18, width, width), jnp.bfloat16),
        ),
        scratch_shapes=[
            pltpu.VMEM(feats.shape, jnp.bfloat16),
            pltpu.VMEM(voxmask.shape, jnp.int32),
            pltpu.VMEM((width, 1024), jnp.float32),
            pltpu.VMEM((quarter, 1024), jnp.float32),
            pltpu.SemaphoreType.DMA((9,)),
            pltpu.SemaphoreType.DMA((18,)),
        ],
        compiler_params=params(12),
        cost_estimate=cost(1024, 1024),
        name="prepare",
    )(far(feats), far(voxmask), far(weight))


def turn_kernel(inner, core, both_changed, turned):
    quarter = core.shape[0]
    valid = windows((quarter, 128), 1)
    mine = aligned(me() % 2, quarter)
    for z in range(8):
        lanes = slice(128 * z, 128 * z + 128)
        for index, rows in enumerate((inner[mine, lanes], core[:, lanes], both_changed[mine, lanes])):
            first = 9 * quarter * index
            for place, moved in enumerate(shifts(rows.astype(jnp.float32), 1, valid)):
                turned[first + place * quarter : first + (place + 1) * quarter, lanes] = moved


def turn(inner, core, both_changed):
    quarter = core.shape[0]
    return pl.pallas_call(
        turn_kernel,
        in_specs=[WHOLE] * 3,
        out_specs=WHOLE,
        out_shape=pltpu.VMEM((27 * quarter, 1024), jnp.bfloat16),
        compiler_params=params(10),
        cost_estimate=cost(1024, 1024),
        name="turn",
    )(near(inner), near(core), near(both_changed))


def copy_picks(outer, table, parcels, picks, planes):
    for dev in range(4):
        planes[256 * dev : 256 * dev + 256, :] = parcels[dev][:256, :]
    for steps in range(outer):
        for slot in range(4):
            start = pl.multiple_of(table[steps * 4 + slot] * 64, 64)
            picks[steps][64 * slot : 64 * slot + 64, :] = planes[pl.ds(start, 64), :]


def route_kernel(outer, *refs):
    position = me()
    parcels, (table, *picks), (codes, links, planes, done) = refs[:4], refs[4:-4], refs[-4:]
    for dev in range(4):
        row = parcels[dev][256:272, :128].astype(jnp.float32)
        codes[8 * dev : 8 * dev + 8, :] = row[:8, :].astype(jnp.int32)
    copy = pltpu.make_async_copy(codes, links, done)
    copy.start()
    copy.wait()
    for place in range(outer * 4):
        table[place] = 0
        table[outer * 4 + 4 + place] = -1
    for plane in range(16):
        dev, side, brick = plane // 4, plane // 2 % 2, plane % 2
        dest = links[dev * 8, brick * 2 + side]

        @pl.when((dest >= 0) & ((dest // 2) % 4 == position % 4))
        def _():
            steps = lax.rem(dest // 8 - position // 4 + outer, outer)
            slot = dest % 2 + (0 if side == 1 else 2)
            table[steps * 4 + slot] = plane
            table[outer * 4 + 4 + ((dest // 8) ^ (position // 4)) * 4 + slot] = plane

    for brick in range(2):
        for side in range(2):
            dest = links[0, brick * 2 + side]
            steps = lax.rem(position // 4 - dest // 8 + outer, outer)
            table[outer * 4 + 2 * side + brick] = jnp.where(dest >= 0, steps, -1)

    copy_picks(outer, table, parcels, picks, planes)


def route(parcels, outer):
    width = parcels[0].shape[1]
    results = pl.pallas_call(
        functools.partial(route_kernel, outer),
        in_specs=[WHOLE] * 4,
        out_specs=[SCALARS] + [WHOLE] * outer,
        out_shape=[jax.ShapeDtypeStruct((outer * 8 + 4,), jnp.int32)]
        + [pltpu.VMEM((256, width), jnp.bfloat16)] * outer,
        scratch_shapes=[
            pltpu.VMEM((32, 128), jnp.int32),
            pltpu.SMEM((32, 128), jnp.int32),
            pltpu.VMEM((1024, width), jnp.bfloat16),
            pltpu.SemaphoreType.DMA(()),
        ],
        compiler_params=params(),
        cost_estimate=cost(1024, 1024),
        name="route",
    )(*[near(x) for x in parcels])
    return results[0], results[1:]


def deal_kernel(outer, table, *refs):
    parcels, (give, keep, planes) = refs[:4], refs[4:]
    for dev in range(4):
        planes[256 * dev : 256 * dev + 256, :] = parcels[dev][:256, :]
    for flip in range(outer):
        target = (give if flip % 2 else keep).at[flip // 2]
        for slot in range(4):
            plane = table[outer * 4 + 4 + flip * 4 + slot]
            rows = planes[aligned(jnp.maximum(plane, 0), 64), :]
            target[64 * slot : 64 * slot + 64, :] = jnp.where(plane >= 0, rows.astype(jnp.float32), 0.0).astype(jnp.bfloat16)
    total = sum(read_extra(ref) for ref in parcels)
    for ref in (give, keep):
        write_exact(total, ref.at[0])
        for index in range(1, outer // 2):
            ref[index, 256:272, :] = jnp.zeros((EXTRA, planes.shape[1]), jnp.bfloat16)


def deal(table, parcels, outer):
    width = parcels[0].shape[1]
    shape = pltpu.VMEM((outer // 2, 256 + EXTRA, width), jnp.bfloat16)
    return pl.pallas_call(
        functools.partial(deal_kernel, outer),
        in_specs=[SCALARS] + [WHOLE] * 4,
        out_specs=(WHOLE, WHOLE),
        out_shape=(shape, shape),
        scratch_shapes=[pltpu.VMEM((1024, width), jnp.bfloat16)],
        compiler_params=params(8),
        cost_estimate=cost(1024, 1024),
        name="deal",
    )(table, *[near(x) for x in parcels])


def merged(keep, got, index):
    planes = keep[index, :256, :].astype(jnp.float32) + got[index, :256, :].astype(jnp.float32)
    return planes


def merge_kernel(kept, got, give, keep):
    total = read_extra(kept.at[0]) + read_extra(got.at[0])
    for index in range(kept.shape[0]):
        target = (give if index % 2 else keep).at[index // 2]
        target[:256, :] = merged(kept, got, index).astype(jnp.bfloat16)
        target[256:272, :] = jnp.zeros((EXTRA, kept.shape[2]), jnp.bfloat16)
    for ref in (give, keep):
        write_exact(total, ref.at[0])


def merge(kept, got):
    shape = pltpu.VMEM((kept.shape[0] // 2, *kept.shape[1:]), jnp.bfloat16)
    return pl.pallas_call(
        merge_kernel,
        in_specs=[WHOLE, WHOLE],
        out_specs=(WHOLE, WHOLE),
        out_shape=(shape, shape),
        compiler_params=params(8),
        cost_estimate=cost(1024, 1024),
        name="merge",
    )(near(kept), near(got))


def chosen(table, slot, arrived):
    rows = slice(64 * slot, 64 * slot + 64)
    plane = jnp.zeros((64, arrived[0].shape[1]), jnp.float32)
    for steps, ref in enumerate(arrived):
        plane = jnp.where(table[4 * len(arrived) + slot] == steps, ref[rows, :].astype(jnp.float32), plane)
    return plane


def forward_kernel(rows, mask, first, weight, bias, cotangent, out, grad, edge, bias_sum, rest, slopes, cols, pre, done):
    width = rows.shape[1]
    fetch_taps(weight, rest, done, 18)
    copies = [
        pltpu.make_async_copy(cotangent.at[:, pl.ds(z, 1)], slopes.at[:, pl.ds(z, 1)], done.at[9 + z]) for z in range(8)
    ]
    for copy in copies:
        copy.start()
    valid = windows((128, width), 0)
    for z in range(8):
        span = slice(128 * z, 128 * z + 128)
        for place, moved in enumerate(shifts(rows[span, :].astype(jnp.float32), 0, valid)):
            cols[span, place * width : (place + 1) * width] = moved

    def taps(ref, start):
        return ref[start : start + 9].reshape(9 * width, width)

    pre[...] = jnp.dot(cols[...], taps(first, 9), preferred_element_type=jnp.float32) + bias[...]
    pre[128:, :] += jnp.dot(cols[:896, :], taps(first, 0), preferred_element_type=jnp.float32)
    for tap in range(9):
        pltpu.make_async_copy(weight.at[18 + tap], rest.at[tap], done.at[tap]).wait()
    pre[:896, :] += jnp.dot(cols[128:, :], taps(rest, 0), preferred_element_type=jnp.float32)
    for copy in copies:
        copy.wait()
    for side in range(2):
        edge[side] = pre[896 * side : 896 * side + 128, :]
    total = jnp.zeros((1, width), jnp.float32)
    for z in range(1, 7):
        span = slice(128 * z, 128 * z + 128)
        act, slope = activate(pre[span, :], both(slopes, z).astype(jnp.float32), wide(mask[span, :]))
        for b in range(2):
            out[b, z] = act[64 * b : 64 * b + 64]
        grad[128 * (z - 1) : 128 * z, :] = slope
        total += jnp.sum(slope.astype(jnp.float32), axis=0, keepdims=True)
    bias_sum[...] = total


def forward_inside(rows, mask, first, weight, bias, cotangent):
    width = rows.shape[1]
    return pl.pallas_call(
        forward_kernel,
        in_specs=[WHOLE] * 3 + [FAR, WHOLE, FAR],
        out_specs=(WHOLE,) * 6,
        out_shape=(
            jax.ShapeDtypeStruct(cotangent.shape, jnp.bfloat16),
            pltpu.VMEM((768, width), jnp.bfloat16),
            pltpu.VMEM((2, 128, width), jnp.float32),
            pltpu.VMEM((1, width), jnp.float32),
            pltpu.VMEM((9, width, width), jnp.bfloat16),
            pltpu.VMEM(cotangent.shape, jnp.bfloat16),
        ),
        scratch_shapes=[
            pltpu.VMEM((1024, 9 * width), jnp.bfloat16),
            pltpu.VMEM((1024, width), jnp.float32),
            pltpu.SemaphoreType.DMA((17,)),
        ],
        compiler_params=params(12),
        cost_estimate=cost(1024, 1024),
        name="forward_inside",
    )(near(rows), near(mask), near(first), far(weight), bias, far(cotangent))


def inner_terms_kernel(mine, others, *refs):
    grads, terms = refs[:4], refs[4]
    rows = mine.shape[0]
    for a in range(3):
        lanes = slice(128 * a, 128 * a + 768)
        total = jnp.dot(mine[:, lanes], grads[0][...], preferred_element_type=jnp.float32)
        for index in range(3):
            total += jnp.dot(
                others[index * rows : (index + 1) * rows, lanes], grads[index + 1][...], preferred_element_type=jnp.float32
            )
        terms[a * rows : (a + 1) * rows, :] = total


def inner_terms(mine, others, grads):
    rows, width = mine.shape[0], grads[0].shape[1]
    return pl.pallas_call(
        inner_terms_kernel,
        in_specs=[WHOLE] * 6,
        out_specs=WHOLE,
        out_shape=pltpu.VMEM((3 * rows, width), jnp.float32),
        compiler_params=params(10),
        cost_estimate=cost(1024, 1024),
        name="inner_terms",
    )(near(mine), near(others), *[near(x) for x in grads])


def edge_kernel(table, mask, first, rest, edge, ends, inner, out_in, *refs):
    arrived, (out, to_inner, to_core, own, planes, flip, done) = refs[:-7], refs[-7:]
    width = edge.shape[2]
    valid = windows((128, width), 0)
    total = inner[...]
    for side in range(2):
        rows = slice(128 * side, 128 * side + 128)
        halo = jnp.concatenate([chosen(table, 2 * side + b, arrived) for b in range(2)], axis=0)
        flip[:, rows] = halo.T
        cols = jnp.concatenate(shifts(halo, 0, valid), axis=1)
        taps = (rest if side else first)[0:9].reshape(9 * width, width)
        pre = edge[side] + jnp.dot(cols, taps, preferred_element_type=jnp.float32)
        z = 7 * side
        keep = wide(mask[128 * z : 128 * z + 128, :])
        act, slope = activate(pre, both(ends, z).astype(jnp.float32), keep)
        for b in range(2):
            planes[side, b, 0] = act[64 * b : 64 * b + 64]
        pltpu.make_async_copy(planes.at[side], out.at[:, pl.ds(z, 1)], done.at[side]).start()
        to_inner[rows, :] = slope
        to_core[rows, :] = slope
        total += jnp.sum(slope.astype(jnp.float32), axis=0, keepdims=True)
    write_exact(total, to_inner)
    write_exact(total, to_core)
    quarters(flip, own, to_inner.at[272:], to_core.at[272:])
    for side in range(2):
        pltpu.make_async_copy(planes.at[side], out.at[:, pl.ds(7 * side, 1)], done.at[side]).wait()


def forward_edges(table, mask, first, rest, edge, ends, inner, out, arrived):
    width = edge.shape[2]
    quarter = width // 4
    return pl.pallas_call(
        edge_kernel,
        in_specs=[SCALARS] + [WHOLE] * 6 + [FAR] + [WHOLE] * len(arrived),
        out_specs=(FAR, WHOLE, WHOLE, WHOLE),
        out_shape=(
            jax.ShapeDtypeStruct(out.shape, out.dtype),
            pltpu.VMEM((256 + EXTRA + 2 * quarter, width), jnp.bfloat16),
            pltpu.VMEM((256 + EXTRA + quarter, width), jnp.bfloat16),
            pltpu.VMEM((quarter, 256), jnp.bfloat16),
        ),
        scratch_shapes=[
            pltpu.VMEM((2, 2, 1, 64, width), jnp.bfloat16),
            pltpu.VMEM((width, 256), jnp.float32),
            pltpu.SemaphoreType.DMA((2,)),
        ],
        input_output_aliases={7: 0},
        compiler_params=params(10),
        cost_estimate=cost(1024, 1024),
        name="forward_edges",
    )(
        table,
        near(mask),
        near(first),
        near(rest),
        near(edge),
        near(ends),
        near(inner),
        out,
        *[near(x) for x in arrived],
    )


def outer_terms_kernel(outer, mine, others, halos, *refs):
    parcels, inner = refs[:4], refs[4]
    gives, stay, cols, total = refs[5 : 4 + outer], refs[4 + outer], refs[5 + outer], refs[6 + outer]
    quarter = halos.shape[0]
    rows = 9 * quarter
    valid = windows((quarter, 128), 1)
    half = aligned(me() % 2, quarter)
    ends = (
        halos,
        parcels[1].at[272 : 272 + 2 * quarter].at[half],
        parcels[2].at[272 : 272 + quarter],
        parcels[3].at[272 : 272 + 2 * quarter].at[half],
    )
    facing = jnp.concatenate(
        [parcel[128 * side : 128 * side + 128, :] for side in range(2) for parcel in parcels], axis=0
    )
    for a in range(3):
        for side in range(2):
            plane = a - 1 + 7 * side
            for who in range(4):
                lanes = slice(128 * (4 * side + who), 128 * (4 * side + who) + 128)
                if 0 <= plane < 8:
                    ref, first = (mine, 0) if who == 0 else (others, rows * (who - 1))
                    cols[:, lanes] = ref[first : first + rows, 128 * plane : 128 * plane + 128]
                else:
                    moved = shifts(ends[who][:, 128 * side : 128 * side + 128].astype(jnp.float32), 1, valid)
                    for place in range(9):
                        cols[place * quarter : (place + 1) * quarter, lanes] = moved[place]
        span = slice(a * rows, (a + 1) * rows)
        total[span, :] = inner[span, :] + jnp.dot(cols[...], facing, preferred_element_type=jnp.float32)
    if total.shape[0] > 3 * rows:
        total[3 * rows :, :] = jnp.zeros((total.shape[0] - 3 * rows, total.shape[1]), jnp.float32)
    z = me() // 4
    for steps in range(outer):
        block = lax.rem(z + steps, outer)
        for unit in range(units(outer)):
            piece = total[aligned(block + outer * unit, 16), :]
            if steps:
                gives[steps - 1][16 * unit : 16 * unit + 16, :] = piece.astype(jnp.bfloat16)
            else:
                stay[16 * unit : 16 * unit + 16, :] = piece


def outer_terms(outer, mine, others, halos, parcels, inner):
    width = inner.shape[1]
    rows = 16 * units(outer)
    results = pl.pallas_call(
        functools.partial(outer_terms_kernel, outer),
        in_specs=[WHOLE] * 8,
        out_specs=[WHOLE] * outer,
        out_shape=[pltpu.VMEM((rows, width), jnp.bfloat16)] * (outer - 1) + [pltpu.VMEM((rows, width), jnp.float32)],
        scratch_shapes=[
            pltpu.VMEM((inner.shape[0] // 3, 1024), jnp.bfloat16),
            pltpu.VMEM((outer * rows, width), jnp.float32),
        ],
        compiler_params=params(12),
        cost_estimate=cost(1024, 1024),
        name="outer_terms",
    )(*[near(x) for x in (mine, others, halos, *parcels, inner)])
    return results[:-1], results[-1]


def backward_kernel(grad, parcel, mask, weight, grad_feats, partial, near_weight, cols, total, fetched):
    width = grad.shape[1]
    fetch_taps(weight, near_weight, fetched)
    valid = windows((128, width), 0)
    planes = [parcel[:128, :]] + [grad[128 * z : 128 * z + 128, :] for z in range(6)] + [parcel[128:256, :]]
    for z, plane in enumerate(planes):
        for at, moved in enumerate(shifts(plane.astype(jnp.float32), 0, valid, -1)):
            cols[128 * z : 128 * z + 128, at * width : (at + 1) * width] = moved
    for a in (1, 0, 2):
        await_taps(9 * a, 9 * a + 9, weight, near_weight, fetched)
        first, start, count = ((128, 0, 896), (0, 0, 1024), (0, 128, 896))[a]
        for at in range(9):
            piece = lax.dot_general(
                cols[first : first + count, at * width : (at + 1) * width],
                near_weight[9 * a + at],
                (((1,), (1,)), ((), ())),
                preferred_element_type=jnp.float32,
            )
            if a == 1 and at == 0:
                total[...] = piece
            else:
                total[start : start + count, :] += piece
    for z in range(1, 7):
        rows = slice(128 * z, 128 * z + 128)
        done = jnp.where(wide(mask[rows, :]), total[rows, :], 0.0).astype(jnp.bfloat16)
        for b in range(2):
            grad_feats[b, z] = done[64 * b : 64 * b + 64]
    for side in range(2):
        partial[side] = total[896 * side : 896 * side + 128, :]


def backward(grad, parcel, mask, weight):
    width = grad.shape[1]
    return pl.pallas_call(
        backward_kernel,
        in_specs=[WHOLE] * 3 + [FAR],
        out_specs=(WHOLE,) * 3,
        out_shape=(
            jax.ShapeDtypeStruct((2, 8, 64, width), jnp.bfloat16),
            pltpu.VMEM((2, 128, width), jnp.float32),
            pltpu.VMEM(weight.shape, jnp.bfloat16),
        ),
        scratch_shapes=[
            pltpu.VMEM((1024, 9 * width), jnp.bfloat16),
            pltpu.VMEM((1024, width), jnp.float32),
            pltpu.SemaphoreType.DMA((weight.shape[0],)),
        ],
        compiler_params=params(16),
        cost_estimate=cost(1024, 1024),
        name="backward",
    )(near(grad), near(parcel), near(mask), far(weight))


def block_copies(outer, places, stacks, out, done):
    position = me()
    blocks = [ref.at[index] for ref in stacks for index in range(ref.shape[0])]
    copies = []
    for index, (ref, (flip, inner, core)) in enumerate(zip(blocks, places)):
        block = (position // 4) ^ flip
        quarter = 4 * ((position % 4) ^ (2 * inner + core))
        if outer == 4:
            copies.append((None, pltpu.make_async_copy(ref, out.at[:, quarter + block], done.at[index, 0])))
            continue
        for unit in range(units(outer)):
            place = block + outer * unit
            here = jnp.minimum(place, 107)
            target = out.at[here // 4, quarter + here % 4]
            copies.append((place < 108, pltpu.make_async_copy(ref.at[unit], target, done.at[index, unit])))
    return copies


def for_each(copies, wait):
    for condition, copy in copies:
        act = copy.wait if wait else copy.start
        if condition is None:
            act()
        else:
            pl.when(condition)(act)


def assemble_kernel(outer, places, count, *refs):
    out, done = refs[-2:]
    copies = block_copies(outer, places, refs[:count], out, done)
    for_each(copies, False)
    for_each(copies, True)


def in_units(stack, outer):
    return near(stack.reshape(stack.shape[0], units(outer), 16, stack.shape[-1]))


def assemble(outer, places, stacks, shape, given):
    before = [] if given is None else [given]
    return pl.pallas_call(
        functools.partial(assemble_kernel, outer, places, len(stacks)),
        in_specs=[WHOLE] * len(stacks) + [FAR] * len(before),
        out_specs=FAR,
        out_shape=jax.ShapeDtypeStruct(shape, jnp.bfloat16),
        scratch_shapes=[pltpu.SemaphoreType.DMA((len(places), units(outer)))],
        input_output_aliases={len(stacks): 0} if before else {},
        compiler_params=params(),
        cost_estimate=cost(1024, 1024),
        name="assemble",
    )(*[in_units(x, outer) for x in stacks], *before)


def finish_kernel(outer, places, partial, mask, weight, kept, got, stack, feats_in, weight_in, *refs):
    grad_feats, grad_weight, bias_sum, planes, sent, done = refs
    copies = block_copies(outer, places, [stack], grad_weight, done)
    for_each(copies, False)
    width = weight.shape[1]
    valid = windows((128, width), 0)
    halos = merged(kept, got, 0)
    for side in range(2):
        total = partial[side]
        for at, moved in enumerate(shifts(halos[128 * side : 128 * side + 128, :], 0, valid, -1)):
            total += lax.dot_general(
                moved,
                weight[18 * (1 - side) + at],
                (((1,), (1,)), ((), ())),
                preferred_element_type=jnp.float32,
            )
        rows = slice(896 * side, 896 * side + 128)
        done_rows = jnp.where(wide(mask[rows, :]), total, 0.0).astype(jnp.bfloat16)
        for b in range(2):
            planes[side, b, 0] = done_rows[64 * b : 64 * b + 64]
        pltpu.make_async_copy(planes.at[side], grad_feats.at[:, pl.ds(7 * side, 1)], sent.at[side]).start()
    bias_sum[...] = read_extra(kept.at[0]) + read_extra(got.at[0])
    for side in range(2):
        pltpu.make_async_copy(planes.at[side], grad_feats.at[:, pl.ds(7 * side, 1)], sent.at[side]).wait()
    for_each(copies, True)


def finish(outer, places, partial, mask, weight, kept, got, stack, grad_feats, grad_weight):
    width = weight.shape[1]
    return pl.pallas_call(
        functools.partial(finish_kernel, outer, places),
        in_specs=[WHOLE] * 6 + [FAR, FAR],
        out_specs=(FAR, FAR, WHOLE),
        out_shape=(
            jax.ShapeDtypeStruct(grad_feats.shape, grad_feats.dtype),
            jax.ShapeDtypeStruct(grad_weight.shape, grad_weight.dtype),
            jax.ShapeDtypeStruct((1, width), jnp.float32),
        ),
        scratch_shapes=[
            pltpu.VMEM((2, 2, 1, 64, width), jnp.bfloat16),
            pltpu.SemaphoreType.DMA((2,)),
            pltpu.SemaphoreType.DMA((len(places), units(outer))),
        ],
        input_output_aliases={6: 0, 7: 1},
        compiler_params=params(10),
        cost_estimate=cost(1024, 1024),
        name="finish",
    )(*[near(x) for x in (partial, mask, weight, kept, got)], in_units(stack, outer), grad_feats, grad_weight)


def per_device(size, feats, voxmask, links, weight, bias, cotangent):
    width = feats.shape[3]
    outer = size // 4

    parcel = rims(links, feats, voxmask)
    mask, rows, give_inner, give_core, turned, first = prepare(feats, voxmask, weight)
    inner, rows = lax.optimization_barrier((swap(parcel, size, 2), rows))
    parcels = [parcel, inner, swap(parcel, size, 1), swap(inner, size, 1)]
    out, grad, edge, bias_local, rest, ends = forward_inside(
        rows, mask, first, weight, bias.reshape(1, width), cotangent
    )
    *parcels, grad = lax.optimization_barrier((*parcels, grad))
    table, picks = route(parcels, outer)

    *picks, give_core, grad = lax.optimization_barrier((*picks, give_core, grad))
    arrived = [rotate(pick, size, steps) if steps else pick for steps, pick in enumerate(picks)]
    got_inner = swap(give_inner, size, 2)
    got_inner, grad = lax.optimization_barrier((got_inner, grad))
    grad_inner = swap(grad, size, 2)
    *arrived, got_inner, grad_inner = lax.optimization_barrier((*arrived, got_inner, grad_inner))
    others = turn(got_inner, swap(give_core, size, 1), swap(got_inner, size, 1))
    grads = [grad, grad_inner, swap(grad, size, 1), swap(grad_inner, size, 1)]

    out, to_inner, to_core, halos = forward_edges(
        table, mask, first, rest, edge, ends, bias_local, out, arrived
    )
    inner = swap(to_inner, size, 2)
    terms = inner_terms(turned, others, grads)
    inner, terms = lax.optimization_barrier((inner, terms))
    parcels = [to_inner, inner, swap(to_core, size, 1), swap(inner, size, 1)]

    gives, stay = outer_terms(outer, turned, others, halos, parcels, terms)
    give, kept = deal(table, parcels, outer)
    give, *gives = lax.optimization_barrier((give, *gives))
    gots = [rotate(x, size, steps) for steps, x in enumerate(gives, 1)]
    got = swap(give, size, 4)
    grad_feats, partial, taps = backward(grad, to_inner, mask, weight)
    bits = outer.bit_length() - 1
    for bit in range(1, bits):
        give, kept = merge(kept, got)
        if bit < bits - 1:
            got = swap(give, size, 4 << bit)
    stay, partial, give, kept = lax.optimization_barrier((stay, partial, give, kept))
    part = (stay + sum(got.astype(jnp.float32) for got in gots)).astype(jnp.bfloat16)

    def stack(*blocks):
        return jnp.concatenate([x.reshape(-1, *part.shape) for x in blocks])

    def place_blocks(keys, blocks, given):
        places = [(*key, core) for core in range(2) for key in keys]
        return assemble(outer, places, [blocks, swap(blocks, size, 1)], (27, 16, width // 16, width), given)

    last = outer - 1
    flips = list(range(1, last))
    blocks = [part]
    for flip in flips:
        blocks.append(swap(blocks[flip & (flip - 1)], size, 4 * (flip & -flip)))
    first_inner = swap(part, size, 2)
    middle = stack(*blocks[1:])
    farthest = swap(blocks[last & (last - 1)], size, 4)
    middle, give = lax.optimization_barrier((middle, give))
    middle_inner = swap(middle, size, 2)
    got = swap(give, size, 4 << (bits - 1))
    grad_weight = place_blocks([(0, 0), (0, 1)] + [(flip, 0) for flip in flips], stack(part, first_inner, middle), None)
    farthest_inner = swap(farthest, size, 2)
    middle_inner, farthest_inner, grad_weight, got = lax.optimization_barrier(
        (middle_inner, farthest_inner, grad_weight, got)
    )
    keys = [(flip, 1) for flip in flips] + [(last, 0), (last, 1)]
    rest = stack(middle_inner, farthest, farthest_inner)
    theirs = swap(rest, size, 1)
    grad_feats, grad_weight, grad_bias = finish(
        outer, [(*key, 0) for key in keys], partial, mask, taps, kept, got, rest, grad_feats, grad_weight
    )
    grad_weight = assemble(outer, [(*key, 1) for key in keys], [theirs], grad_weight.shape, grad_weight)
    return out, grad_feats, grad_weight.reshape(weight.shape), grad_bias.reshape(width)


def solution(mesh):
    return jax.shard_map(
        functools.partial(per_device, mesh.shape["zslab"]),
        mesh=mesh,
        in_specs=(
            P(("groups", "zslab"), None, None, None),
            P(("groups", "zslab"), None),
            P(("groups", "zslab"), None),
            P(),
            P(),
            P(("groups", "zslab"), None, None, None),
        ),
        out_specs=(
            P(("groups", "zslab"), None, None, None),
            P(("groups", "zslab"), None, None, None),
            P("groups", None, None),
            P("groups"),
        ),
        check_vma=False,
    )
```

```python
import functools

import jax
import jax.numpy as jnp
from jax import lax
from jax.experimental import pallas as pl
from jax.experimental.pallas import tpu as pltpu
from jax.sharding import PartitionSpec as P

EXTRA = 16


def params(mebibytes=6):
    return pltpu.CompilerParams(vmem_limit_bytes=mebibytes * 1024 * 1024)


def cost(flops, bytes_accessed):
    return pl.CostEstimate(flops=flops, bytes_accessed=bytes_accessed, transcendentals=0)


def near(x):
    return pltpu.with_memory_space_constraint(x, pltpu.VMEM)


def far(x):
    return pltpu.with_memory_space_constraint(x, pltpu.HBM)


SCALARS = pl.BlockSpec(memory_space=pltpu.SMEM)
WHOLE = pl.BlockSpec(memory_space=pltpu.VMEM)
FAR = pl.BlockSpec(memory_space=pl.ANY)


def swap(x, size, bit):
    return lax.ppermute(x, "zslab", [(i, i ^ bit) for i in range(size)])


def rotate(x, size, steps):
    return lax.ppermute(x, "zslab", [(i, (i + 4 * steps) % size) for i in range(size)])


def me():
    return lax.axis_index("zslab")


def units(outer):
    return -(-108 // outer)


def mask_rows(voxmask, z):
    lanes = slice(64 * z, 64 * z + 64)
    line = jnp.concatenate([voxmask[0:1, lanes], voxmask[1:2, lanes]], axis=1)
    return jnp.broadcast_to((line == 1).astype(jnp.float32), (128, 128)).T


def wide(mask):
    return jnp.concatenate([mask, mask], axis=1) > 0


def both(ref, z):
    return jnp.concatenate([ref[0, z], ref[1, z]], axis=0)


def inside(shape, dim, rows, cols):
    index = lax.broadcasted_iota(jnp.int32, shape, dim)
    row = (index // 8) % 8 + rows
    col = index % 8 + cols
    return (row >= 0) & (row < 8) & (col >= 0) & (col < 8)


def windows(shape, dim):
    return [inside(shape, dim, p, q) for p in (-1, 0, 1) for q in (-1, 0, 1)]


def shifts(x, dim, valid, sign=1):
    count = x.shape[dim]
    moved = []
    for place in range(9):
        at = place if sign == 1 else 8 - place
        move = 8 * (at // 3 - 1) + at % 3 - 1
        turned = pltpu.roll(x, (-move) % count, dim) if move else x
        moved.append(jnp.where(valid[at], turned, 0.0).astype(jnp.bfloat16))
    return moved


def activate(pre, cotangent, keep):
    sigma = 1.0 / (1.0 + jnp.exp(-pre))
    out = jnp.where(keep, pre * sigma, 0.0)
    grad = jnp.where(keep, cotangent * sigma * (1.0 + pre * (1.0 - sigma)), 0.0)
    return out.astype(jnp.bfloat16), grad.astype(jnp.bfloat16)


def write_exact(rows, ref):
    high = rows.astype(jnp.bfloat16)
    left = rows - high.astype(jnp.float32)
    middle = left.astype(jnp.bfloat16)
    low = (left - middle.astype(jnp.float32)).astype(jnp.bfloat16)
    zeros = jnp.zeros((EXTRA - 3, rows.shape[1]), jnp.float32)
    terms = [term.astype(jnp.float32) for term in (high, middle, low)]
    ref[256:272, :] = jnp.concatenate(terms + [zeros], axis=0).astype(jnp.bfloat16)


def read_extra(ref):
    return jnp.sum(ref[256:272, :].astype(jnp.float32), axis=0, keepdims=True)


def rims_kernel(links, feats, voxmask, parcel, planes, masks, codes, done):
    width = feats.shape[3]
    copies = [
        pltpu.make_async_copy(feats.at[:, pl.ds(0, 1)], planes.at[0], done.at[0]),
        pltpu.make_async_copy(feats.at[:, pl.ds(7, 1)], planes.at[1], done.at[1]),
        pltpu.make_async_copy(voxmask, masks, done.at[2]),
        pltpu.make_async_copy(links, codes, done.at[3]),
    ]
    for copy in copies:
        copy.start()
    for copy in copies:
        copy.wait()
    for side in range(2):
        keep = wide(mask_rows(masks, 7 * side))
        plane = jnp.concatenate([planes[side, 0, 0], planes[side, 1, 0]], axis=0).astype(jnp.float32)
        parcel[128 * side : 128 * side + 128, :] = jnp.where(keep, plane, 0.0).astype(jnp.bfloat16)
    lane = lax.broadcasted_iota(jnp.int32, (EXTRA, width), 1)
    row = jnp.zeros((EXTRA, width), jnp.float32)
    for place in range(4):
        row = jnp.where(lane == place, codes[place // 2, place % 2].astype(jnp.float32), row)
    parcel[256:272, :] = row.astype(jnp.bfloat16)


def rims(links, feats, voxmask):
    width = feats.shape[3]
    return pl.pallas_call(
        rims_kernel,
        in_specs=[FAR] * 3,
        out_specs=WHOLE,
        out_shape=pltpu.VMEM((256 + EXTRA, width), jnp.bfloat16),
        scratch_shapes=[
            pltpu.VMEM((2, 2, 1, 64, width), jnp.bfloat16),
            pltpu.VMEM(voxmask.shape, jnp.int32),
            pltpu.SMEM(links.shape, jnp.int32),
            pltpu.SemaphoreType.DMA((4,)),
        ],
        compiler_params=params(),
        cost_estimate=cost(1024, 1024),
        name="rims",
    )(far(links), far(feats), far(voxmask))


def fetch_taps(weight, near_weight, done):
    for tap in range(weight.shape[0]):
        pltpu.make_async_copy(weight.at[tap], near_weight.at[tap], done.at[tap]).start()


def await_taps(first, last, weight, near_weight, done):
    for tap in range(first, last):
        pltpu.make_async_copy(weight.at[tap], near_weight.at[tap], done.at[tap]).wait()


def aligned(index, rows):
    return pl.ds(pl.multiple_of(index * rows, rows), rows)


def quarters(flip, own, give_inner, give_core):
    position = me() % 4
    rows = flip.shape[0] // 4
    if own is not None:
        own[...] = flip[aligned(position, rows), :].astype(own.dtype)
    give_inner[...] = flip[aligned(1 - position // 2, 2 * rows), :].astype(jnp.bfloat16)
    give_core[...] = flip[aligned(position // 2 * 2 + 1 - position % 2, rows), :].astype(jnp.bfloat16)


def turn_rows(flip, lanes, valid, turned, first):
    rows = flip.shape[0]
    for place, moved in enumerate(shifts(flip[:, lanes].astype(jnp.float32), 1, valid)):
        turned[first + place * rows : first + (place + 1) * rows, lanes] = moved


def prepare_kernel(
    feats, voxmask, weight, cotangent, mask, rows, give_inner, give_core, turned, taps, slopes, planes, masks, flip, own, done, fetched
):
    count = weight.shape[0]
    pltpu.make_async_copy(voxmask, masks, done.at[8]).start()
    for z in range(8):
        pltpu.make_async_copy(feats.at[:, pl.ds(z, 1)], planes.at[:, pl.ds(z, 1)], done.at[z]).start()
    fetch_taps(weight, taps, fetched)
    for z in range(8):
        pltpu.make_async_copy(cotangent.at[:, pl.ds(z, 1)], slopes.at[:, pl.ds(z, 1)], fetched.at[count + z]).start()
    valid = windows((own.shape[0], 128), 1)
    pltpu.make_async_copy(voxmask, masks, done.at[8]).wait()
    for z in range(8):
        pltpu.make_async_copy(feats.at[:, pl.ds(z, 1)], planes.at[:, pl.ds(z, 1)], done.at[z]).wait()
        span = slice(128 * z, 128 * z + 128)
        keep = mask_rows(masks, z)
        mask[span, :] = keep
        plane = jnp.where(wide(keep), both(planes, z).astype(jnp.float32), 0.0)
        rows[span, :] = plane.astype(jnp.bfloat16)
        flip[:, span] = plane.T
    quarters(flip, own, give_inner, give_core)
    for z in range(8):
        turn_rows(own, slice(128 * z, 128 * z + 128), valid, turned, 0)
    await_taps(0, count, weight, taps, fetched)
    for z in range(8):
        pltpu.make_async_copy(cotangent.at[:, pl.ds(z, 1)], slopes.at[:, pl.ds(z, 1)], fetched.at[count + z]).wait()


def prepare(feats, voxmask, weight, cotangent):
    width = feats.shape[3]
    quarter = width // 4
    return pl.pallas_call(
        prepare_kernel,
        in_specs=[FAR] * 4,
        out_specs=(WHOLE,) * 7,
        out_shape=(
            pltpu.VMEM((1024, 128), jnp.float32),
            pltpu.VMEM((1024, width), jnp.bfloat16),
            pltpu.VMEM((2 * quarter, 1024), jnp.bfloat16),
            pltpu.VMEM((quarter, 1024), jnp.bfloat16),
            pltpu.VMEM((9 * quarter, 1024), jnp.bfloat16),
            pltpu.VMEM(weight.shape, jnp.bfloat16),
            pltpu.VMEM(cotangent.shape, jnp.bfloat16),
        ),
        scratch_shapes=[
            pltpu.VMEM(feats.shape, jnp.bfloat16),
            pltpu.VMEM(voxmask.shape, jnp.int32),
            pltpu.VMEM((width, 1024), jnp.float32),
            pltpu.VMEM((quarter, 1024), jnp.float32),
            pltpu.SemaphoreType.DMA((9,)),
            pltpu.SemaphoreType.DMA((weight.shape[0] + 8,)),
        ],
        compiler_params=params(12),
        cost_estimate=cost(1024, 1024),
        name="prepare",
    )(far(feats), far(voxmask), far(weight), far(cotangent))


def turn_kernel(inner, core, both_changed, turned):
    quarter = core.shape[0]
    valid = windows((quarter, 128), 1)
    mine = aligned(me() % 2, quarter)
    for z in range(8):
        lanes = slice(128 * z, 128 * z + 128)
        for index, rows in enumerate((inner[mine, lanes], core[:, lanes], both_changed[mine, lanes])):
            first = 9 * quarter * index
            for place, moved in enumerate(shifts(rows.astype(jnp.float32), 1, valid)):
                turned[first + place * quarter : first + (place + 1) * quarter, lanes] = moved


def turn(inner, core, both_changed):
    quarter = core.shape[0]
    return pl.pallas_call(
        turn_kernel,
        in_specs=[WHOLE] * 3,
        out_specs=WHOLE,
        out_shape=pltpu.VMEM((27 * quarter, 1024), jnp.bfloat16),
        compiler_params=params(10),
        cost_estimate=cost(1024, 1024),
        name="turn",
    )(near(inner), near(core), near(both_changed))


def copy_picks(outer, table, parcels, picks, planes):
    for dev in range(4):
        planes[256 * dev : 256 * dev + 256, :] = parcels[dev][:256, :]
    for steps in range(outer):
        for slot in range(4):
            start = pl.multiple_of(table[steps * 4 + slot] * 64, 64)
            picks[steps][64 * slot : 64 * slot + 64, :] = planes[pl.ds(start, 64), :]


def route_kernel(outer, *refs):
    position = me()
    parcels, (table, *picks), (codes, links, planes, done) = refs[:4], refs[4:-4], refs[-4:]
    for dev in range(4):
        row = parcels[dev][256:272, :128].astype(jnp.float32)
        codes[8 * dev : 8 * dev + 8, :] = row[:8, :].astype(jnp.int32)
    copy = pltpu.make_async_copy(codes, links, done)
    copy.start()
    copy.wait()
    for place in range(outer * 4):
        table[place] = 0
        table[outer * 4 + 4 + place] = -1
    for plane in range(16):
        dev, side, brick = plane // 4, plane // 2 % 2, plane % 2
        dest = links[dev * 8, brick * 2 + side]

        @pl.when((dest >= 0) & ((dest // 2) % 4 == position % 4))
        def _():
            steps = lax.rem(dest // 8 - position // 4 + outer, outer)
            slot = dest % 2 + (0 if side == 1 else 2)
            table[steps * 4 + slot] = plane
            table[outer * 4 + 4 + ((dest // 8) ^ (position // 4)) * 4 + slot] = plane

    for brick in range(2):
        for side in range(2):
            dest = links[0, brick * 2 + side]
            steps = lax.rem(position // 4 - dest // 8 + outer, outer)
            table[outer * 4 + 2 * side + brick] = jnp.where(dest >= 0, steps, -1)

    copy_picks(outer, table, parcels, picks, planes)


def route(parcels, outer):
    width = parcels[0].shape[1]
    results = pl.pallas_call(
        functools.partial(route_kernel, outer),
        in_specs=[WHOLE] * 4,
        out_specs=[SCALARS] + [WHOLE] * outer,
        out_shape=[jax.ShapeDtypeStruct((outer * 8 + 4,), jnp.int32)]
        + [pltpu.VMEM((256, width), jnp.bfloat16)] * outer,
        scratch_shapes=[
            pltpu.VMEM((32, 128), jnp.int32),
            pltpu.SMEM((32, 128), jnp.int32),
            pltpu.VMEM((1024, width), jnp.bfloat16),
            pltpu.SemaphoreType.DMA(()),
        ],
        compiler_params=params(),
        cost_estimate=cost(1024, 1024),
        name="route",
    )(*[near(x) for x in parcels])
    return results[0], results[1:]


def deal_kernel(outer, table, *refs):
    parcels, (give, keep, planes) = refs[:4], refs[4:]
    for dev in range(4):
        planes[256 * dev : 256 * dev + 256, :] = parcels[dev][:256, :]
    for flip in range(outer):
        target = (give if flip % 2 else keep).at[flip // 2]
        for slot in range(4):
            plane = table[outer * 4 + 4 + flip * 4 + slot]
            rows = planes[aligned(jnp.maximum(plane, 0), 64), :]
            target[64 * slot : 64 * slot + 64, :] = jnp.where(plane >= 0, rows.astype(jnp.float32), 0.0).astype(jnp.bfloat16)
    total = sum(read_extra(ref) for ref in parcels)
    for ref in (give, keep):
        write_exact(total, ref.at[0])
        for index in range(1, outer // 2):
            ref[index, 256:272, :] = jnp.zeros((EXTRA, planes.shape[1]), jnp.bfloat16)


def deal(table, parcels, outer):
    width = parcels[0].shape[1]
    shape = pltpu.VMEM((outer // 2, 256 + EXTRA, width), jnp.bfloat16)
    return pl.pallas_call(
        functools.partial(deal_kernel, outer),
        in_specs=[SCALARS] + [WHOLE] * 4,
        out_specs=(WHOLE, WHOLE),
        out_shape=(shape, shape),
        scratch_shapes=[pltpu.VMEM((1024, width), jnp.bfloat16)],
        compiler_params=params(8),
        cost_estimate=cost(1024, 1024),
        name="deal",
    )(table, *[near(x) for x in parcels])


def merged(keep, got, index):
    planes = keep[index, :256, :].astype(jnp.float32) + got[index, :256, :].astype(jnp.float32)
    return planes


def merge_kernel(kept, got, give, keep):
    total = read_extra(kept.at[0]) + read_extra(got.at[0])
    for index in range(kept.shape[0]):
        target = (give if index % 2 else keep).at[index // 2]
        target[:256, :] = merged(kept, got, index).astype(jnp.bfloat16)
        target[256:272, :] = jnp.zeros((EXTRA, kept.shape[2]), jnp.bfloat16)
    for ref in (give, keep):
        write_exact(total, ref.at[0])


def merge(kept, got):
    shape = pltpu.VMEM((kept.shape[0] // 2, *kept.shape[1:]), jnp.bfloat16)
    return pl.pallas_call(
        merge_kernel,
        in_specs=[WHOLE, WHOLE],
        out_specs=(WHOLE, WHOLE),
        out_shape=(shape, shape),
        compiler_params=params(8),
        cost_estimate=cost(1024, 1024),
        name="merge",
    )(near(kept), near(got))


def chosen(table, slot, arrived):
    rows = slice(64 * slot, 64 * slot + 64)
    plane = jnp.zeros((64, arrived[0].shape[1]), jnp.float32)
    for steps, ref in enumerate(arrived):
        plane = jnp.where(table[4 * len(arrived) + slot] == steps, ref[rows, :].astype(jnp.float32), plane)
    return plane


def forward_kernel(rows, mask, weight, bias, slopes, out, grad, edge, bias_sum, cols, pre):
    width = rows.shape[1]
    valid = windows((128, width), 0)
    for z in range(8):
        span = slice(128 * z, 128 * z + 128)
        for place, moved in enumerate(shifts(rows[span, :].astype(jnp.float32), 0, valid)):
            cols[span, place * width : (place + 1) * width] = moved

    def taps(a):
        return weight[9 * a : 9 * a + 9].reshape(9 * width, width)

    pre[...] = jnp.dot(cols[...], taps(1), preferred_element_type=jnp.float32) + bias[...]
    pre[128:, :] += jnp.dot(cols[:896, :], taps(0), preferred_element_type=jnp.float32)
    pre[:896, :] += jnp.dot(cols[128:, :], taps(2), preferred_element_type=jnp.float32)
    for side in range(2):
        edge[side] = pre[896 * side : 896 * side + 128, :]
    total = jnp.zeros((1, width), jnp.float32)
    for z in range(1, 7):
        span = slice(128 * z, 128 * z + 128)
        act, slope = activate(pre[span, :], both(slopes, z).astype(jnp.float32), wide(mask[span, :]))
        for b in range(2):
            out[b, z] = act[64 * b : 64 * b + 64]
        grad[128 * (z - 1) : 128 * z, :] = slope
        total += jnp.sum(slope.astype(jnp.float32), axis=0, keepdims=True)
    bias_sum[...] = total


def forward_inside(rows, mask, weight, bias, cotangent):
    width = rows.shape[1]
    return pl.pallas_call(
        forward_kernel,
        in_specs=[WHOLE] * 5,
        out_specs=(WHOLE,) * 4,
        out_shape=(
            jax.ShapeDtypeStruct(cotangent.shape, jnp.bfloat16),
            pltpu.VMEM((768, width), jnp.bfloat16),
            pltpu.VMEM((2, 128, width), jnp.float32),
            pltpu.VMEM((1, width), jnp.float32),
        ),
        scratch_shapes=[
            pltpu.VMEM((1024, 9 * width), jnp.bfloat16),
            pltpu.VMEM((1024, width), jnp.float32),
        ],
        compiler_params=params(12),
        cost_estimate=cost(1024, 1024),
        name="forward_inside",
    )(near(rows), near(mask), near(weight), bias, near(cotangent))


def inner_terms_kernel(mine, others, *refs):
    grads, terms = refs[:4], refs[4]
    rows = mine.shape[0]
    for a in range(3):
        lanes = slice(128 * a, 128 * a + 768)
        total = jnp.dot(mine[:, lanes], grads[0][...], preferred_element_type=jnp.float32)
        for index in range(3):
            total += jnp.dot(
                others[index * rows : (index + 1) * rows, lanes], grads[index + 1][...], preferred_element_type=jnp.float32
            )
        terms[a * rows : (a + 1) * rows, :] = total


def inner_terms(mine, others, grads):
    rows, width = mine.shape[0], grads[0].shape[1]
    return pl.pallas_call(
        inner_terms_kernel,
        in_specs=[WHOLE] * 6,
        out_specs=WHOLE,
        out_shape=pltpu.VMEM((3 * rows, width), jnp.float32),
        compiler_params=params(10),
        cost_estimate=cost(1024, 1024),
        name="inner_terms",
    )(near(mine), near(others), *[near(x) for x in grads])


def edge_kernel(table, mask, weight, edge, ends, inner, out_in, *refs):
    arrived, (out, to_inner, to_core, own, planes, flip, done) = refs[:-7], refs[-7:]
    width = edge.shape[2]
    valid = windows((128, width), 0)
    total = inner[...]
    for side in range(2):
        rows = slice(128 * side, 128 * side + 128)
        halo = jnp.concatenate([chosen(table, 2 * side + b, arrived) for b in range(2)], axis=0)
        flip[:, rows] = halo.T
        cols = jnp.concatenate(shifts(halo, 0, valid), axis=1)
        taps = weight[18 * side : 18 * side + 9].reshape(9 * width, width)
        pre = edge[side] + jnp.dot(cols, taps, preferred_element_type=jnp.float32)
        z = 7 * side
        keep = wide(mask[128 * z : 128 * z + 128, :])
        act, slope = activate(pre, both(ends, z).astype(jnp.float32), keep)
        for b in range(2):
            planes[side, b, 0] = act[64 * b : 64 * b + 64]
        pltpu.make_async_copy(planes.at[side], out.at[:, pl.ds(z, 1)], done.at[side]).start()
        to_inner[rows, :] = slope
        to_core[rows, :] = slope
        total += jnp.sum(slope.astype(jnp.float32), axis=0, keepdims=True)
    write_exact(total, to_inner)
    write_exact(total, to_core)
    quarters(flip, own, to_inner.at[272:], to_core.at[272:])
    for side in range(2):
        pltpu.make_async_copy(planes.at[side], out.at[:, pl.ds(7 * side, 1)], done.at[side]).wait()


def forward_edges(table, mask, weight, edge, ends, inner, out, arrived):
    width = edge.shape[2]
    quarter = width // 4
    return pl.pallas_call(
        edge_kernel,
        in_specs=[SCALARS] + [WHOLE] * 5 + [FAR] + [WHOLE] * len(arrived),
        out_specs=(FAR, WHOLE, WHOLE, WHOLE),
        out_shape=(
            jax.ShapeDtypeStruct(out.shape, out.dtype),
            pltpu.VMEM((256 + EXTRA + 2 * quarter, width), jnp.bfloat16),
            pltpu.VMEM((256 + EXTRA + quarter, width), jnp.bfloat16),
            pltpu.VMEM((quarter, 256), jnp.bfloat16),
        ),
        scratch_shapes=[
            pltpu.VMEM((2, 2, 1, 64, width), jnp.bfloat16),
            pltpu.VMEM((width, 256), jnp.float32),
            pltpu.SemaphoreType.DMA((2,)),
        ],
        input_output_aliases={6: 0},
        compiler_params=params(10),
        cost_estimate=cost(1024, 1024),
        name="forward_edges",
    )(
        table,
        near(mask),
        near(weight),
        near(edge),
        near(ends),
        near(inner),
        out,
        *[near(x) for x in arrived],
    )


def outer_terms_kernel(outer, mine, others, halos, *refs):
    parcels, inner = refs[:4], refs[4]
    gives, stay, cols, total = refs[5 : 4 + outer], refs[4 + outer], refs[5 + outer], refs[6 + outer]
    quarter = halos.shape[0]
    rows = 9 * quarter
    valid = windows((quarter, 128), 1)
    half = aligned(me() % 2, quarter)
    ends = (
        halos,
        parcels[1].at[272 : 272 + 2 * quarter].at[half],
        parcels[2].at[272 : 272 + quarter],
        parcels[3].at[272 : 272 + 2 * quarter].at[half],
    )
    facing = jnp.concatenate(
        [parcel[128 * side : 128 * side + 128, :] for side in range(2) for parcel in parcels], axis=0
    )
    for a in range(3):
        for side in range(2):
            plane = a - 1 + 7 * side
            for who in range(4):
                lanes = slice(128 * (4 * side + who), 128 * (4 * side + who) + 128)
                if 0 <= plane < 8:
                    ref, first = (mine, 0) if who == 0 else (others, rows * (who - 1))
                    cols[:, lanes] = ref[first : first + rows, 128 * plane : 128 * plane + 128]
                else:
                    moved = shifts(ends[who][:, 128 * side : 128 * side + 128].astype(jnp.float32), 1, valid)
                    for place in range(9):
                        cols[place * quarter : (place + 1) * quarter, lanes] = moved[place]
        span = slice(a * rows, (a + 1) * rows)
        total[span, :] = inner[span, :] + jnp.dot(cols[...], facing, preferred_element_type=jnp.float32)
    if total.shape[0] > 3 * rows:
        total[3 * rows :, :] = jnp.zeros((total.shape[0] - 3 * rows, total.shape[1]), jnp.float32)
    z = me() // 4
    for steps in range(outer):
        block = lax.rem(z + steps, outer)
        for unit in range(units(outer)):
            piece = total[aligned(block + outer * unit, 16), :]
            if steps:
                gives[steps - 1][16 * unit : 16 * unit + 16, :] = piece.astype(jnp.bfloat16)
            else:
                stay[16 * unit : 16 * unit + 16, :] = piece


def outer_terms(outer, mine, others, halos, parcels, inner):
    width = inner.shape[1]
    rows = 16 * units(outer)
    results = pl.pallas_call(
        functools.partial(outer_terms_kernel, outer),
        in_specs=[WHOLE] * 8,
        out_specs=[WHOLE] * outer,
        out_shape=[pltpu.VMEM((rows, width), jnp.bfloat16)] * (outer - 1) + [pltpu.VMEM((rows, width), jnp.float32)],
        scratch_shapes=[
            pltpu.VMEM((inner.shape[0] // 3, 1024), jnp.bfloat16),
            pltpu.VMEM((outer * rows, width), jnp.float32),
        ],
        compiler_params=params(12),
        cost_estimate=cost(1024, 1024),
        name="outer_terms",
    )(*[near(x) for x in (mine, others, halos, *parcels, inner)])
    return results[:-1], results[-1]


def backward_kernel(grad, parcel, mask, weight, grad_feats, partial, near_weight, cols, total, fetched):
    width = grad.shape[1]
    fetch_taps(weight, near_weight, fetched)
    valid = windows((128, width), 0)
    planes = [parcel[:128, :]] + [grad[128 * z : 128 * z + 128, :] for z in range(6)] + [parcel[128:256, :]]
    for z, plane in enumerate(planes):
        for at, moved in enumerate(shifts(plane.astype(jnp.float32), 0, valid, -1)):
            cols[128 * z : 128 * z + 128, at * width : (at + 1) * width] = moved
    for a in (1, 0, 2):
        await_taps(9 * a, 9 * a + 9, weight, near_weight, fetched)
        first, start, count = ((128, 0, 896), (0, 0, 1024), (0, 128, 896))[a]
        for at in range(9):
            piece = lax.dot_general(
                cols[first : first + count, at * width : (at + 1) * width],
                near_weight[9 * a + at],
                (((1,), (1,)), ((), ())),
                preferred_element_type=jnp.float32,
            )
            if a == 1 and at == 0:
                total[...] = piece
            else:
                total[start : start + count, :] += piece
    for z in range(1, 7):
        rows = slice(128 * z, 128 * z + 128)
        done = jnp.where(wide(mask[rows, :]), total[rows, :], 0.0).astype(jnp.bfloat16)
        for b in range(2):
            grad_feats[b, z] = done[64 * b : 64 * b + 64]
    for side in range(2):
        partial[side] = total[896 * side : 896 * side + 128, :]


def backward(grad, parcel, mask, weight):
    width = grad.shape[1]
    return pl.pallas_call(
        backward_kernel,
        in_specs=[WHOLE] * 3 + [FAR],
        out_specs=(WHOLE,) * 3,
        out_shape=(
            jax.ShapeDtypeStruct((2, 8, 64, width), jnp.bfloat16),
            pltpu.VMEM((2, 128, width), jnp.float32),
            pltpu.VMEM(weight.shape, jnp.bfloat16),
        ),
        scratch_shapes=[
            pltpu.VMEM((1024, 9 * width), jnp.bfloat16),
            pltpu.VMEM((1024, width), jnp.float32),
            pltpu.SemaphoreType.DMA((weight.shape[0],)),
        ],
        compiler_params=params(16),
        cost_estimate=cost(1024, 1024),
        name="backward",
    )(near(grad), near(parcel), near(mask), far(weight))


def block_copies(outer, places, stacks, out, done):
    position = me()
    blocks = [ref.at[index] for ref in stacks for index in range(ref.shape[0])]
    copies = []
    for index, (ref, (flip, inner, core)) in enumerate(zip(blocks, places)):
        block = (position // 4) ^ flip
        quarter = 4 * ((position % 4) ^ (2 * inner + core))
        if outer == 4:
            copies.append((None, pltpu.make_async_copy(ref, out.at[:, quarter + block], done.at[index, 0])))
            continue
        for unit in range(units(outer)):
            place = block + outer * unit
            here = jnp.minimum(place, 107)
            target = out.at[here // 4, quarter + here % 4]
            copies.append((place < 108, pltpu.make_async_copy(ref.at[unit], target, done.at[index, unit])))
    return copies


def for_each(copies, wait):
    for condition, copy in copies:
        act = copy.wait if wait else copy.start
        if condition is None:
            act()
        else:
            pl.when(condition)(act)


def assemble_kernel(outer, places, count, *refs):
    out, done = refs[-2:]
    copies = block_copies(outer, places, refs[:count], out, done)
    for_each(copies, False)
    for_each(copies, True)


def in_units(stack, outer):
    return near(stack.reshape(stack.shape[0], units(outer), 16, stack.shape[-1]))


def assemble(outer, places, stacks, shape, given):
    before = [] if given is None else [given]
    return pl.pallas_call(
        functools.partial(assemble_kernel, outer, places, len(stacks)),
        in_specs=[WHOLE] * len(stacks) + [FAR] * len(before),
        out_specs=FAR,
        out_shape=jax.ShapeDtypeStruct(shape, jnp.bfloat16),
        scratch_shapes=[pltpu.SemaphoreType.DMA((len(places), units(outer)))],
        input_output_aliases={len(stacks): 0} if before else {},
        compiler_params=params(),
        cost_estimate=cost(1024, 1024),
        name="assemble",
    )(*[in_units(x, outer) for x in stacks], *before)


def finish_kernel(outer, places, partial, mask, weight, kept, got, stack, feats_in, weight_in, *refs):
    grad_feats, grad_weight, bias_sum, planes, sent, done = refs
    copies = block_copies(outer, places, [stack], grad_weight, done)
    for_each(copies, False)
    width = weight.shape[1]
    valid = windows((128, width), 0)
    halos = merged(kept, got, 0)
    for side in range(2):
        total = partial[side]
        for at, moved in enumerate(shifts(halos[128 * side : 128 * side + 128, :], 0, valid, -1)):
            total += lax.dot_general(
                moved,
                weight[18 * (1 - side) + at],
                (((1,), (1,)), ((), ())),
                preferred_element_type=jnp.float32,
            )
        rows = slice(896 * side, 896 * side + 128)
        done_rows = jnp.where(wide(mask[rows, :]), total, 0.0).astype(jnp.bfloat16)
        for b in range(2):
            planes[side, b, 0] = done_rows[64 * b : 64 * b + 64]
        pltpu.make_async_copy(planes.at[side], grad_feats.at[:, pl.ds(7 * side, 1)], sent.at[side]).start()
    bias_sum[...] = read_extra(kept.at[0]) + read_extra(got.at[0])
    for side in range(2):
        pltpu.make_async_copy(planes.at[side], grad_feats.at[:, pl.ds(7 * side, 1)], sent.at[side]).wait()
    for_each(copies, True)


def finish(outer, places, partial, mask, weight, kept, got, stack, grad_feats, grad_weight):
    width = weight.shape[1]
    return pl.pallas_call(
        functools.partial(finish_kernel, outer, places),
        in_specs=[WHOLE] * 6 + [FAR, FAR],
        out_specs=(FAR, FAR, WHOLE),
        out_shape=(
            jax.ShapeDtypeStruct(grad_feats.shape, grad_feats.dtype),
            jax.ShapeDtypeStruct(grad_weight.shape, grad_weight.dtype),
            jax.ShapeDtypeStruct((1, width), jnp.float32),
        ),
        scratch_shapes=[
            pltpu.VMEM((2, 2, 1, 64, width), jnp.bfloat16),
            pltpu.SemaphoreType.DMA((2,)),
            pltpu.SemaphoreType.DMA((len(places), units(outer))),
        ],
        input_output_aliases={6: 0, 7: 1},
        compiler_params=params(10),
        cost_estimate=cost(1024, 1024),
        name="finish",
    )(*[near(x) for x in (partial, mask, weight, kept, got)], in_units(stack, outer), grad_feats, grad_weight)


def per_device(size, feats, voxmask, links, weight, bias, cotangent):
    width = feats.shape[3]
    outer = size // 4

    parcel = rims(links, feats, voxmask)
    mask, rows, give_inner, give_core, turned, taps, ends = prepare(feats, voxmask, weight, cotangent)
    inner, rows = lax.optimization_barrier((swap(parcel, size, 2), rows))
    parcels = [parcel, inner, swap(parcel, size, 1), swap(inner, size, 1)]
    out, grad, edge, bias_local = forward_inside(rows, mask, taps, bias.reshape(1, width), ends)
    *parcels, grad = lax.optimization_barrier((*parcels, grad))
    table, picks = route(parcels, outer)

    got_inner = swap(give_inner, size, 2)
    *picks, give_core, got_inner = lax.optimization_barrier((*picks, give_core, got_inner))
    arrived = [rotate(pick, size, steps) if steps else pick for steps, pick in enumerate(picks)]
    grad_inner = swap(grad, size, 2)
    *arrived, got_inner, grad_inner = lax.optimization_barrier((*arrived, got_inner, grad_inner))
    others = turn(got_inner, swap(give_core, size, 1), swap(got_inner, size, 1))
    grads = [grad, grad_inner, swap(grad, size, 1), swap(grad_inner, size, 1)]

    out, to_inner, to_core, halos = forward_edges(table, mask, taps, edge, ends, bias_local, out, arrived)
    inner = swap(to_inner, size, 2)
    terms = inner_terms(turned, others, grads)
    inner, terms = lax.optimization_barrier((inner, terms))
    parcels = [to_inner, inner, swap(to_core, size, 1), swap(inner, size, 1)]

    gives, stay = outer_terms(outer, turned, others, halos, parcels, terms)
    gots = [rotate(give, size, steps + 1) for steps, give in enumerate(gives)]
    give, kept = deal(table, parcels, outer)
    got = swap(give, size, 4)
    grad_feats, partial, taps = backward(grad, to_inner, mask, weight)
    bits = outer.bit_length() - 1
    for bit in range(1, bits):
        give, kept = merge(kept, got)
        if bit < bits - 1:
            got = swap(give, size, 4 << bit)
    stay, partial, give, kept = lax.optimization_barrier((stay, partial, give, kept))
    part = (stay + sum(got.astype(jnp.float32) for got in gots)).astype(jnp.bfloat16)

    def stack(*blocks):
        return jnp.concatenate([x.reshape(-1, *part.shape) for x in blocks])

    def place_blocks(keys, blocks, given):
        places = [(*key, core) for core in range(2) for key in keys]
        return assemble(outer, places, [blocks, swap(blocks, size, 1)], (27, 16, width // 16, width), given)

    last = outer - 1
    flips = list(range(1, last))
    blocks = [part]
    for flip in flips:
        blocks.append(swap(blocks[flip & (flip - 1)], size, 4 * (flip & -flip)))
    first_inner = swap(part, size, 2)
    middle = stack(*blocks[1:])
    farthest = swap(blocks[last & (last - 1)], size, 4)
    middle, give = lax.optimization_barrier((middle, give))
    middle_inner = swap(middle, size, 2)
    got = swap(give, size, 4 << (bits - 1))
    grad_weight = place_blocks([(0, 0), (0, 1)] + [(flip, 0) for flip in flips], stack(part, first_inner, middle), None)
    farthest_inner = swap(farthest, size, 2)
    middle_inner, farthest_inner, grad_weight, got = lax.optimization_barrier(
        (middle_inner, farthest_inner, grad_weight, got)
    )
    keys = [(flip, 1) for flip in flips] + [(last, 0), (last, 1)]
    rest = stack(middle_inner, farthest, farthest_inner)
    theirs = swap(rest, size, 1)
    grad_feats, grad_weight, grad_bias = finish(
        outer, [(*key, 0) for key in keys], partial, mask, taps, kept, got, rest, grad_feats, grad_weight
    )
    grad_weight = assemble(outer, [(*key, 1) for key in keys], [theirs], grad_weight.shape, grad_weight)
    return out, grad_feats, grad_weight.reshape(weight.shape), grad_bias.reshape(width)


def solution(mesh):
    return jax.shard_map(
        functools.partial(per_device, mesh.shape["zslab"]),
        mesh=mesh,
        in_specs=(
            P(("groups", "zslab"), None, None, None),
            P(("groups", "zslab"), None),
            P(("groups", "zslab"), None),
            P(),
            P(),
            P(("groups", "zslab"), None, None, None),
        ),
        out_specs=(
            P(("groups", "zslab"), None, None, None),
            P(("groups", "zslab"), None, None, None),
            P("groups", None, None),
            P("groups"),
        ),
        check_vma=False,
    )
```
